128 devices in a mesh: seq: 64 (over z, x, y_lo, core), batch: 2 (over y_hi).
Axes of the slice: x: 4, y: 4 (y_hi: 2, y_lo: 2; y = y_hi * 2 + y_lo), z: 4, core: 2. Of those that a mesh axis runs over, the one named last changes fastest.
Arguments:
- tokens: bfloat16 [2, 8192, 768], P('batch', 'seq'), may hold values from -16 to 16
- seg_lengths: int32 [2, 16], P('batch'), may hold values from 256 to 512, as said below
- ln1_gain: bfloat16 [768], P('seq'), may hold values from 0.5 to 1.5
- ln1_bias: bfloat16 [768], P('seq'), may hold values from -3 to 3
- w_query: bfloat16 [768, 768], P('seq'), may hold values from -0.21875 to 0.21875
- q_bias: bfloat16 [768], P('seq'), may hold values from -3 to 3
- w_key: bfloat16 [768, 768], P('seq'), may hold values from -0.21875 to 0.21875
- w_value: bfloat16 [768, 768], P('seq'), may hold values from -0.21875 to 0.21875
- v_bias: bfloat16 [768], P('seq'), may hold values from -3 to 3
- w_out: bfloat16 [768, 768], P('seq'), may hold values from -0.875 to 0.875
- o_bias: bfloat16 [768], P('seq'), may hold values from -3 to 3
- ln2_gain: bfloat16 [768], P('seq'), may hold values from 0.5 to 1.5
- ln2_bias: bfloat16 [768], P('seq'), may hold values from -3 to 3
- w_up: bfloat16 [768, 3072], P('seq'), may hold values from -0.21875 to 0.21875
- up_bias: bfloat16 [3072], P('seq'), may hold values from -3 to 3
- w_down: bfloat16 [768, 3072], P('seq'), may hold values from -0.109375 to 0.109375
- down_bias: bfloat16 [768], P('seq'), may hold values from -3 to 3
- d_out: bfloat16 [2, 8192, 768], P('batch', 'seq'), may hold values from -6 to 6
Outputs:
- output: bfloat16 [2, 8192, 768], P('batch', 'seq')
- g_tokens: float32 [2, 8192, 768], P('batch', 'seq')
- g_ln1_gain: float32 [768], P('seq')
- g_ln1_bias: float32 [768], P('seq')
- g_w_query: float32 [768, 768], P('seq')
- g_q_bias: float32 [768], P('seq')
- g_w_key: float32 [768, 768], P('seq')
- g_w_value: float32 [768, 768], P('seq')
- g_v_bias: float32 [768], P('seq')
- g_w_out: float32 [768, 768], P('seq')
- g_o_bias: float32 [768], P('seq')
- g_ln2_gain: float32 [768], P('seq')
- g_ln2_bias: float32 [768], P('seq')
- g_w_up: float32 [768, 3072], P('seq')
- g_up_bias: float32 [3072], P('seq')
- g_w_down: float32 [768, 3072], P('seq')
- g_down_bias: float32 [768], P('seq')
The draws below stay inside these ranges and needn't reach their ends.
Inputs may be any that keep to these rules, and one draw needn't show every extreme that they name: `seg_lengths`: in every item one segment slot holds exactly 512 real tokens and another exactly half of 512.
All inputs are finite; a program needn't handle non-finite values.
Results may differ from the reference program's by a relative error of at most 0.024.
Values may be sent and summed in bfloat16 or wider, within the bound.
A program may use at most 128 MiB of HBM per device.

```python
import math
from functools import partial
import jax
import jax.numpy as jnp
from jax import lax

D = 768
HEADS = 12
HEAD = 64
FF = 3072
SUMMARY = 50
SEGS = 16
ITEMS = 2
ITEM = 8192
SEG_CAP = 512


def draw_seg_lengths(key, part):
    key = jax.random.fold_in(key, 7)
    first_key, second_key, third_key = jax.random.split(key, 3)
    lengths = jax.random.randint(first_key, (ITEMS, SEGS), SEG_CAP // 2, SEG_CAP + 1)
    longest = jax.random.randint(second_key, (ITEMS, 1), 0, SEGS)
    shortest = (longest + jax.random.randint(third_key, (ITEMS, 1), 1, SEGS)) % SEGS
    columns = jnp.arange(SEGS)[None, :]
    lengths = jnp.where(columns == longest, SEG_CAP, lengths)
    lengths = jnp.where(columns == shortest, SEG_CAP // 2, lengths)
    return lengths.astype(jnp.int32)


def spiked(entries, own_key, source, target, shards_of, factor):
    owner, partner = [(jnp.arange(entries.shape[axis_at]) // (entries.shape[axis_at] // shards_of)).reshape([-1 if axis == axis_at else 1 for axis in range(entries.ndim)]) for axis_at in (source, target)]
    chosen = jax.random.permutation(own_key, shards_of)[partner]
    strong = (owner == chosen) | (owner == (partner + shards_of // 2) % shards_of)
    return jnp.where(strong, factor * entries, entries)


def levels(own_key, dims, pieces, smallest, high):
    level = 1.0
    for position, shards_of in pieces:
        draws = jax.random.uniform(jax.random.fold_in(jax.random.fold_in(own_key, 6), position), (shards_of,), jnp.float32, smallest / len(pieces), high / len(pieces))
        level = level * jnp.repeat(jnp.exp(draws), dims[position] // shards_of).reshape((-1,) + (1,) * (len(dims) - 1 - position))
    return level


def gaussian(own_key, dims, scale, reach, cuts=(), held_as=jnp.bfloat16):
    values = jax.random.normal(own_key, dims, jnp.float32) * scale
    if len(cuts) > 0:
        values = levels(own_key, dims, cuts, -0.22, 0.18) * values
    return jnp.clip(values, min=-reach, max=reach).astype(held_as)


def gaussian_with(key, shape, width, limit, cuts, heavy, kind=jnp.bfloat16):
    values = width * jax.random.normal(key, shape, jnp.float32)
    if cuts:
        values = values * levels(key, shape, cuts, -0.22, 0.18)
    return jnp.clip(spiked(values, jax.random.fold_in(key, 3), *heavy), -limit, limit).astype(kind)


def setup_inputs(seed: int = 0) -> dict:
    arg_keys = jax.random.split(jax.random.key(seed), 19)
    tokens = gaussian_with(arg_keys[0], (ITEMS, ITEM, D), 1.0, 16.0, ((0, 2), (1, 64)), (1, 2, 64, 4.0))
    seg_lengths = draw_seg_lengths(jax.random.fold_in(arg_keys[18], 71), 0)
    ln1_gain = jnp.clip(1.0 + 0.1 * jax.random.normal(arg_keys[2], (D,), jnp.float32), 0.5, 1.5).astype(jnp.bfloat16)
    ln1_bias = gaussian(arg_keys[3], (D,), 0.5, 3.0, ((0, 64),))
    w_query = gaussian(arg_keys[4], (D, D), D ** -0.5, 0.21875, ((0, 64),))
    q_bias = gaussian(arg_keys[5], (D,), 0.5, 3.0, ((0, 64),))
    w_key = gaussian(arg_keys[6], (D, D), D ** -0.5, 0.21875, ((0, 64),))
    w_value = gaussian(arg_keys[7], (D, D), D ** -0.5, 0.21875, ((0, 64),))
    v_bias = gaussian(arg_keys[8], (D,), 0.5, 3.0, ((0, 64),))
    w_out = gaussian(arg_keys[9], (D, D), (D // 16) ** -0.5, 0.875, ((0, 64),))
    o_bias = gaussian(arg_keys[10], (D,), 0.5, 3.0, ((0, 64),))
    ln2_gain = jnp.clip(1.0 + 0.1 * jax.random.normal(arg_keys[11], (D,), jnp.float32), 0.5, 1.5).astype(jnp.bfloat16)
    ln2_bias = gaussian(arg_keys[12], (D,), 0.5, 3.0, ((0, 64),))
    w_up = gaussian(arg_keys[13], (D, FF), D ** -0.5, 0.21875, ((0, 64),))
    up_bias = gaussian(arg_keys[14], (FF,), 0.5, 3.0, ((0, 64),))
    w_down = gaussian(arg_keys[15], (D, FF), FF ** -0.5, 0.109375, ((0, 64),))
    down_bias = gaussian(arg_keys[16], (D,), 0.5, 3.0, ((0, 64),))
    d_out = gaussian(arg_keys[17], (ITEMS, ITEM, D), 1.0, 6.0, ((0, 2), (1, 64)))
    return {"tokens": tokens, "seg_lengths": seg_lengths, "ln1_gain": ln1_gain, "ln1_bias": ln1_bias, "w_query": w_query, "q_bias": q_bias, "w_key": w_key, "w_value": w_value, "v_bias": v_bias, "w_out": w_out, "o_bias": o_bias, "ln2_gain": ln2_gain, "ln2_bias": ln2_bias, "w_up": w_up, "up_bias": up_bias, "w_down": w_down, "down_bias": down_bias, "d_out": d_out}


@jax.custom_vjp
def low(v):
    return lax.optimization_barrier(v.astype(jnp.bfloat16)).astype(jnp.float32)

@jax.custom_vjp
def low_back(v):
    return v

def low_keep(v):
    return (low(v), None)

def low_pass(kept, grad):
    return (grad,)

def back_keep(v):
    return (v, None)

def back_low(kept, grad):
    return (low(grad),)
low.defvjp(low_keep, low_pass)
low_back.defvjp(back_keep, back_low)
HIGHEST = lax.Precision.HIGHEST
EPSILON = 1e-05
MASKED = -1e+30

def norm_rows(values, scale_gain, scale_shift):
    center = values - lax.optimization_barrier(jnp.mean(values, axis=-1, keepdims=True))
    spread = lax.optimization_barrier(jnp.mean(center * center, axis=-1, keepdims=True))
    return center * lax.rsqrt(spread + EPSILON) * scale_gain + scale_shift

def rounded(values):
    return low_back(low(values))

def matmul(left_rows, right_cols):
    return jnp.dot(left_rows, right_cols, precision=HIGHEST)

def item_attention(queries, key_rows, value_rows, lengths_row):
    slot_ids = jnp.arange(SEGS * SUMMARY, dtype=jnp.int32)
    slot_seg = slot_ids // SUMMARY
    slot_pick = slot_seg[:, None] == jnp.arange(SEGS, dtype=jnp.int32)[None, :]
    slot_len = lax.optimization_barrier(jnp.sum(jnp.where(slot_pick, lengths_row[None, :], 0), axis=1)).astype(jnp.int32)
    slot_pos = (slot_seg * SEG_CAP + slot_len - SUMMARY + (slot_ids - slot_seg * SUMMARY)).astype(jnp.int32)
    summary_keys = jnp.take(key_rows, slot_pos, axis=0)
    summary_values = jnp.take(value_rows, slot_pos, axis=0)
    block_rows = math.gcd(512, SEG_CAP)

    def one_block(first_row):
        q_rows = lax.dynamic_slice_in_dim(queries, first_row, block_rows, 0)
        seg_index = (first_row // SEG_CAP).astype(jnp.int32)
        seg_start = (seg_index * SEG_CAP).astype(jnp.int32)
        k_seg = lax.dynamic_slice_in_dim(key_rows, seg_start, SEG_CAP, 0)
        v_seg = lax.dynamic_slice_in_dim(value_rows, seg_start, SEG_CAP, 0)
        seg_len = jnp.sum(jnp.where(jnp.arange(SEGS, dtype=jnp.int32) == seg_index, lengths_row, 0))
        q_pos = first_row + jnp.arange(block_rows, dtype=jnp.int32)
        k_off = jnp.arange(SEG_CAP, dtype=jnp.int32)
        k_pos = seg_start + k_off
        present = k_off < seg_len
        own_seg = (k_pos[None, :] <= q_pos[:, None]) & (present[None, :] | (k_pos[None, :] == q_pos[:, None]))
        earlier = jnp.broadcast_to(slot_seg[None, :] < seg_index, (block_rows, SEGS * SUMMARY))
        allowed = jnp.concatenate([own_seg, earlier], axis=1)
        keys_all = jnp.concatenate([k_seg, summary_keys], axis=0)
        values_all = jnp.concatenate([v_seg, summary_values], axis=0)
        scores = low_back(jnp.einsum('qhd,khd->hqk', q_rows, keys_all, precision=HIGHEST))
        scores = jnp.where(allowed[None], scores, MASKED)
        row_peak = lax.optimization_barrier(jnp.max(scores, axis=-1, keepdims=True))
        powers = jnp.exp(scores - row_peak)
        weights = powers / lax.optimization_barrier(jnp.sum(powers, axis=-1, keepdims=True))
        return jnp.einsum('hqk,khd->qhd', low(weights), values_all, precision=HIGHEST)
    starts = jnp.arange(ITEM // block_rows, dtype=jnp.int32) * block_rows
    return lax.map(jax.checkpoint(one_block), starts).reshape(ITEM, HEADS * HEAD)

def forward_layer(seg_lengths, tokens, ln1_gain, ln1_bias, w_query, q_bias, w_key, w_value, v_bias, w_out, o_bias, ln2_gain, ln2_bias, w_up, up_bias, w_down, down_bias):
    flat_rows = tokens.reshape(ITEMS * ITEM, D)
    normed = low(norm_rows(flat_rows, ln1_gain, ln1_bias))
    queries = rounded((matmul(normed, w_query) + q_bias) * 0.125)
    key_rows = rounded(matmul(normed, w_key))
    value_rows = rounded(matmul(normed, w_value) + v_bias)
    head_shape = (ITEMS, ITEM, HEADS, HEAD)
    attended = lax.map(lambda packed: item_attention(packed[0], packed[1], packed[2], packed[3]), (queries.reshape(head_shape), key_rows.reshape(head_shape), value_rows.reshape(head_shape), seg_lengths))
    attended = rounded(attended.reshape(ITEMS * ITEM, D))
    hidden = flat_rows + low_back(matmul(attended, w_out) + o_bias)
    normed_mid = low(norm_rows(hidden, ln2_gain, ln2_bias))
    pre_act = low_back(matmul(normed_mid, w_up) + up_bias)
    active = low(jax.nn.gelu(pre_act, approximate=True))
    result = hidden + low_back(matmul(active, w_down.T) + down_bias)
    return result.reshape(ITEMS, ITEM, D)

def reference(tokens, seg_lengths, ln1_gain, ln1_bias, w_query, q_bias, w_key, w_value, v_bias, w_out, o_bias, ln2_gain, ln2_bias, w_up, up_bias, w_down, down_bias, d_out):
    floats = [argument.astype(jnp.float32) for argument in (tokens, ln1_gain, ln1_bias, w_query, q_bias, w_key, w_value, v_bias, w_out, o_bias, ln2_gain, ln2_bias, w_up, up_bias, w_down, down_bias)]
    result, backward = jax.vjp(partial(forward_layer, seg_lengths), *floats)
    grads = backward(d_out.astype(jnp.float32))
    return (result.astype(jnp.bfloat16), grads[0], grads[1], grads[2], grads[3], grads[4], grads[5], grads[6], grads[7], grads[8], grads[9], grads[10], grads[11], grads[12], grads[13], grads[14], grads[15])
```

```python
import functools
import types

import jax
import jax.numpy as jnp
from jax import lax
from jax.experimental import pallas as pl
from jax.experimental.pallas import tpu as pltpu
from jax.sharding import PartitionSpec as P

BF = jnp.bfloat16
F32 = jnp.float32
MESH = pl.DeviceIdType.MESH
EPSILON = 1e-05
MASKED = -1e30
HIGHEST = lax.Precision.HIGHEST

ROWS = 128
SEG = 512
D = 768
HW = 192
HEADS = 3
SUMMARY = 50
SLOT = 64
SLOTS = 16
KEYS = SEG + SLOTS * SLOT
SUMS = SLOTS * SLOT


def dot(a, b, **kw):
    return jnp.dot(a, b, preferred_element_type=F32, **kw)


def dot_nt(a, b):
    return lax.dot_general(a, b, (((1,), (1,)), ((), ())), preferred_element_type=F32)


def dot_tn(a, b):
    return lax.dot_general(a, b, (((0,), (0,)), ((), ())), preferred_element_type=F32)


def iota(shape, dim):
    return lax.broadcasted_iota(jnp.int32, shape, dim)


def norm_stats(values):
    center = values - jnp.mean(values, axis=-1, keepdims=True)
    spread = jnp.mean(center * center, axis=-1, keepdims=True)
    return center, lax.rsqrt(spread + EPSILON)


SCRATCH = dict(
    pk1=((4, 16, D), BF),
    pk2=((4, 16, 2 * D), BF),
    p01=((4, 16, D), BF),
    p02=((4, 16, 2 * D), BF),
    w1=((4, 4, 48, D), BF),
    w2=((4, 4, 48, 2 * D), BF),
    wosl=((4, D, HW), BF),
    wof=((D, D), BF),
    vb=((16, D), BF),
    vg=((3, 16, D), BF),
    vs1=((16, D), BF),
    vx=((3, 16, D), BF),
    vs2=((16, D), BF),
    vz=((3, 16, D), BF),
    vecs=((16, D), F32),
    toka=((SEG, D), BF),
    doa=((SEG, D), BF),
    nrm=((SEG, D), BF),
    nrmt=((D, SEG), BF),
    dot_=((D, SEG), BF),
    bias=((SEG, SEG), F32),
    q=((SEG, HW), BF),
    kv=((2, KEYS, HW), BF),
    ssrc=((2, SLOT, HW), BF),
    sloc=((HEADS, SEG, SEG), F32),
    ssum=((SEG, SUMS), F32),
    prob=((HEADS, SEG, KEYS), BF),
    att=((SEG, HW), F32),
    atta=((4, SEG, HW), BF),
    attt=((D, SEG), BF),
    hid=((SEG, D), F32),
    nm=((SEG, D), BF),
    nmt=((D, SEG), BF),
    pre=((SEG, D), F32),
    ga=((SEG, D), F32),
    act=((SEG, D), BF),
    gp=((SEG, D), BF),
    rm_s=((SEG, D), BF),
    rm_1=((2, ROWS, D), BF),
    rm_x=((ROWS, D), BF),
    rm_2=((ROWS, D), BF),
    ro_s=((SEG, D), BF),
    ro_1=((2, ROWS, D), BF),
    ro_x=((ROWS, D), BF),
    ro_2=((ROWS, D), BF),
    rn_s=((SEG, D), BF),
    rn_1=((2, ROWS, D), BF),
    rn_x=((ROWS, D), BF),
    rn_2=((ROWS, D), BF),
    gm=((ROWS, D), F32),
    gh=((ROWS, D), F32),
    gbr=((ROWS, D), BF),
    sa=((4, ROWS, HW), BF),
    sb=((4, ROWS, HW), BF),
    do=((4, ROWS, HW), BF),
    gba=((4, ROWS, HW), BF),
    ds=((SEG, SUMS), BF),
    dq=((SEG, HW), F32),
    dkt=((HW, SEG), F32),
    dvt=((HW, SEG), F32),
    dkst=((HW, SUMS), F32),
    dvst=((HW, SUMS), F32),
    dkvs=((2, SUMS, HW), BF),
    sumg=((SLOTS, 2, SLOT, HW), BF),
    dqkv=((SEG, 3 * HW), BF),
    g1=((4, 4, 48, D), BF),
    g2=((4, 4, 48, 2 * D), BF),
    rza1=((3, 4, 48, D // 2), BF),
    rxa1=((3, 48, D // 2), BF),
    rxb1=((3, 4, 48, D // 2), BF),
    rzb1=((3, 48, D // 2), BF),
    ha1=((4, 48, D // 2), BF),
    hb1=((4, 48, D // 2), BF),
    rza2=((3, 4, 48, D), BF),
    rxa2=((3, 48, D), BF),
    rxb2=((3, 4, 48, D), BF),
    rzb2=((3, 48, D), BF),
    ha2=((4, 48, D), BF),
    hb2=((4, 48, D), BF),
    fx1=((4, 16, D), BF),
    fx2=((4, 16, 2 * D), BF),
    fin1=((8, 16, D), BF),
    fin2=((8, 16, 2 * D), BF),
    vgr=((16, D), F32),
    vgx=((3, 16, D), F32),
    vgs=((16, D), F32),
    vgz=((3, 16, D), F32),
    vgt=((16, D), F32),
    vfin=((8, 16, D), F32),
)
COPIES = 224


def layer_kernel(
    seg_ref, tok, dout, wq, wk, wv, wo, wu, wd, vec,
    out_o, gtok_o, gq_o, gk_o, gv_o, go_o, gu_o, gd_o, gvec_o,
    *scratch,
):
    m = types.SimpleNamespace(**dict(zip(SCRATCH, scratch[:-2])))
    ss, rs = scratch[-2:]
    batch = lax.axis_index("batch")
    place = lax.axis_index("seq")
    s = place // 4
    t = place % 4
    z = s // 4
    x = s % 4
    sib = t + 1 - 2 * (t % 2)
    over = (t + 2) % 4
    diag = 3 - t

    def dev(seg, tt, bb):
        return (4 * seg + tt, bb)

    used = [0]
    sent = []

    def take(n=1):
        first = used[0]
        used[0] += n
        return first

    def send(src, dst, device):
        k = take()
        copy = pltpu.make_async_remote_copy(
            src_ref=src, dst_ref=dst, send_sem=ss.at[k], recv_sem=rs.at[k],
            device_id=device, device_id_type=MESH,
        )
        copy.start()
        sent.append(copy)
        return copy

    def rows_of(ref, k):
        return ref.at[pl.ds(pl.multiple_of(k * ROWS, ROWS), ROWS)]

    def get_rows(ref, k):
        return ref[pl.ds(pl.multiple_of(k * ROWS, ROWS), ROWS), :]

    def put_rows(ref, k, value):
        ref[pl.ds(pl.multiple_of(k * ROWS, ROWS), ROWS), :] = value

    group = (over, diag, sib)

    def blocks(count, size, fn, unroll=1):
        def step(j, carry):
            fn(pl.ds(pl.multiple_of(j * size, size), size), j * size)
            return carry

        lax.fori_loop(0, count, step, 0, unroll=unroll)

    m.kv[:, SEG:, :] = jnp.zeros((2, SUMS, HW), BF)
    m.sumg[...] = jnp.zeros((SLOTS, 2, SLOT, HW), BF)
    barrier = pltpu.get_barrier_semaphore()
    partners = [dev(s, u, batch) for u in group]
    partners += [dev((s + k) % 16, t, batch) for k in range(1, 16)]
    partners += [dev(s, u, 1 - batch) for u in (t, sib, over, diag)]
    for partner in partners:
        pl.semaphore_signal(barrier, inc=1, device_id=partner, device_id_type=MESH)
    m.pk1[...] = jnp.zeros((4, 16, D), BF)
    m.pk2[...] = jnp.zeros((4, 16, 2 * D), BF)
    for u in range(4):
        cols = slice(HW * u, HW * u + HW)
        m.pk1[u, 0:12, :] = jnp.concatenate(
            [wq[:, cols], wk[:, cols], wv[:, cols], wo[:, cols]], axis=1
        )
        wide = slice(D * u, D * u + D)
        m.pk2[u, 0:12, 0:D] = wu[:, wide]
        m.pk2[u, 0:12, D:] = wd[:, wide]
    shift = iota((128, D), 1) - iota((128, D), 0)
    put_12 = (shift == 12 * place).astype(BF)
    put_48 = (shift == 48 * (place % 16)).astype(BF)
    narrow = dot(vec[...], put_12)
    wider = dot(vec[...], put_48)
    vec_row = iota((16, D), 0)
    m.vb[...] = jnp.where(
        vec_row < 8, narrow, jnp.where(vec_row == 8 + z, wider[8:9, :], 0.0)
    ).astype(BF)
    pl.semaphore_wait(barrier, len(partners))

    first1 = [send(m.pk1.at[u], m.p01.at[t], dev(s, u, batch)) for u in group]
    firstv = [
        send(m.vb, m.vg.at[k], dev(s, u, batch)) for k, u in enumerate((sib, over, diag))
    ]

    def gather_start(src, ref):
        return [
            send(src, rows_of(ref, t), dev(s, over, batch)),
            send(src, rows_of(ref, t), dev(s, sib, batch)),
        ]

    def gather_pass(copies, ref):
        copies[0].wait_recv()
        copies.append(send(rows_of(ref, over), rows_of(ref, over), dev(s, sib, batch)))

    def gather_end(copies):
        copies[1].wait_recv()
        copies[2].wait_recv()

    ag_tok = gather_start(tok, m.toka)
    first2 = [send(m.pk2.at[u], m.p02.at[t], dev(s, u, batch)) for u in group]
    ag_do = gather_start(dout, m.doa)
    m.p01[t] = m.pk1[t]
    m.p02[t] = m.pk2[t]
    put_rows(m.toka, t, tok[...])
    put_rows(m.doa, t, dout[...])

    row48 = iota((48, 64), 0)
    owner48 = (
        (row48 >= 12).astype(jnp.int32)
        + (row48 >= 24).astype(jnp.int32)
        + (row48 >= 36).astype(jnp.int32)
    )
    squeeze = (iota((48, 64), 1) == row48 + 4 * owner48).astype(BF)

    def spread_start(w, p0, copies, half):
        for copy in copies:
            copy.wait_recv()
        w[z, x] = dot(squeeze, p0[...].reshape(64, 2 * half)).astype(BF)
        a_cols, b_cols = pl.ds(0, half), pl.ds(half, half)
        a = [
            send(w.at[z, x, :, a_cols], w.at[z, x, :, a_cols], dev(4 * z + (x + k) % 4, t, batch))
            for k in (1, 3, 2)
        ]
        b = [
            send(w.at[z, x, :, b_cols], w.at[z, x, :, b_cols], dev(4 * ((z + k) % 4) + x, t, batch))
            for k in (1, 3, 2)
        ]
        return a, b

    def spread_pass(w, phase, half):
        a, b = phase
        a_cols, b_cols = pl.ds(0, half), pl.ds(half, half)
        for copy in a:
            copy.wait_recv()
        a2 = [
            send(w.at[z, :, :, a_cols], w.at[z, :, :, a_cols], dev(4 * ((z + k) % 4) + x, t, batch))
            for k in (1, 3, 2)
        ]
        for copy in b:
            copy.wait_recv()
        b2 = [
            send(w.at[:, x, :, b_cols], w.at[:, x, :, b_cols], dev(4 * z + (x + k) % 4, t, batch))
            for k in (1, 3, 2)
        ]
        return a2 + b2

    def finish(copies):
        for copy in copies:
            copy.wait_recv()

    phase1 = spread_start(m.w1, m.p01, first1, D // 2)
    finish(firstv)
    m.vs1[...] = (
        m.vb[...].astype(F32) + m.vg[0].astype(F32) + m.vg[1].astype(F32) + m.vg[2].astype(F32)
    ).astype(BF)
    vx = [
        send(m.vs1, m.vx.at[k - 1], dev(4 * z + (x + k) % 4, t, batch)) for k in (1, 2, 3)
    ]
    phase2 = spread_start(m.w2, m.p02, first2, D)
    gather_pass(ag_tok, m.toka)
    ends1 = spread_pass(m.w1, phase1, D // 2)
    finish(vx)
    m.vs2[...] = (
        m.vs1[...].astype(F32) + m.vx[0].astype(F32) + m.vx[1].astype(F32) + m.vx[2].astype(F32)
    ).astype(BF)
    vz = [
        send(m.vs2, m.vz.at[k - 1], dev(4 * ((z + k) % 4) + x, t, batch)) for k in (1, 2, 3)
    ]
    gather_pass(ag_do, m.doa)

    seg_len = seg_ref[0, s]
    q_pos = iota((ROWS, SEG), 0)
    k_pos = iota((ROWS, SEG), 1)
    for k in range(4):
        mine = q_pos + ROWS * k
        ok = ((k_pos <= mine) & (k_pos < seg_len)) | (k_pos == mine)
        m.bias[k * ROWS:(k + 1) * ROWS, :] = jnp.where(ok, 0.0, MASKED)
    s_col = iota((8, SUMS), 1)
    sum_bias = jnp.where((s_col < SLOT * s) & (s_col % SLOT < SUMMARY), 0.0, MASKED)[0:1, :]
    pick = (
        (iota((SLOT, SEG), 1) == seg_len - SUMMARY + iota((SLOT, SEG), 0))
        & (iota((SLOT, SEG), 0) < SUMMARY)
    ).astype(BF)
    lane_head = iota((1, HW), 1) // 64

    def of_head(value, h):
        return jnp.where(lane_head == h, value, jnp.zeros_like(value))

    ends2 = spread_pass(m.w2, phase2, D)
    gather_end(ag_tok)
    finish(vz)
    m.vecs[...] = (
        m.vs2[...].astype(F32) + m.vz[0].astype(F32) + m.vz[1].astype(F32) + m.vz[2].astype(F32)
    )
    gain1, shift1 = m.vecs[0:1, :], m.vecs[1:2, :]
    gain2, shift2 = m.vecs[5:6, :], m.vecs[6:7, :]
    o_bias, down_bias = m.vecs[4:5, :], m.vecs[7:8, :]

    def my_cols(row):
        whole = m.vecs[row:row + 1, :]
        value = whole[:, 0:HW]
        for u in range(1, 4):
            value = jnp.where(t == u, whole[:, HW * u:HW * u + HW], value)
        return value

    q_bias, v_bias = my_cols(2), my_cols(3)
    up_bias = m.vecs[8:9, :]
    for u in range(1, 4):
        up_bias = jnp.where(t == u, m.vecs[8 + u:9 + u, :], up_bias)

    def norm1(rows, _):
        center, scale = norm_stats(m.toka[rows, :].astype(F32))
        m.nrm[rows, :] = (center * scale * gain1 + shift1).astype(BF)

    blocks(8, 64, norm1)
    m.nrmt[...] = m.nrm[...].T
    gather_end(ag_do)
    m.dot_[...] = m.doa[...].T

    finish(ends1)
    w1 = m.w1[...].reshape(D, D)
    m.wosl[t] = w1[:, 3 * HW:]
    ag_wo = [
        send(m.wosl.at[t], m.wosl.at[t], dev(s, over, batch)),
        send(m.wosl.at[t], m.wosl.at[t], dev(s, sib, batch)),
    ]
    qkv = dot(m.nrm[...], w1)
    m.q[...] = ((qkv[:, 0:HW] + q_bias) * 0.125).astype(BF)
    m.kv[0, 0:SEG, :] = qkv[:, HW:2 * HW].astype(BF)
    m.kv[1, 0:SEG, :] = (qkv[:, 2 * HW:3 * HW] + v_bias).astype(BF)

    m.ssrc[0] = dot(pick, m.kv[0, 0:SEG, :]).astype(BF)
    m.ssrc[1] = dot(pick, m.kv[1, 0:SEG, :]).astype(BF)
    sum_at = take(16)

    def sum_copy(j):
        return pltpu.make_async_remote_copy(
            src_ref=m.ssrc,
            dst_ref=m.kv.at[:, pl.ds(pl.multiple_of(SEG + SLOT * s, SLOT), SLOT), :],
            send_sem=ss.at[sum_at + j], recv_sem=rs.at[sum_at + s],
            device_id=dev(j, t, batch), device_id_type=MESH,
        )

    for j in range(1, 16):
        @pl.when(j > s)
        def _(j=j):
            sum_copy(j).start()

    for h in range(HEADS):
        m.sloc[h] = dot_nt(of_head(m.q[...], h), m.kv[0, 0:SEG, :]) + m.bias[...]
    ag_wo[0].wait_recv()
    ag_wo.append(send(m.wosl.at[over], m.wosl.at[over], dev(s, sib, batch)))

    def sum_arrived(j):
        pltpu.make_async_remote_copy(
            src_ref=m.ssrc,
            dst_ref=m.kv.at[:, pl.ds(SEG + SLOT * j, SLOT), :],
            send_sem=ss.at[sum_at + j], recv_sem=rs.at[sum_at + j],
            device_id=dev(j, t, batch), device_id_type=MESH,
        ).wait_recv()

    for j in range(15):
        @pl.when(j < s)
        def _(j=j):
            sum_arrived(j)

    for h in range(HEADS):
        m.ssum[...] = dot_nt(of_head(m.q[...], h), m.kv[0, SEG:, :]) + sum_bias

        def soften(rows, _, h=h):
            local = m.sloc[h, rows, :]
            other = m.ssum[rows, :]
            peak = jnp.maximum(
                jnp.max(local, axis=-1, keepdims=True), jnp.max(other, axis=-1, keepdims=True)
            )
            local = jnp.exp(local - peak)
            other = jnp.exp(other - peak)
            total = jnp.sum(local, axis=-1, keepdims=True) + jnp.sum(other, axis=-1, keepdims=True)
            share = 1.0 / total
            m.prob[h, rows, 0:SEG] = (local * share).astype(BF)
            m.prob[h, rows, SEG:] = (other * share).astype(BF)

        blocks(16, 32, soften, unroll=2)
        part = dot(m.prob[h], of_head(m.kv[1], h))
        m.att[...] = part if h == 0 else m.att[...] + part
    m.atta[t] = m.att[...].astype(BF)
    ag_att = [
        send(m.atta.at[t], m.atta.at[t], dev(s, over, batch)),
        send(m.atta.at[t], m.atta.at[t], dev(s, sib, batch)),
    ]
    ag_wo[1].wait_recv()
    ag_wo[2].wait_recv()
    m.wof[...] = jnp.concatenate([m.wosl[0], m.wosl[1], m.wosl[2], m.wosl[3]], axis=1)
    finish(ends2)
    m.ga[...] = dot(m.doa[...], m.w2[:, :, :, D:].reshape(D, D))
    ag_att[0].wait_recv()
    ag_att.append(send(m.atta.at[over], m.atta.at[over], dev(s, sib, batch)))
    ag_att[1].wait_recv()
    ag_att[2].wait_recv()

    branch = dot(m.atta[0], m.wof[0:HW, :])
    for u in range(1, 4):
        branch = branch + dot(m.atta[u], m.wof[HW * u:HW * u + HW, :])
    m.hid[...] = m.toka[...].astype(F32) + branch + o_bias

    def norm2(rows, _):
        center, scale = norm_stats(m.hid[rows, :])
        m.nm[rows, :] = (center * scale * gain2 + shift2).astype(BF)

    blocks(8, 64, norm2)

    w_up = m.w2[:, :, :, 0:D].reshape(D, D)
    m.pre[...] = dot(m.nm[...], w_up) + up_bias

    def gelu(rows, _):
        a = m.pre[rows, :]
        square = a * a
        bend = jnp.tanh(0.7978845608028654 * (a + 0.044715 * (square * a)))
        half = 0.5 * (1.0 + bend)
        m.act[rows, :] = (a * half).astype(BF)
        slope = half + (0.5 * a) * (1.0 - bend * bend) * (
            0.7978845608028654 * (1.0 + 0.134145 * square)
        )
        m.gp[rows, :] = (m.ga[rows, :] * slope).astype(BF)

    blocks(16, 32, gelu)

    def scatter_start(name):
        src, r1 = getattr(m, name + "_s"), getattr(m, name + "_1")
        return [
            send(rows_of(src, diag), r1.at[1], dev(s, sib, batch)),
            send(rows_of(src, sib), r1.at[0], dev(s, sib, batch)),
        ]

    def scatter_pass(name, copies):
        src, r1 = getattr(m, name + "_s"), getattr(m, name + "_1")
        cross, r2 = getattr(m, name + "_x"), getattr(m, name + "_2")
        copies[0].wait_recv()
        cross[...] = (get_rows(src, over).astype(F32) + r1[1].astype(F32)).astype(BF)
        copies.append(send(cross, r2, dev(s, over, batch)))

    def scatter_end(name, copies):
        src, r1 = getattr(m, name + "_s"), getattr(m, name + "_1")
        r2 = getattr(m, name + "_2")
        copies[1].wait_recv()
        copies[2].wait_recv()
        return get_rows(src, t).astype(F32) + r1[0].astype(F32) + r2[...].astype(F32)

    m.rm_s[...] = dot_nt(m.gp[...], m.w2[:, :, :, 0:D].reshape(D, D)).astype(BF)
    rm = scatter_start("rm")
    m.nmt[...] = m.nm[...].T
    scatter_pass("rm", rm)
    m.g2[:, :, :, 0:D] = dot(m.nmt[...], m.gp[...]).astype(BF).reshape(4, 4, 48, D)
    m.g2[:, :, :, D:] = dot(m.dot_[...], m.act[...]).astype(BF).reshape(4, 4, 48, D)

    def reduce_start(g, tag, half):
        rza, rxb = getattr(m, "rza" + tag), getattr(m, "rxb" + tag)
        a_cols, b_cols = pl.ds(0, half), pl.ds(half, half)
        a = [
            send(g.at[(z + k) % 4, :, :, a_cols], rza.at[k - 1],
                 dev(4 * ((z + k) % 4) + x, t, batch))
            for k in (1, 3, 2)
        ]
        b = [
            send(g.at[:, (x + k) % 4, :, b_cols], rxb.at[k - 1],
                 dev(4 * z + (x + k) % 4, t, batch))
            for k in (1, 3, 2)
        ]
        return a, b

    def add4(own, got):
        return (
            own.astype(F32) + got[0].astype(F32) + got[1].astype(F32) + got[2].astype(F32)
        )

    def reduce_pass(g, tag, half, phase):
        a, b = phase
        rza, rxb = getattr(m, "rza" + tag), getattr(m, "rxb" + tag)
        rxa, rzb = getattr(m, "rxa" + tag), getattr(m, "rzb" + tag)
        ha, hb = getattr(m, "ha" + tag), getattr(m, "hb" + tag)
        finish(a)
        for k in range(4):
            ha[k] = add4(g[z, k, :, 0:half], [rza[j, k] for j in range(3)]).astype(BF)
        a2 = [
            send(ha.at[(x + k) % 4], rxa.at[k - 1], dev(4 * z + (x + k) % 4, t, batch))
            for k in (1, 3, 2)
        ]
        finish(b)
        for k in range(4):
            hb[k] = add4(g[k, x, :, half:], [rxb[j, k] for j in range(3)]).astype(BF)
        b2 = [
            send(hb.at[(z + k) % 4], rzb.at[k - 1], dev(4 * ((z + k) % 4) + x, t, batch))
            for k in (1, 3, 2)
        ]
        return a2 + b2

    row64 = iota((64, 48), 0)
    expand = (
        (iota((64, 48), 1) == row64 - 4 * (row64 // 16)) & (row64 % 16 < 12)
    ).astype(BF)

    def reduce_last(tag, half, phase):
        rxa, rzb = getattr(m, "rxa" + tag), getattr(m, "rzb" + tag)
        ha, hb = getattr(m, "ha" + tag), getattr(m, "hb" + tag)
        fx, fin = getattr(m, "fx" + tag), getattr(m, "fin" + tag)
        finish(phase)
        a = add4(ha[x], [rxa[j] for j in range(3)]).astype(BF)
        b = add4(hb[z], [rzb[j] for j in range(3)]).astype(BF)
        fx[:, :, 0:half] = dot(expand, a).astype(BF).reshape(4, 16, half)
        fx[:, :, half:] = dot(expand, b).astype(BF).reshape(4, 16, half)
        mine = 4 * batch + t
        copies = [
            send(fx.at[u], fin.at[mine], dev(s, u, 1 - batch)) for u in (over, diag, sib, t)
        ]
        copies += [send(fx.at[u], fin.at[mine], dev(s, u, batch)) for u in group]
        fin[mine] = fx[t]
        return copies

    rg2 = reduce_start(m.g2, "2", D)
    m.ro_s[...] = dot_nt(m.act[...], m.w2[:, :, :, D:].reshape(D, D)).astype(BF)

    m.gm[...] = scatter_end("rm", rm)
    own = t * ROWS
    zero_row = jnp.zeros((1, D), F32)

    def norm_back(values, grads, gain):
        center, scale = norm_stats(values)
        unit = center * scale
        inner = grads * gain
        return (
            scale * (
                inner
                - jnp.mean(inner, axis=-1, keepdims=True)
                - unit * jnp.mean(inner * unit, axis=-1, keepdims=True)
            ),
            jnp.sum(grads * unit, axis=0, keepdims=True),
            jnp.sum(grads, axis=0, keepdims=True),
        )

    g_gain2, g_shift2, g_obias, g_dbias = zero_row, zero_row, zero_row, zero_row
    for k in range(2):
        at = pl.ds(pl.multiple_of(own + 64 * k, 64), 64)
        here = slice(64 * k, 64 * k + 64)
        into, d_gain, d_shift = norm_back(m.hid[at, :], m.gm[here, :], gain2)
        cot = dout[here, :].astype(F32)
        into = into + cot
        m.gh[here, :] = into
        low = into.astype(BF)
        m.gbr[here, :] = low
        g_gain2 += d_gain
        g_shift2 += d_shift
        g_obias += jnp.sum(low.astype(F32), axis=0, keepdims=True)
        g_dbias += jnp.sum(cot, axis=0, keepdims=True)
    for u in range(4):
        m.sa[u] = dot_nt(m.gbr[...], m.wof[HW * u:HW * u + HW, :]).astype(BF)
    aa = [send(m.sa.at[u], m.do.at[t], dev(s, u, batch)) for u in group]
    m.do[t] = m.sa[t]
    for u in range(4):
        m.sb[u] = m.gbr[:, HW * u:HW * u + HW]
    ab = [send(m.sb.at[u], m.gba.at[t], dev(s, u, batch)) for u in group]
    m.gba[t] = m.sb[t]
    ro = scatter_start("ro")
    for u in range(4):
        m.attt[HW * u:HW * u + HW, :] = m.atta[u].T
    qt = m.q[...].T
    scatter_pass("ro", ro)
    ends_g2 = reduce_pass(m.g2, "2", D, rg2)
    finish(aa)

    do_all = m.do[...].reshape(SEG, HW)
    dot_t = do_all.T
    weighed = do_all.astype(F32) * m.att[...]
    delta = [jnp.sum(of_head(weighed, h), axis=-1, keepdims=True) for h in range(HEADS)]
    m.dq[...] = jnp.zeros((SEG, HW), F32)
    delta_of = jnp.concatenate(delta, axis=1)
    m.att[:, 0:HEADS] = delta_of

    for h in range(HEADS):
        d_head = of_head(do_all, h)
        m.ssum[...] = dot_nt(d_head, m.kv[1, SEG:, :])

        def back_sum(rows, _, h=h):
            w = m.prob[h, rows, SEG:].astype(F32)
            m.ds[rows, :] = (w * (m.ssum[rows, :] - m.att[rows, h:h + 1])).astype(BF)

        blocks(16, 32, back_sum, unroll=2)
        m.dq[...] += dot(m.ds[...], of_head(m.kv[0, SEG:, :], h))
        feat = slice(64 * h, 64 * h + 64)
        m.dkst[feat, :] = dot(qt[feat, :], m.ds[...])
        m.dvst[feat, :] = dot(dot_t[feat, :], m.prob[h, :, SEG:])
    m.dkvs[0] = m.dkst[...].T.astype(BF)
    m.dkvs[1] = m.dvst[...].T.astype(BF)
    grad_at = take(16)

    def grad_copy(j):
        return pltpu.make_async_remote_copy(
            src_ref=m.dkvs.at[:, pl.ds(SLOT * j, SLOT), :],
            dst_ref=m.sumg.at[s],
            send_sem=ss.at[grad_at + j], recv_sem=rs.at[grad_at + s],
            device_id=dev(j, t, batch), device_id_type=MESH,
        )

    for j in range(15):
        @pl.when(j < s)
        def _(j=j):
            grad_copy(j).start()

    for h in range(HEADS):
        m.sloc[h] = dot_nt(of_head(do_all, h), m.kv[1, 0:SEG, :])
    for h in range(HEADS):
        def back_own(rows, _, h=h):
            w = m.prob[h, rows, 0:SEG].astype(F32)
            m.ds[rows, 0:SEG] = (w * (m.sloc[h, rows, :] - m.att[rows, h:h + 1])).astype(BF)

        blocks(8, 64, back_own, unroll=2)
        score_grads = m.ds[:, 0:SEG]
        m.dq[...] += dot(score_grads, of_head(m.kv[0, 0:SEG, :], h))
        feat = slice(64 * h, 64 * h + 64)
        m.dkt[feat, :] = dot(qt[feat, :], score_grads)
        m.dvt[feat, :] = dot(dot_t[feat, :], m.prob[h, :, 0:SEG])
    fin_g2 = reduce_last("2", D, ends_g2)
    finish(ab)
    grad_out_cols = m.gba[...].reshape(SEG, HW)
    g_o = dot(m.attt[...], grad_out_cols)

    for j in range(1, 16):
        @pl.when(j > s)
        def _(j=j):
            pltpu.make_async_remote_copy(
                src_ref=m.dkvs.at[:, pl.ds(0, SLOT), :],
                dst_ref=m.sumg.at[j],
                send_sem=ss.at[grad_at + j], recv_sem=rs.at[grad_at + j],
                device_id=dev(j, t, batch), device_id_type=MESH,
            ).wait_recv()

    def returned(which):
        total = m.sumg[0, which].astype(F32)
        for j in range(1, SLOTS):
            total = total + m.sumg[j, which].astype(F32)
        high = total.astype(BF)
        rest = (total - high.astype(F32)).astype(BF)
        return dot_tn(high, pick) + dot_tn(rest, pick)

    dk = (m.dkt[...] + returned(0)).T.astype(BF)
    dv = (m.dvt[...] + returned(1)).T.astype(BF)
    dq = m.dq[...].astype(BF) * jnp.asarray(0.125, BF)
    m.dqkv[...] = jnp.concatenate([dq, dk, dv], axis=1)

    m.rn_s[...] = dot_nt(m.dqkv[...], m.w1[...].reshape(D, D)[:, 0:3 * HW]).astype(BF)
    rn = scatter_start("rn")
    g_qkv = dot(m.nrmt[...], m.dqkv[...])
    m.g1[...] = jnp.concatenate([g_qkv, g_o], axis=1).astype(BF).reshape(4, 4, 48, D)
    rg1 = reduce_start(m.g1, "1", D // 2)
    scatter_pass("rn", rn)
    out_o[...] = (
        scatter_end("ro", ro) + get_rows(m.hid, t) + down_bias
    ).astype(BF)
    g_qb = jnp.sum(dq.astype(F32), axis=0, keepdims=True)
    g_vb = jnp.sum(dv.astype(F32), axis=0, keepdims=True)
    g_ub = zero_row
    for k in range(4):
        g_ub += jnp.sum(m.gp[ROWS * k:ROWS * k + ROWS, :].astype(F32), axis=0, keepdims=True)

    def in_place(row):
        none = jnp.zeros((1, HW), F32)
        return jnp.concatenate([jnp.where(t == u, row, none) for u in range(4)], axis=1)

    g_qb, g_vb = in_place(g_qb), in_place(g_vb)
    m.gm[...] = scatter_end("rn", rn)
    g_gain1, g_shift1 = zero_row, zero_row
    for k in range(2):
        here = slice(64 * k, 64 * k + 64)
        into, d_gain, d_shift = norm_back(tok[here, :].astype(F32), m.gm[here, :], gain1)
        gtok_o[here, :] = into + m.gh[here, :]
        g_gain1 += d_gain
        g_shift1 += d_shift
    rows8 = (g_gain1, g_shift1, g_qb, g_vb, g_obias, g_gain2, g_shift2, g_dbias)
    m.vgr[...] = jnp.zeros((16, D), F32)
    for k, row in enumerate(rows8):
        m.vgr[k:k + 1, :] = row
    for u in range(4):
        m.vgr[8 + u:9 + u, :] = jnp.where(t == u, g_ub, zero_row)
    vgx = [
        send(m.vgr, m.vgx.at[k - 1], dev(4 * z + (x + k) % 4, t, batch)) for k in (1, 2, 3)
    ]
    ends_g1 = reduce_pass(m.g1, "1", D // 2, rg1)
    finish(vgx)
    m.vgs[...] = add4(m.vgr[...], [m.vgx[j] for j in range(3)])
    vgz = [
        send(m.vgs, m.vgz.at[k - 1], dev(4 * ((z + k) % 4) + x, t, batch)) for k in (1, 2, 3)
    ]
    fin_g1 = reduce_last("1", D // 2, ends_g1)
    finish(vgz)
    m.vgt[...] = add4(m.vgs[...], [m.vgz[j] for j in range(3)])
    mine = 4 * batch + t
    fin_v = [send(m.vgt, m.vfin.at[mine], dev(s, u, 1 - batch)) for u in (over, diag, sib, t)]
    fin_v += [send(m.vgt, m.vfin.at[mine], dev(s, u, batch)) for u in group]
    m.vfin[mine] = m.vgt[...]

    def both(fin, u, cols):
        return fin[u, 0:12, cols].astype(F32) + fin[4 + u, 0:12, cols].astype(F32)

    finish(fin_g2)
    for u in range(4):
        wide = slice(D * u, D * u + D)
        gu_o[:, wide] = both(m.fin2, u, slice(0, D))
        gd_o[:, wide] = both(m.fin2, u, slice(D, 2 * D))
    finish(fin_g1)
    parts = [both(m.fin1, u, slice(0, D)) for u in range(4)]
    for k, ref in enumerate((gq_o, gk_o, gv_o, go_o)):
        ref[...] = jnp.concatenate([p[:, HW * k:HW * k + HW] for p in parts], axis=1)
    finish(fin_v)
    total = m.vfin[0]
    for k in range(1, 8):
        total = total + m.vfin[k]
    back = iota((D, 128), 0) - iota((D, 128), 1)
    lane = iota((D, 128), 1)
    get_12 = ((back == 12 * place) & (lane < 12)).astype(F32)
    get_48 = ((back == 48 * (place % 16)) & (lane < 48)).astype(F32)
    small = dot(total, get_12, precision=HIGHEST)
    large = dot(total, get_48, precision=HIGHEST)
    row16 = iota((16, 128), 0)
    chosen = jnp.sum(jnp.where(row16 == 8 + z, large, 0.0), axis=0, keepdims=True)
    gvec_o[...] = jnp.where(row16 < 8, small, jnp.where(row16 == 8, chosen, 0.0))

    for copy in sent:
        copy.wait_send()
    for j in range(1, 16):
        @pl.when(j > s)
        def _(j=j):
            sum_copy(j).wait_send()
    for j in range(15):
        @pl.when(j < s)
        def _(j=j):
            grad_copy(j).wait_send()
    assert used[0] <= COPIES, used[0]


def body(
    tokens, seg_lengths, ln1_gain, ln1_bias, w_query, q_bias, w_key, w_value, v_bias,
    w_out, o_bias, ln2_gain, ln2_bias, w_up, up_bias, w_down, down_bias, d_out,
):
    narrow = jnp.stack(
        [ln1_gain, ln1_bias, q_bias, v_bias, o_bias, ln2_gain, ln2_bias, down_bias]
    )
    vec = jnp.zeros((16, 128), BF)
    vec = vec.at[0:8, 0:12].set(narrow).at[8, 0:48].set(up_bias)
    shape = jax.ShapeDtypeStruct
    vmem = pl.BlockSpec(memory_space=pltpu.VMEM)
    outs = pl.pallas_call(
        layer_kernel,
        out_shape=[
            shape((ROWS, D), BF),
            shape((ROWS, D), F32),
            shape((12, D), F32),
            shape((12, D), F32),
            shape((12, D), F32),
            shape((12, D), F32),
            shape((12, 4 * D), F32),
            shape((12, 4 * D), F32),
            shape((16, 128), F32),
        ],
        in_specs=[pl.BlockSpec(memory_space=pltpu.SMEM)] + [vmem] * 9,
        out_specs=[vmem] * 9,
        scratch_shapes=[pltpu.VMEM(dims, kind) for dims, kind in SCRATCH.values()]
        + [pltpu.SemaphoreType.DMA((COPIES,)), pltpu.SemaphoreType.DMA((COPIES,))],
        compiler_params=pltpu.CompilerParams(
            collective_id=0, has_side_effects=True, vmem_limit_bytes=62 * 2**20
        ),
        name="layer",
    )(
        seg_lengths, tokens[0], d_out[0], w_query, w_key, w_value, w_out, w_up, w_down, vec
    )
    out, g_tok, g_q, g_k, g_v, g_o, g_up, g_down, g_vec = outs
    return (
        out[None],
        g_tok[None],
        g_vec[0, 0:12],
        g_vec[1, 0:12],
        g_q,
        g_vec[2, 0:12],
        g_k,
        g_v,
        g_vec[3, 0:12],
        g_o,
        g_vec[4, 0:12],
        g_vec[5, 0:12],
        g_vec[6, 0:12],
        g_up,
        g_vec[8, 0:48],
        g_down,
        g_vec[7, 0:12],
    )


def solution(mesh):
    rows, cols = P("batch", "seq", None), P("seq", None)
    one = P("seq")
    placed = (
        rows, P("batch", None), one, one, cols, one, cols, cols, one,
        cols, one, one, one, cols, one, cols, one, rows,
    )
    return jax.shard_map(
        body,
        mesh=mesh,
        in_specs=placed,
        out_specs=(
            rows, rows, one, one, cols, one, cols, cols, one,
            cols, one, one, one, cols, one, cols, one,
        ),
        check_vma=False,
    )
```

```python
import functools
import types

import jax
import jax.numpy as jnp
from jax import lax
from jax.experimental import pallas as pl
from jax.experimental.pallas import tpu as pltpu
from jax.sharding import PartitionSpec as P

BF = jnp.bfloat16
F32 = jnp.float32
MESH = pl.DeviceIdType.MESH
EPSILON = 1e-05
MASKED = -1e30
HIGHEST = lax.Precision.HIGHEST

ROWS = 128
SEG = 512
D = 768
HW = 192
HEADS = 3
HALF = 64
CHUNK = 256
SUMMARY = 50
SLOT = 64
SLOTS = 16
SUMS = SLOTS * SLOT


def dot(a, b, **kw):
    return jnp.dot(a, b, preferred_element_type=F32, **kw)


def dot_nt(a, b):
    return lax.dot_general(a, b, (((1,), (1,)), ((), ())), preferred_element_type=F32)


def dot_tn(a, b):
    return lax.dot_general(a, b, (((0,), (0,)), ((), ())), preferred_element_type=F32)


def iota(shape, dim):
    return lax.broadcasted_iota(jnp.int32, shape, dim)


def norm_stats(values):
    center = values - jnp.mean(values, axis=-1, keepdims=True)
    spread = jnp.mean(center * center, axis=-1, keepdims=True)
    return center, lax.rsqrt(spread + EPSILON)


SCRATCH = dict(
    pk1=((4, 16, D), BF),
    pk2=((4, 16, 2 * D), BF),
    p01=((4, 16, D), BF),
    p02=((4, 16, 2 * D), BF),
    w1=((4, 4, 48, D), BF),
    w2=((4, 4, 48, 2 * D), BF),
    wosl=((4, D, HW), BF),
    wof=((D, D), BF),
    vin=((16, 128), F32),
    vb=((16, D), BF),
    vg=((3, 16, D), BF),
    vs1=((16, D), BF),
    vx=((3, 16, D), BF),
    vs2=((16, D), BF),
    vz=((3, 16, D), BF),
    vecs=((16, D), F32),
    toka=((SEG, D), BF),
    doa=((SEG, D), BF),
    nrm=((SEG, D), BF),
    nrmt=((D, SEG), BF),
    dot_=((D, SEG), BF),
    stat=((SEG, 128), F32),
    bias=((SEG, SEG), F32),
    q=((SEG, HW), BF),
    kv=((2, SEG, HW), BF),
    kvs=((2, SUMS, HW), BF),
    ssrc=((2, SLOT, HW), BF),
    sloc=((HEADS, SEG, SEG), F32),
    ssum=((SEG, SUMS), F32),
    prob1=((HEADS, SEG, SEG), BF),
    prob2=((HEADS, SEG, SUMS), BF),
    m1=((SEG, 128), F32),
    l1=((SEG, 128), F32),
    m2=((SEG, 128), F32),
    l2=((SEG, 128), F32),
    a1=((SEG, 128), F32),
    a2=((SEG, 128), F32),
    delta=((SEG, 128), F32),
    a1x=((SEG, HW), F32),
    a2x=((SEG, HW), F32),
    o1=((SEG, HW), F32),
    att=((SEG, HW), F32),
    atta=((4, SEG, HW), BF),
    attt=((D, SEG), BF),
    hid=((SEG, D), F32),
    nm=((SEG, D), BF),
    nmt=((D, SEG), BF),
    pre=((SEG, D), F32),
    ga=((SEG, D), F32),
    act=((SEG, D), BF),
    gp=((SEG, D), BF),
    rm_s=((SEG, D), BF),
    rm_1=((2, 2, HALF, D), BF),
    rm_x=((2, HALF, D), BF),
    rm_2=((2, HALF, D), BF),
    ro_s=((SEG, D), BF),
    ro_1=((2, 2, HALF, D), BF),
    ro_x=((2, HALF, D), BF),
    ro_2=((2, HALF, D), BF),
    rn_s=((SEG, D), BF),
    rn_1=((2, 2, HALF, D), BF),
    rn_x=((2, HALF, D), BF),
    rn_2=((2, HALF, D), BF),
    gh=((ROWS, D), F32),
    gbr=((ROWS, D), BF),
    sa=((2, 4, HALF, HW), BF),
    sb=((2, 4, HALF, HW), BF),
    do=((2, 4, HALF, HW), BF),
    gba=((2, 4, HALF, HW), BF),
    ds=((SEG, SUMS), BF),
    dq=((SEG, HW), F32),
    dkt=((HW, SEG), F32),
    dvt=((HW, SEG), F32),
    dkst=((HW, SUMS), F32),
    dvst=((HW, SUMS), F32),
    dkvs=((2, SUMS, HW), BF),
    sumg=((SLOTS, 2, SLOT, HW), BF),
    dqkv=((SEG, 3 * HW), BF),
    g1=((4, 4, 48, D), BF),
    g2=((4, 4, 48, 2 * D), BF),
    rza1=((3, 4, 48, D // 2), BF),
    rxa1=((3, 48, D // 2), BF),
    rxb1=((3, 4, 48, D // 2), BF),
    rzb1=((3, 48, D // 2), BF),
    ha1=((4, 48, D // 2), BF),
    hb1=((4, 48, D // 2), BF),
    rza2=((3, 4, 48, D), BF),
    rxa2=((3, 48, D), BF),
    rxb2=((3, 4, 48, D), BF),
    rzb2=((3, 48, D), BF),
    ha2=((4, 48, D), BF),
    hb2=((4, 48, D), BF),
    fx1=((4, 16, D), BF),
    fx2=((4, 16, 2 * D), BF),
    fin1=((8, 16, D), BF),
    fin2=((8, 16, 2 * D), BF),
    vgr=((16, D), F32),
    vgx=((3, 16, D), F32),
    vgs=((16, D), F32),
    vgz=((3, 16, D), F32),
    vgt=((16, D), F32),
    vfin=((8, 16, D), F32),
)
SENDS = 24
RECVS = 100


class Flight:
    def __init__(self, waiter):
        self.waiter = waiter
        self.arrived = False
        self.left = False

    def wait_recv(self):
        if not self.arrived:
            self.waiter.wait_recv()
        self.arrived = True

    def wait_send(self):
        if not self.left:
            self.waiter.wait_send()
        self.left = True


def layer_kernel(
    seg_ref, tok, dout, wq, wk, wv, wo, wu, wd, *refs,
):
    vectors, refs = refs[:9], refs[9:]
    out_o, gtok_o, gq_o, gk_o, gv_o, go_o, gu_o, gd_o, gvec_o = refs[:9]
    scratch = refs[9:]
    m = types.SimpleNamespace(**dict(zip(SCRATCH, scratch[:-3])))
    ss, rs, sum_ss = scratch[-3:]
    batch = lax.axis_index("batch")
    place = lax.axis_index("seq")
    s = place // 4
    t = place % 4
    z = s // 4
    x = s % 4
    sib = t + 1 - 2 * (t % 2)
    over = (t + 2) % 4
    diag = 3 - t
    group = (over, diag, sib)

    def dev(seg, tt, bb):
        return (4 * seg + tt, bb)

    def here(tt):
        return dev(s, tt, batch)

    def along_x(k):
        return dev(4 * z + (x + k) % 4, t, batch)

    def along_z(k):
        return dev(4 * ((z + k) % 4) + x, t, batch)

    used = [0]
    sent = []

    def take(n=1):
        first = used[0]
        used[0] += n
        return first

    def fly(copies, total=None):
        k = len(sent)
        if k >= SENDS:
            sent[k - SENDS].wait_send()
        send_sem, recv_sem = ss.at[k % SENDS], rs.at[take()]
        for src, dst, device in copies:
            copy = pltpu.make_async_remote_copy(
                src_ref=src, dst_ref=dst, send_sem=send_sem, recv_sem=recv_sem,
                device_id=device, device_id_type=MESH,
            )
            copy.start()
        if total is not None:
            copy = pltpu.make_async_remote_copy(
                src_ref=total, dst_ref=total, send_sem=send_sem, recv_sem=recv_sem,
                device_id=device, device_id_type=MESH,
            )
        flight = Flight(copy)
        sent.append(flight)
        return flight

    def block(c, k):
        return pl.ds(pl.multiple_of(CHUNK * c + HALF * k, HALF), HALF)

    def loop(first, count, size, fn, unroll=1):
        def step(j, carry):
            fn(pl.ds(pl.multiple_of(first + j * size, size), size))
            return carry

        lax.fori_loop(0, count, step, 0, unroll=unroll)

    m.kvs[...] = jnp.zeros((2, SUMS, HW), BF)
    m.sumg[...] = jnp.zeros((SLOTS, 2, SLOT, HW), BF)
    barrier = pltpu.get_barrier_semaphore()
    partners = [here(u) for u in group]
    partners += [dev((s + k) % 16, t, batch) for k in range(1, 16)]
    partners += [dev(s, u, 1 - batch) for u in (t, sib, over, diag)]
    for partner in partners:
        pl.semaphore_signal(barrier, inc=1, device_id=partner, device_id_type=MESH)
    m.pk1[...] = jnp.zeros((4, 16, D), BF)
    for u in range(4):
        cols = slice(HW * u, HW * u + HW)
        m.pk1[u, 0:12, :] = jnp.concatenate(
            [wq[:, cols], wk[:, cols], wv[:, cols], wo[:, cols]], axis=1
        )
    m.vin[...] = jnp.zeros((16, 128), F32)
    for k, ref in enumerate(vectors[:8]):
        m.vin[k:k + 1, 0:12] = ref[...].astype(F32)
    m.vin[8:9, 0:48] = vectors[8][...].astype(F32)
    shift = iota((128, D), 1) - iota((128, D), 0)
    narrow = dot(m.vin[...].astype(BF), (shift == 12 * place).astype(BF))
    wider = dot(m.vin[...].astype(BF), (shift == 48 * (place % 16)).astype(BF))
    vec_row = iota((16, D), 0)
    m.vb[...] = jnp.where(
        vec_row < 8, narrow, jnp.where(vec_row == 8 + z, wider[8:9, :], 0.0)
    ).astype(BF)
    pl.semaphore_wait(barrier, len(partners))

    first1 = fly([(m.pk1.at[u], m.p01.at[t], here(u)) for u in group], m.p01.at[0:3])
    firstv = fly(
        [(m.vb, m.vg.at[k], here(u)) for k, u in enumerate((sib, over, diag))], m.vg
    )
    m.p01[t] = m.pk1[t]
    m.pk2[...] = jnp.zeros((4, 16, 2 * D), BF)
    for u in range(4):
        wide = slice(D * u, D * u + D)
        m.pk2[u, 0:12, 0:D] = wu[:, wide]
        m.pk2[u, 0:12, D:] = wd[:, wide]
    m.p02[t] = m.pk2[t]
    for c in range(2):
        m.toka[block(c, t), :] = tok[HALF * c:HALF * c + HALF, :]
        m.doa[block(c, t), :] = dout[HALF * c:HALF * c + HALF, :]

    def gather_start(ref):
        moves = [
            fly([(ref.at[block(c, t)], ref.at[block(c, t)], here(u)) for c in (0, 1)],
                ref.at[0:ROWS])
            for u in (over, sib)
        ]
        return moves

    def gather_pass(moves, ref):
        moves[0].wait_recv()
        moves.append(
            fly([(ref.at[block(c, over)], ref.at[block(c, over)], here(sib)) for c in (0, 1)],
                ref.at[0:ROWS])
        )

    def finish(moves):
        for move in moves:
            move.wait_recv()

    row48 = iota((48, 64), 0)
    owner48 = (
        (row48 >= 12).astype(jnp.int32)
        + (row48 >= 24).astype(jnp.int32)
        + (row48 >= 36).astype(jnp.int32)
    )
    squeeze = (iota((48, 64), 1) == row48 + 4 * owner48).astype(BF)

    def spread_start(w, half):
        a, b = pl.ds(0, half), pl.ds(half, half)
        mine_a, mine_b = w.at[z, x, :, a], w.at[z, x, :, b]
        return (
            fly([(mine_a, mine_a, along_x(k)) for k in (1, 3, 2)], w.at[0, 0:3, :, a]),
            fly([(mine_b, mine_b, along_z(k)) for k in (1, 3, 2)], w.at[0, 0:3, :, b]),
        )

    def spread_pass(w, half, moves):
        a, b = pl.ds(0, half), pl.ds(half, half)
        plane_a, plane_b = w.at[z, :, :, a], w.at[:, x, :, b]
        moves[0].wait_recv()
        a2 = fly([(plane_a, plane_a, along_z(k)) for k in (1, 3, 2)], w.at[0:3, :, :, a])
        moves[1].wait_recv()
        b2 = fly([(plane_b, plane_b, along_x(k)) for k in (1, 3, 2)], w.at[0:3, :, :, b])
        return a2, b2

    first1.wait_recv()
    m.w1[z, x] = dot(squeeze, m.p01[...].reshape(64, D)).astype(BF)
    phase1 = spread_start(m.w1, D // 2)
    first2 = fly([(m.pk2.at[u], m.p02.at[t], here(u)) for u in group], m.p02.at[0:3])
    ag_tok = gather_start(m.toka)

    seg_len = seg_ref[0, s]

    def token_of(rows):
        return rows + 64 * ((rows % CHUNK) // HALF) - 192 * (rows // CHUNK)

    k_pos = token_of(iota((1, SEG), 1))

    def mask(rows):
        mine = token_of(rows.start + iota((ROWS, 1), 0))
        ok = ((k_pos <= mine) & (k_pos < seg_len)) | (k_pos == mine)
        m.bias[rows, :] = jnp.where(ok, 0.0, MASKED)

    loop(0, 4, ROWS, mask)
    s_col = iota((8, SUMS), 1)
    sum_bias = jnp.where((s_col < SLOT * s) & (s_col % SLOT < SUMMARY), 0.0, MASKED)[0:1, :]
    pick_row = iota((SLOT, SEG), 0)
    pick = ((k_pos == seg_len - SUMMARY + pick_row) & (pick_row < SUMMARY)).astype(BF)
    lane_head = iota((1, HW), 1) // 64

    def of_head(value, h):
        return jnp.where(lane_head == h, value, jnp.zeros_like(value))

    def by_head(cols):
        return jnp.where(
            lane_head == 0, cols[:, 0:1], jnp.where(lane_head == 1, cols[:, 1:2], cols[:, 2:3])
        )

    def add4(own, got):
        return own.astype(F32) + got[0].astype(F32) + got[1].astype(F32) + got[2].astype(F32)

    firstv.wait_recv()
    m.vs1[...] = add4(m.vb[...], m.vg).astype(BF)
    vx = fly([(m.vs1, m.vx.at[k - 1], along_x(k)) for k in (1, 2, 3)], m.vx)
    ends1 = spread_pass(m.w1, D // 2, phase1)
    vx.wait_recv()
    m.vs2[...] = add4(m.vs1[...], m.vx).astype(BF)
    vz = fly([(m.vs2, m.vz.at[k - 1], along_z(k)) for k in (1, 2, 3)], m.vz)
    first2.wait_recv()
    m.w2[z, x] = dot(squeeze, m.p02[...].reshape(64, 2 * D)).astype(BF)
    gather_pass(ag_tok, m.toka)
    vz.wait_recv()
    m.vecs[...] = add4(m.vs2[...], m.vz)
    gain1, shift1 = m.vecs[0:1, :], m.vecs[1:2, :]
    gain2, shift2 = m.vecs[5:6, :], m.vecs[6:7, :]
    o_bias, down_bias = m.vecs[4:5, :], m.vecs[7:8, :]

    def my_cols(row):
        whole = m.vecs[row:row + 1, :]
        value = whole[:, 0:HW]
        for u in range(1, 4):
            value = jnp.where(t == u, whole[:, HW * u:HW * u + HW], value)
        return value

    q_bias, v_bias = my_cols(2), my_cols(3)
    up_bias = m.vecs[8:9, :]
    for u in range(1, 4):
        up_bias = jnp.where(t == u, m.vecs[8 + u:9 + u, :], up_bias)

    finish(ag_tok)

    def norm1(rows):
        values = m.toka[rows, :].astype(F32)
        mean = jnp.mean(values, axis=-1, keepdims=True)
        center = values - mean
        scale = lax.rsqrt(jnp.mean(center * center, axis=-1, keepdims=True) + EPSILON)
        m.nrm[rows, :] = (center * scale * gain1 + shift1).astype(BF)
        m.stat[rows, 0:1] = mean
        m.stat[rows, 1:2] = scale

    loop(0, 4, ROWS, norm1)
    m.nrmt[...] = m.nrm[...].T

    finish(ends1)
    phase2 = spread_start(m.w2, D)
    w1 = m.w1[...].reshape(D, D)
    qkv = dot(m.nrm[...], w1)
    m.q[...] = ((qkv[:, 0:HW] + q_bias) * 0.125).astype(BF)
    m.kv[0] = qkv[:, HW:2 * HW].astype(BF)
    m.kv[1] = (qkv[:, 2 * HW:3 * HW] + v_bias).astype(BF)

    m.ssrc[0] = dot(pick, m.kv[0]).astype(BF)
    m.ssrc[1] = dot(pick, m.kv[1]).astype(BF)
    sum_at = take(16)

    def sum_copy(j):
        return pltpu.make_async_remote_copy(
            src_ref=m.ssrc,
            dst_ref=m.kvs.at[:, pl.ds(pl.multiple_of(SLOT * s, SLOT), SLOT), :],
            send_sem=sum_ss.at[j], recv_sem=rs.at[sum_at + s],
            device_id=dev(j, t, batch), device_id_type=MESH,
        )

    def sum_arrived(j):
        pltpu.make_async_remote_copy(
            src_ref=m.ssrc,
            dst_ref=m.kvs.at[:, pl.ds(SLOT * j, SLOT), :],
            send_sem=sum_ss.at[j], recv_sem=rs.at[sum_at + j],
            device_id=dev(j, t, batch), device_id_type=MESH,
        ).wait_recv()

    for j in range(1, 16):
        @pl.when(j > s)
        def _(j=j):
            sum_copy(j).start()
    m.wosl[t] = m.w1[...].reshape(D, D)[:, 3 * HW:]
    ag_wo = [fly([(m.wosl.at[t], m.wosl.at[t], here(u))]) for u in (over, sib)]

    for h in range(HEADS):
        m.sloc[h] = dot_nt(of_head(m.q[...], h), m.kv[0]) + m.bias[...]
    for h in range(HEADS):
        def soften1(rows, h=h):
            score = m.sloc[h, rows, :]
            peak = jnp.max(score, axis=-1, keepdims=True)
            power = jnp.exp(score - peak)
            m.prob1[h, rows, :] = power.astype(BF)
            m.m1[rows, h:h + 1] = peak
            m.l1[rows, h:h + 1] = jnp.sum(power, axis=-1, keepdims=True)

        loop(0, 4, ROWS, soften1)
        part = dot(m.prob1[h], of_head(m.kv[1], h))
        m.o1[...] = part if h == 0 else m.o1[...] + part
    ag_wo[0].wait_recv()
    ag_wo.append(fly([(m.wosl.at[over], m.wosl.at[over], here(sib))]))
    ag_do = gather_start(m.doa)

    for j in range(15):
        @pl.when(j < s)
        def _(j=j):
            sum_arrived(j)
    ends2 = spread_pass(m.w2, D, phase2)

    ag_att = []
    for c in range(2):
        rows_c = slice(CHUNK * c, CHUNK * c + CHUNK)
        part = None
        for h in range(HEADS):
            m.ssum[rows_c, :] = dot_nt(of_head(m.q[rows_c, :], h), m.kvs[0]) + sum_bias

            def soften2(rows, h=h):
                score = m.ssum[rows, :]
                peak = jnp.max(score, axis=-1, keepdims=True)
                power = jnp.exp(score - peak)
                m.prob2[h, rows, :] = power.astype(BF)
                m.m2[rows, h:h + 1] = peak
                m.l2[rows, h:h + 1] = jnp.sum(power, axis=-1, keepdims=True)

            loop(CHUNK * c, 2, ROWS, soften2)
            more = dot(m.prob2[h, rows_c, :], of_head(m.kvs[1], h))
            part = more if h == 0 else part + more
        m1, m2 = m.m1[rows_c, 0:HEADS], m.m2[rows_c, 0:HEADS]
        peak = jnp.maximum(m1, m2)
        e1, e2 = jnp.exp(m1 - peak), jnp.exp(m2 - peak)
        share = 1.0 / (m.l1[rows_c, 0:HEADS] * e1 + m.l2[rows_c, 0:HEADS] * e2)
        a1, a2 = e1 * share, e2 * share
        m.a1[rows_c, 0:HEADS] = a1
        m.a2[rows_c, 0:HEADS] = a2
        a1x, a2x = by_head(a1), by_head(a2)
        m.a1x[rows_c, :] = a1x
        m.a2x[rows_c, :] = a2x
        attended = m.o1[rows_c, :] * a1x + part * a2x
        m.att[rows_c, :] = attended
        m.atta[t, rows_c, :] = attended.astype(BF)
        mine_c = m.atta.at[t, rows_c]
        ag_att.append([fly([(mine_c, mine_c, here(u))]) for u in (over, sib)])
        if c == 0:
            finish(ag_wo)
            m.wof[...] = jnp.concatenate([m.wosl[u] for u in range(4)], axis=1)

    def att_pass(c):
        rows_c = slice(CHUNK * c, CHUNK * c + CHUNK)
        ag_att[c][0].wait_recv()
        theirs = m.atta.at[over, rows_c]
        ag_att[c].append(fly([(theirs, theirs, here(sib))]))

    def scatter_start(name, cs):
        src, r1 = getattr(m, name + "_s"), getattr(m, name + "_1")
        return [
            fly([(src.at[block(c, k)], r1.at[c, i], here(sib)) for c in cs],
                r1.at[0:len(cs), i])
            for i, k in ((1, diag), (0, sib))
        ]

    def scatter_pass(name, cs, moves):
        src, r1 = getattr(m, name + "_s"), getattr(m, name + "_1")
        cross, r2 = getattr(m, name + "_x"), getattr(m, name + "_2")
        moves[0].wait_recv()
        for c in cs:
            cross[c] = (src[block(c, over), :].astype(F32) + r1[c, 1].astype(F32)).astype(BF)
        moves.append(
            fly([(cross.at[c], r2.at[c], here(over)) for c in cs], r2.at[0:len(cs)])
        )

    def scatter_end(name, c, moves):
        src, r1 = getattr(m, name + "_s"), getattr(m, name + "_1")
        r2 = getattr(m, name + "_2")
        moves[1].wait_recv()
        moves[2].wait_recv()
        return src[block(c, t), :].astype(F32) + r1[c, 0].astype(F32) + r2[c].astype(F32)

    def gelu(rows):
        a = m.pre[rows, :]
        square = a * a
        bend = jnp.tanh(0.7978845608028654 * (a + 0.044715 * (square * a)))
        half = 0.5 * (1.0 + bend)
        m.act[rows, :] = (a * half).astype(BF)
        slope = half + (0.5 * a) * (1.0 - bend * bend) * (
            0.7978845608028654 * (1.0 + 0.134145 * square)
        )
        m.gp[rows, :] = (m.ga[rows, :] * slope).astype(BF)

    def norm2(rows):
        center, scale = norm_stats(m.hid[rows, :])
        m.nm[rows, :] = (center * scale * gain2 + shift2).astype(BF)

    def project(c):
        rows_c = slice(CHUNK * c, CHUNK * c + CHUNK)
        finish(ag_att[c])
        branch = dot(m.atta[0, rows_c, :], m.wof[0:HW, :])
        for u in range(1, 4):
            branch = branch + dot(m.atta[u, rows_c, :], m.wof[HW * u:HW * u + HW, :])
        m.hid[rows_c, :] = m.toka[rows_c, :].astype(F32) + branch + o_bias
        loop(CHUNK * c, 2, ROWS, norm2)

    def feed(c):
        rows_c = slice(CHUNK * c, CHUNK * c + CHUNK)
        m.pre[rows_c, :] = dot(m.nm[rows_c, :], m.w2[:, :, :, 0:D].reshape(D, D)) + up_bias
        m.ga[rows_c, :] = dot(m.doa[rows_c, :], m.w2[:, :, :, D:].reshape(D, D))
        loop(CHUNK * c, 4, 64, gelu)
        m.rm_s[rows_c, :] = dot_nt(m.gp[rows_c, :], m.w2[:, :, :, 0:D].reshape(D, D)).astype(BF)
        return scatter_start("rm", (c,))

    gather_pass(ag_do, m.doa)
    att_pass(0)
    project(0)
    att_pass(1)
    finish(ag_do)
    finish(ends2)
    rm0 = feed(0)
    project(1)
    scatter_pass("rm", (0,), rm0)
    rm1 = feed(1)

    m.dot_[...] = m.doa[...].T
    m.nmt[...] = m.nm[...].T
    scatter_pass("rm", (1,), rm1)
    m.g2[:, :, :, 0:D] = dot(m.nmt[...], m.gp[...]).astype(BF).reshape(4, 4, 48, D)
    m.g2[:, :, :, D:] = dot(m.dot_[...], m.act[...]).astype(BF).reshape(4, 4, 48, D)

    def reduce_start(g, tag, half):
        rza, rxb = getattr(m, "rza" + tag), getattr(m, "rxb" + tag)
        a, b = pl.ds(0, half), pl.ds(half, half)
        return (
            fly([(g.at[(z + k) % 4, :, :, a], rza.at[k - 1], along_z(k)) for k in (1, 3, 2)], rza),
            fly([(g.at[:, (x + k) % 4, :, b], rxb.at[k - 1], along_x(k)) for k in (1, 3, 2)], rxb),
        )

    def reduce_pass(g, tag, half, moves):
        rza, rxb = getattr(m, "rza" + tag), getattr(m, "rxb" + tag)
        rxa, rzb = getattr(m, "rxa" + tag), getattr(m, "rzb" + tag)
        ha, hb = getattr(m, "ha" + tag), getattr(m, "hb" + tag)
        moves[0].wait_recv()
        for k in range(4):
            ha[k] = add4(g[z, k, :, 0:half], [rza[j, k] for j in range(3)]).astype(BF)
        a2 = fly([(ha.at[(x + k) % 4], rxa.at[k - 1], along_x(k)) for k in (1, 3, 2)], rxa)
        moves[1].wait_recv()
        for k in range(4):
            hb[k] = add4(g[k, x, :, half:], [rxb[j, k] for j in range(3)]).astype(BF)
        b2 = fly([(hb.at[(z + k) % 4], rzb.at[k - 1], along_z(k)) for k in (1, 3, 2)], rzb)
        return a2, b2

    row64 = iota((64, 48), 0)
    expand = (
        (iota((64, 48), 1) == row64 - 4 * (row64 // 16)) & (row64 % 16 < 12)
    ).astype(BF)
    mine = 4 * batch + t
    everyone = [(u, dev(s, u, 1 - batch)) for u in (over, diag, sib, t)]
    everyone += [(u, here(u)) for u in group]

    def reduce_last(tag, half, moves):
        rxa, rzb = getattr(m, "rxa" + tag), getattr(m, "rzb" + tag)
        ha, hb = getattr(m, "ha" + tag), getattr(m, "hb" + tag)
        fx, fin = getattr(m, "fx" + tag), getattr(m, "fin" + tag)
        finish(moves)
        a = add4(ha[x], [rxa[j] for j in range(3)]).astype(BF)
        b = add4(hb[z], [rzb[j] for j in range(3)]).astype(BF)
        fx[:, :, 0:half] = dot(expand, a).astype(BF).reshape(4, 16, half)
        fx[:, :, half:] = dot(expand, b).astype(BF).reshape(4, 16, half)
        moves = fly([(fx.at[u], fin.at[mine], device) for u, device in everyone], fin.at[0:7])
        fin[mine] = fx[t]
        return moves

    rg2 = reduce_start(m.g2, "2", D)

    zero_row = jnp.zeros((1, D), F32)
    ones = jnp.ones((8, SEG), BF)

    def col_sums(value):
        return dot(ones[:, 0:value.shape[0]], value)[0:1, :]

    def norm_back(values, grads, gain):
        center, scale = norm_stats(values)
        unit = center * scale
        inner = grads * gain
        return unit, scale * (
            inner
            - jnp.mean(inner, axis=-1, keepdims=True)
            - unit * jnp.mean(inner * unit, axis=-1, keepdims=True)
        )

    g_gain2, g_shift2 = zero_row, zero_row
    aa = []
    for c in range(2):
        at = slice(HALF * c, HALF * c + HALF)
        grads = scatter_end("rm", c, rm0 if c == 0 else rm1)
        unit, into = norm_back(m.hid[block(c, t), :], grads, gain2)
        into = into + dout[at, :].astype(F32)
        m.gh[at, :] = into
        low = into.astype(BF)
        m.gbr[at, :] = low
        for u in range(4):
            m.sa[c, u] = dot_nt(low, m.wof[HW * u:HW * u + HW, :]).astype(BF)
        aa.append(
            fly([(m.sa.at[c, u], m.do.at[c, t], here(u)) for u in group], m.do.at[c, 0:3])
        )
        m.do[c, t] = m.sa[c, t]
        g_gain2 += jnp.sum(grads * unit, axis=0, keepdims=True)
        g_shift2 += jnp.sum(grads, axis=0, keepdims=True)
    m.ro_s[...] = dot_nt(m.act[...], m.w2[:, :, :, D:].reshape(D, D)).astype(BF)
    for u in range(4):
        cols = m.gbr[:, HW * u:HW * u + HW]
        m.sb[0, u] = cols[0:HALF, :]
        m.sb[1, u] = cols[HALF:, :]
    qt = m.q[...].T
    m.dq[...] = jnp.zeros((SEG, HW), F32)

    finish(aa)
    do_all = m.do[...].reshape(SEG, HW)
    do_wide = do_all.astype(F32)
    weighed = do_wide * m.att[...]
    for h in range(HEADS):
        m.delta[:, h:h + 1] = jnp.sum(of_head(weighed, h), axis=-1, keepdims=True)
    dot1 = (do_wide * m.a1x[...]).astype(BF).T
    dot2 = (do_wide * m.a2x[...]).astype(BF).T
    ab = fly(
        [(m.sb.at[c, u], m.gba.at[c, t], here(u)) for u in group for c in (0, 1)],
        m.gba.at[:, 0:3],
    )
    m.gba[0, t] = m.sb[0, t]
    m.gba[1, t] = m.sb[1, t]
    ro = scatter_start("ro", (0, 1))
    for h in range(HEADS):
        m.ssum[...] = dot_nt(of_head(do_all, h), m.kvs[1])

        def back_sum(rows, h=h):
            weight = m.prob2[h, rows, :].astype(F32)
            slope = (m.ssum[rows, :] - m.delta[rows, h:h + 1]) * m.a2[rows, h:h + 1]
            m.ds[rows, :] = (weight * slope).astype(BF)

        loop(0, 4, ROWS, back_sum)
        m.dq[...] += dot(m.ds[...], of_head(m.kvs[0], h))
        feat = slice(64 * h, 64 * h + 64)
        m.dkst[feat, :] = dot(qt[feat, :], m.ds[...])
        m.dvst[feat, :] = dot(dot2[feat, :], m.prob2[h])
    m.dkvs[0] = m.dkst[...].T.astype(BF)
    m.dkvs[1] = m.dvst[...].T.astype(BF)
    for j in range(1, 16):
        @pl.when(j > s)
        def _(j=j):
            sum_copy(j).wait_send()
    grad_at = take(16)

    def grad_copy(j):
        return pltpu.make_async_remote_copy(
            src_ref=m.dkvs.at[:, pl.ds(SLOT * j, SLOT), :],
            dst_ref=m.sumg.at[s],
            send_sem=sum_ss.at[j], recv_sem=rs.at[grad_at + s],
            device_id=dev(j, t, batch), device_id_type=MESH,
        )

    def grad_arrived(j):
        pltpu.make_async_remote_copy(
            src_ref=m.dkvs.at[:, pl.ds(0, SLOT), :],
            dst_ref=m.sumg.at[j],
            send_sem=sum_ss.at[j], recv_sem=rs.at[grad_at + j],
            device_id=dev(j, t, batch), device_id_type=MESH,
        ).wait_recv()

    for j in range(15):
        @pl.when(j < s)
        def _(j=j):
            grad_copy(j).start()
    scatter_pass("ro", (0, 1), ro)

    for h in range(HEADS):
        m.sloc[h] = dot_nt(of_head(do_all, h), m.kv[1])
    for h in range(HEADS):
        def back_own(rows, h=h):
            weight = m.prob1[h, rows, :].astype(F32)
            slope = (m.sloc[h, rows, :] - m.delta[rows, h:h + 1]) * m.a1[rows, h:h + 1]
            m.ds[rows, 0:SEG] = (weight * slope).astype(BF)

        loop(0, 4, ROWS, back_own)
        score_grads = m.ds[:, 0:SEG]
        m.dq[...] += dot(score_grads, of_head(m.kv[0], h))
        feat = slice(64 * h, 64 * h + 64)
        m.dkt[feat, :] = dot(qt[feat, :], score_grads)
        m.dvt[feat, :] = dot(dot1[feat, :], m.prob1[h])
    for u in range(4):
        m.attt[HW * u:HW * u + HW, :] = m.atta[u].T
    ab.wait_recv()
    g_o = dot(m.attt[...], m.gba[...].reshape(SEG, HW))
    ends_g2 = reduce_pass(m.g2, "2", D, rg2)

    for j in range(1, 16):
        @pl.when(j > s)
        def _(j=j):
            grad_arrived(j)

    def returned(which):
        total = m.sumg[0, which].astype(F32)
        for j in range(1, SLOTS):
            total = total + m.sumg[j, which].astype(F32)
        high = total.astype(BF)
        rest = (total - high.astype(F32)).astype(BF)
        return dot_tn(high, pick) + dot_tn(rest, pick)

    dk = (m.dkt[...] + returned(0)).T.astype(BF)
    dv = (m.dvt[...] + returned(1)).T.astype(BF)
    dq = m.dq[...].astype(BF) * jnp.asarray(0.125, BF)
    m.dqkv[...] = jnp.concatenate([dq, dk, dv], axis=1)

    g_qkv = dot(m.nrmt[...], m.dqkv[...])
    m.g1[...] = jnp.concatenate([g_qkv, g_o], axis=1).astype(BF).reshape(4, 4, 48, D)
    rg1 = reduce_start(m.g1, "1", D // 2)
    m.rn_s[...] = dot_nt(m.dqkv[...], m.w1[...].reshape(D, D)[:, 0:3 * HW]).astype(BF)
    rn = [scatter_start("rn", (c,)) for c in range(2)]

    def gain_grads(j, carry):
        rows = pl.ds(pl.multiple_of(j * 64, 64), 64)
        grads = m.rn_s[rows, :].astype(F32)
        unit = (m.toka[rows, :].astype(F32) - m.stat[rows, 0:1]) * m.stat[rows, 1:2]
        return (
            carry[0] + jnp.sum((grads * unit).reshape(8, 8, D), axis=0),
            carry[1] + jnp.sum(grads.reshape(8, 8, D), axis=0),
        )

    zero8 = jnp.zeros((8, D), F32)
    g_gain1, g_shift1 = lax.fori_loop(0, 8, gain_grads, (zero8, zero8))
    scatter_pass("rn", (0,), rn[0])
    scatter_pass("rn", (1,), rn[1])
    g_qkvb = col_sums(m.dqkv[...])

    def in_place(row):
        none = jnp.zeros((1, HW), F32)
        return jnp.concatenate([jnp.where(t == u, row, none) for u in range(4)], axis=1)

    rows8 = (
        jnp.sum(g_gain1, axis=0, keepdims=True),
        jnp.sum(g_shift1, axis=0, keepdims=True),
        in_place(g_qkvb[:, 0:HW]),
        in_place(g_qkvb[:, 2 * HW:]),
        col_sums(m.gbr[...]),
        g_gain2,
        g_shift2,
        col_sums(dout[...]),
    )
    m.vgr[...] = jnp.zeros((16, D), F32)
    for k, row in enumerate(rows8):
        m.vgr[k:k + 1, :] = row
    g_ub = col_sums(m.gp[...])
    for u in range(4):
        m.vgr[8 + u:9 + u, :] = jnp.where(t == u, g_ub, zero_row)
    vgx = fly([(m.vgr, m.vgx.at[k - 1], along_x(k)) for k in (1, 2, 3)], m.vgx)
    fin_g2 = reduce_last("2", D, ends_g2)
    for c in range(2):
        out_o[HALF * c:HALF * c + HALF, :] = (
            scatter_end("ro", c, ro) + m.hid[block(c, t), :] + down_bias
        ).astype(BF)
    ends_g1 = reduce_pass(m.g1, "1", D // 2, rg1)
    vgx.wait_recv()
    m.vgs[...] = add4(m.vgr[...], m.vgx)
    vgz = fly([(m.vgs, m.vgz.at[k - 1], along_z(k)) for k in (1, 2, 3)], m.vgz)

    for c in range(2):
        at = slice(HALF * c, HALF * c + HALF)
        grads = scatter_end("rn", c, rn[c])
        _, into = norm_back(tok[at, :].astype(F32), grads, gain1)
        gtok_o[at, :] = into + m.gh[at, :]
    vgz.wait_recv()
    m.vgt[...] = add4(m.vgs[...], m.vgz)
    fin_v = fly([(m.vgt, m.vfin.at[mine], device) for _, device in everyone], m.vfin.at[0:7])
    m.vfin[mine] = m.vgt[...]
    fin_g1 = reduce_last("1", D // 2, ends_g1)

    def both(fin, u, cols):
        return fin[u, 0:12, cols].astype(F32) + fin[4 + u, 0:12, cols].astype(F32)

    fin_g2.wait_recv()
    for u in range(4):
        wide = slice(D * u, D * u + D)
        gu_o[:, wide] = both(m.fin2, u, slice(0, D))
        gd_o[:, wide] = both(m.fin2, u, slice(D, 2 * D))
    fin_v.wait_recv()
    total = m.vfin[0]
    for k in range(1, 8):
        total = total + m.vfin[k]
    back = iota((D, 128), 0) - iota((D, 128), 1)
    lane = iota((D, 128), 1)
    get_12 = ((back == 12 * place) & (lane < 12)).astype(F32)
    get_48 = ((back == 48 * (place % 16)) & (lane < 48)).astype(F32)
    small = dot(total, get_12, precision=HIGHEST)
    large = dot(total, get_48, precision=HIGHEST)
    row16 = iota((16, 128), 0)
    chosen = jnp.sum(jnp.where(row16 == 8 + z, large, 0.0), axis=0, keepdims=True)
    gvec_o[...] = jnp.where(row16 < 8, small, jnp.where(row16 == 8, chosen, 0.0))
    fin_g1.wait_recv()
    parts = [both(m.fin1, u, slice(0, D)) for u in range(4)]
    for k, ref in enumerate((gq_o, gk_o, gv_o, go_o)):
        ref[...] = jnp.concatenate([p[:, HW * k:HW * k + HW] for p in parts], axis=1)

    for flight in sent:
        flight.wait_send()
    for j in range(15):
        @pl.when(j < s)
        def _(j=j):
            grad_copy(j).wait_send()
    assert used[0] <= RECVS, used[0]


def hand_out(*refs):
    whole, vec, outs = refs[:8], refs[8], refs[9:]
    for src, dst in zip(whole, outs[:8]):
        dst[...] = src[...]
    for k, dst in enumerate(outs[8:16]):
        dst[...] = vec[k:k + 1, 0:12]
    outs[16][...] = vec[8:9, 0:48]


def body(
    tokens, seg_lengths, ln1_gain, ln1_bias, w_query, q_bias, w_key, w_value, v_bias,
    w_out, o_bias, ln2_gain, ln2_bias, w_up, up_bias, w_down, down_bias, d_out,
):
    vectors = [ln1_gain, ln1_bias, q_bias, v_bias, o_bias, ln2_gain, ln2_bias, down_bias, up_bias]
    shape = jax.ShapeDtypeStruct
    vmem = pl.BlockSpec(memory_space=pltpu.VMEM)
    shapes = [
        shape((ROWS, D), BF),
        shape((ROWS, D), F32),
        shape((12, D), F32),
        shape((12, D), F32),
        shape((12, D), F32),
        shape((12, D), F32),
        shape((12, 4 * D), F32),
        shape((12, 4 * D), F32),
    ]
    outs = pl.pallas_call(
        layer_kernel,
        out_shape=shapes + [shape((16, 128), F32)],
        in_specs=[pl.BlockSpec(memory_space=pltpu.SMEM)] + [vmem] * 17,
        out_specs=[vmem] * 9,
        scratch_shapes=[pltpu.VMEM(dims, kind) for dims, kind in SCRATCH.values()]
        + [pltpu.SemaphoreType.DMA((n,)) for n in (SENDS, RECVS, SLOTS)],
        compiler_params=pltpu.CompilerParams(
            collective_id=0, has_side_effects=True, vmem_limit_bytes=62 * 2**20
        ),
        name="layer",
    )(
        seg_lengths, tokens[0], d_out[0], w_query, w_key, w_value, w_out, w_up, w_down,
        *[v.reshape(1, -1) for v in vectors],
    )
    outs = pl.pallas_call(
        hand_out,
        out_shape=shapes + [shape((1, 12), F32)] * 8 + [shape((1, 48), F32)],
        in_specs=[vmem] * 9,
        out_specs=[vmem] * 17,
        compiler_params=pltpu.CompilerParams(vmem_limit_bytes=62 * 2**20),
        name="hand_out",
    )(*outs)
    out, g_tok, g_q, g_k, g_v, g_o, g_up, g_down = outs[:8]
    l1g, l1b, qb, vb, ob, l2g, l2b, db, ub = [v.reshape(-1) for v in outs[8:]]
    return (
        out[None], g_tok[None], l1g, l1b, g_q, qb, g_k, g_v, vb,
        g_o, ob, l2g, l2b, g_up, ub, g_down, db,
    )


def solution(mesh):
    rows, cols = P("batch", "seq", None), P("seq", None)
    one = P("seq")
    placed = (
        rows, P("batch", None), one, one, cols, one, cols, cols, one,
        cols, one, one, one, cols, one, cols, one, rows,
    )
    return jax.shard_map(
        body,
        mesh=mesh,
        in_specs=placed,
        out_specs=(
            rows, rows, one, one, cols, one, cols, cols, one,
            cols, one, one, one, cols, one, cols, one,
        ),
        check_vma=False,
    )
```

```python
import functools
import types

import jax
import jax.numpy as jnp
from jax import lax
from jax.experimental import pallas as pl
from jax.experimental.pallas import tpu as pltpu
from jax.sharding import PartitionSpec as P

BF = jnp.bfloat16
F32 = jnp.float32
MESH = pl.DeviceIdType.MESH
EPSILON = 1e-05
MASKED = -1e30
HIGHEST = lax.Precision.HIGHEST

ROWS = 128
SEG = 512
D = 768
HW = 192
HEADS = 3
HALF = 64
CHUNK = 256
SUMMARY = 50
SLOT = 64
SLOTS = 16
SUMS = SLOTS * SLOT


def dot(a, b, **kw):
    return jnp.dot(a, b, preferred_element_type=F32, **kw)


def dot_nt(a, b):
    return lax.dot_general(a, b, (((1,), (1,)), ((), ())), preferred_element_type=F32)


def dot_tn(a, b):
    return lax.dot_general(a, b, (((0,), (0,)), ((), ())), preferred_element_type=F32)


def iota(shape, dim):
    return lax.broadcasted_iota(jnp.int32, shape, dim)


def norm_stats(values):
    center = values - jnp.mean(values, axis=-1, keepdims=True)
    spread = jnp.mean(center * center, axis=-1, keepdims=True)
    return center, lax.rsqrt(spread + EPSILON)


SCRATCH = dict(
    pk1=((4, 16, D), BF),
    pk2=((4, 16, 2 * D), BF),
    p01=((4, 16, D), BF),
    p02=((4, 16, 2 * D), BF),
    w1=((4, 4, 48, D), BF),
    w2=((4, 4, 48, 2 * D), BF),
    wosl=((4, D // 2, 2 * HW), BF),
    wof=((D, D), BF),
    vin=((16, 128), F32),
    vb=((16, D), BF),
    vg=((3, 16, D), BF),
    vs1=((16, D), BF),
    vx=((3, 16, D), BF),
    vs2=((16, D), BF),
    vz=((3, 16, D), BF),
    vecs=((16, D), F32),
    toka=((SEG, D), BF),
    doa=((SEG, D), BF),
    nrm=((SEG, D), BF),
    nrmt=((D, SEG), BF),
    dot_=((D, SEG), BF),
    stat=((SEG, 128), F32),
    bias=((SEG, SEG), F32),
    q=((SEG, HW), BF),
    kv=((2, SEG, HW), BF),
    kvl=((SEG, 2 * HW), BF),
    kvs=((SUMS, 2 * HW), BF),
    ks=((SUMS, HW), BF),
    vs=((SUMS, HW), BF),
    ssrc=((SLOT, 2 * HW), BF),
    big=((SEG, HEADS * SEG), F32),
    ssum=((HEADS, SEG, SUMS), F32),
    prob1=((HEADS, SEG, SEG), BF),
    prob2=((HEADS, SEG, SUMS), BF),
    m1=((SEG, 128), F32),
    l1=((SEG, 128), F32),
    m2=((SEG, 128), F32),
    l2=((SEG, 128), F32),
    a1=((SEG, 128), F32),
    a2=((SEG, 128), F32),
    delta=((SEG, 128), F32),
    a1x=((SEG, HW), F32),
    a2x=((SEG, HW), F32),
    o1=((SEG, HW), F32),
    att=((SEG, HW), F32),
    attp=((4, 2, ROWS, 2 * HW), BF),
    atta=((4, SEG, HW), BF),
    attt=((D, SEG), BF),
    hid=((SEG, D), F32),
    nm=((SEG, D), BF),
    nmt=((D, SEG), BF),
    act=((SEG, D), BF),
    gp=((SEG, D), BF),
    rm_s=((SEG, D), BF),
    rm_1=((2, 2, HALF, D), BF),
    rm_x=((2, HALF, D), BF),
    rm_2=((2, HALF, D), BF),
    ro_s=((SEG, D), BF),
    ro_1=((2, 2, HALF, D), BF),
    ro_x=((2, HALF, D), BF),
    ro_2=((2, HALF, D), BF),
    rn_s=((SEG, D), BF),
    rn_1=((2, 2, HALF, D), BF),
    rn_x=((2, HALF, D), BF),
    rn_2=((2, HALF, D), BF),
    gh=((ROWS, D), F32),
    gbr=((ROWS, D), BF),
    sa=((2, 4, HALF, HW), BF),
    sb=((2, 4, HALF, HW), BF),
    do=((2, 4, HALF, HW), BF),
    gba=((2, 4, HALF, HW), BF),
    ds=((HEADS, SEG, SUMS), BF),
    dq=((SEG, HW), F32),
    dkvt=((2 * HW, SEG), F32),
    dkvst=((2 * HW, SUMS), F32),
    dkvs=((SUMS, 2 * HW), BF),
    sumg=((SLOTS, SLOT, 2 * HW), BF),
    dqkv=((SEG, 3 * HW), BF),
    g1=((4, 4, 48, D), BF),
    g2=((4, 4, 48, 2 * D), BF),
    rza1=((3, 4, 48, D // 2), BF),
    rxa1=((3, 48, D // 2), BF),
    rxb1=((3, 4, 48, D // 2), BF),
    rzb1=((3, 48, D // 2), BF),
    ha1=((4, 48, D // 2), BF),
    hb1=((4, 48, D // 2), BF),
    rza2=((3, 4, 48, D), BF),
    rxa2=((3, 48, D), BF),
    rxb2=((3, 4, 48, D), BF),
    rzb2=((3, 48, D), BF),
    ha2=((4, 48, D), BF),
    hb2=((4, 48, D), BF),
    fx1=((4, 16, D), BF),
    fx2=((4, 16, 2 * D), BF),
    fin1=((8, 16, D), BF),
    fin2=((8, 16, 2 * D), BF),
    vgr=((16, D), F32),
    vgx=((3, 16, D), F32),
    vgs=((16, D), F32),
    vgz=((3, 16, D), F32),
    sel=((D, 384), BF),
    vgt=((16, 256), F32),
    vfin=((8, 16, 256), F32),
)
SENDS = 24
RECVS = 100


class Flight:
    def __init__(self, waiter):
        self.waiter = waiter
        self.arrived = False
        self.left = False

    def wait_recv(self):
        if not self.arrived:
            self.waiter.wait_recv()
        self.arrived = True

    def wait_send(self):
        if not self.left:
            self.waiter.wait_send()
        self.left = True


def layer_kernel(
    seg_ref, tok, dout, wq, wk, wv, wo, wu, wd, *refs,
):
    vectors, refs = refs[:9], refs[9:]
    out_o, gtok_o, gq_o, gk_o, gv_o, go_o, gu_o, gd_o, gvec_o = refs[:9]
    scratch = refs[9:]
    m = types.SimpleNamespace(**dict(zip(SCRATCH, scratch[:-3])))
    ss, rs, sum_ss = scratch[-3:]
    batch = lax.axis_index("batch")
    place = lax.axis_index("seq")
    s = place // 4
    t = place % 4
    z = s // 4
    x = s % 4
    sib = t + 1 - 2 * (t % 2)
    over = (t + 2) % 4
    diag = 3 - t
    group = (over, diag, sib)

    def dev(seg, tt, bb):
        return (4 * seg + tt, bb)

    def here(tt):
        return dev(s, tt, batch)

    def along_x(k):
        return dev(4 * z + (x + k) % 4, t, batch)

    def along_z(k):
        return dev(4 * ((z + k) % 4) + x, t, batch)

    used = [0]
    sent = []

    def take(n=1):
        first = used[0]
        used[0] += n
        return first

    def fly(copies, total=None):
        k = len(sent)
        if k >= SENDS:
            sent[k - SENDS].wait_send()
        send_sem, recv_sem = ss.at[k % SENDS], rs.at[take()]
        for src, dst, device in copies:
            copy = pltpu.make_async_remote_copy(
                src_ref=src, dst_ref=dst, send_sem=send_sem, recv_sem=recv_sem,
                device_id=device, device_id_type=MESH,
            )
            copy.start()
        if total is not None:
            copy = pltpu.make_async_remote_copy(
                src_ref=total, dst_ref=total, send_sem=send_sem, recv_sem=recv_sem,
                device_id=device, device_id_type=MESH,
            )
        flight = Flight(copy)
        sent.append(flight)
        return flight

    def block(c, k):
        return pl.ds(pl.multiple_of(CHUNK * c + HALF * k, HALF), HALF)

    def loop(first, count, size, fn, unroll=4):
        def step(j, carry):
            fn(pl.ds(pl.multiple_of(first + j * size, size), size))
            return carry

        lax.fori_loop(0, count, step, 0, unroll=unroll)

    m.kvs[...] = jnp.zeros((SUMS, 2 * HW), BF)
    m.sumg[...] = jnp.zeros((SLOTS, SLOT, 2 * HW), BF)
    barrier = pltpu.get_barrier_semaphore()
    partners = [here(u) for u in group]
    partners += [dev((s + k) % 16, t, batch) for k in range(1, 16)]
    partners += [dev(s, u, 1 - batch) for u in (t, sib, over, diag)]
    for partner in partners:
        pl.semaphore_signal(barrier, inc=1, device_id=partner, device_id_type=MESH)
    m.pk1[...] = jnp.zeros((4, 16, D), BF)
    for u in range(4):
        cols = slice(HW * u, HW * u + HW)
        m.pk1[u, 0:12, :] = jnp.concatenate(
            [wq[:, cols], wk[:, cols], wv[:, cols], wo[:, cols]], axis=1
        )
    m.vin[...] = jnp.zeros((16, 128), F32)
    for k, ref in enumerate(vectors[:8]):
        m.vin[k:k + 1, 0:12] = ref[...].astype(F32)
    m.vin[8:9, 0:48] = vectors[8][...].astype(F32)
    shift = iota((128, D), 1) - iota((128, D), 0)
    narrow = dot(m.vin[...].astype(BF), (shift == 12 * place).astype(BF))
    wider = dot(m.vin[...].astype(BF), (shift == 48 * (place % 16)).astype(BF))
    vec_row = iota((16, D), 0)
    m.vb[...] = jnp.where(
        vec_row < 8, narrow, jnp.where(vec_row == 8 + z, wider[8:9, :], 0.0)
    ).astype(BF)
    pl.semaphore_wait(barrier, len(partners))

    first1 = fly([(m.pk1.at[u], m.p01.at[t], here(u)) for u in group], m.p01.at[0:3])
    firstv = fly(
        [(m.vb, m.vg.at[k], here(u)) for k, u in enumerate((sib, over, diag))], m.vg
    )
    m.p01[t] = m.pk1[t]
    m.pk2[...] = jnp.zeros((4, 16, 2 * D), BF)
    for u in range(4):
        wide = slice(D * u, D * u + D)
        m.pk2[u, 0:12, 0:D] = wu[:, wide]
        m.pk2[u, 0:12, D:] = wd[:, wide]
    m.p02[t] = m.pk2[t]
    for c in range(2):
        m.toka[block(c, t), :] = tok[HALF * c:HALF * c + HALF, :]
        m.doa[block(c, t), :] = dout[HALF * c:HALF * c + HALF, :]

    def gather_start(ref):
        moves = [
            fly([(ref.at[block(c, t)], ref.at[block(c, t)], here(u)) for c in (0, 1)],
                ref.at[0:ROWS])
            for u in (over, sib)
        ]
        return moves

    def gather_pass(moves, ref):
        moves[0].wait_recv()
        moves.append(
            fly([(ref.at[block(c, over)], ref.at[block(c, over)], here(sib)) for c in (0, 1)],
                ref.at[0:ROWS])
        )

    def finish(moves):
        for move in moves:
            move.wait_recv()

    row48 = iota((48, 64), 0)
    owner48 = (
        (row48 >= 12).astype(jnp.int32)
        + (row48 >= 24).astype(jnp.int32)
        + (row48 >= 36).astype(jnp.int32)
    )
    squeeze = (iota((48, 64), 1) == row48 + 4 * owner48).astype(BF)

    def spread_start(w, half):
        a, b = pl.ds(0, half), pl.ds(half, half)
        mine_a, mine_b = w.at[z, x, :, a], w.at[z, x, :, b]
        return (
            fly([(mine_a, mine_a, along_x(k)) for k in (1, 3, 2)], w.at[0, 0:3, :, a]),
            fly([(mine_b, mine_b, along_z(k)) for k in (1, 3, 2)], w.at[0, 0:3, :, b]),
        )

    def spread_pass(w, half, moves):
        a, b = pl.ds(0, half), pl.ds(half, half)
        plane_a, plane_b = w.at[z, :, :, a], w.at[:, x, :, b]
        moves[0].wait_recv()
        a2 = fly([(plane_a, plane_a, along_z(k)) for k in (1, 3, 2)], w.at[0:3, :, :, a])
        moves[1].wait_recv()
        b2 = fly([(plane_b, plane_b, along_x(k)) for k in (1, 3, 2)], w.at[0:3, :, :, b])
        return a2, b2

    first1.wait_recv()
    m.w1[z, x] = dot(squeeze, m.p01[...].reshape(64, D)).astype(BF)
    phase1 = spread_start(m.w1, D // 2)
    first2 = fly([(m.pk2.at[u], m.p02.at[t], here(u)) for u in group], m.p02.at[0:3])
    ag_tok = gather_start(m.toka)

    seg_len = seg_ref[0, s]

    def token_of(rows):
        return rows + 64 * ((rows % CHUNK) // HALF) - 192 * (rows // CHUNK)

    k_pos = token_of(iota((1, SEG), 1))

    def mask(rows):
        mine = token_of(rows.start + iota((ROWS, 1), 0))
        ok = ((k_pos <= mine) & (k_pos < seg_len)) | (k_pos == mine)
        m.bias[rows, :] = jnp.where(ok, 0.0, MASKED)

    loop(0, 4, ROWS, mask)
    s_col = iota((8, SUMS), 1)
    sum_bias = jnp.where((s_col < SLOT * s) & (s_col % SLOT < SUMMARY), 0.0, MASKED)[0:1, :]
    pick_row = iota((SLOT, SEG), 0)
    pick = ((k_pos == seg_len - SUMMARY + pick_row) & (pick_row < SUMMARY)).astype(BF)
    lane_head = iota((1, HW), 1) // 64

    def of_head(value, h):
        return jnp.where(lane_head == h, value, jnp.zeros_like(value))

    def by_head(cols):
        return jnp.where(
            lane_head == 0, cols[:, 0:1], jnp.where(lane_head == 1, cols[:, 1:2], cols[:, 2:3])
        )

    def add4(own, got):
        return own.astype(F32) + got[0].astype(F32) + got[1].astype(F32) + got[2].astype(F32)

    def moved_by(rows, one_hot):
        high = rows.astype(BF)
        rest = rows - high.astype(F32)
        mid = rest.astype(BF)
        low = (rest - mid.astype(F32)).astype(BF)
        pieces = dot(jnp.concatenate([high, mid, low], axis=0), one_hot)
        return pieces[0:16, :] + pieces[16:32, :] + pieces[32:48, :]

    feature, lane = iota((D, 128), 0), iota((D, 128), 1)
    m.sel[:, 0:128] = ((feature - lane == 48 * s) & (lane < 48)).astype(BF)
    feature, lane = iota((D, 256), 0), iota((D, 256), 1)
    m.sel[:, 128:384] = ((feature - lane == 192 * x) & (lane < 192)).astype(BF)

    firstv.wait_recv()
    m.vs1[...] = add4(m.vb[...], m.vg).astype(BF)
    vx = fly([(m.vs1, m.vx.at[k - 1], along_x(k)) for k in (1, 2, 3)], m.vx)
    ends1 = spread_pass(m.w1, D // 2, phase1)
    vx.wait_recv()
    m.vs2[...] = add4(m.vs1[...], m.vx).astype(BF)
    vz = fly([(m.vs2, m.vz.at[k - 1], along_z(k)) for k in (1, 2, 3)], m.vz)
    first2.wait_recv()
    m.w2[z, x] = dot(squeeze, m.p02[...].reshape(64, 2 * D)).astype(BF)
    phase2 = spread_start(m.w2, D)
    gather_pass(ag_tok, m.toka)
    ag_do = gather_start(m.doa)
    vz.wait_recv()
    m.vecs[...] = add4(m.vs2[...], m.vz)
    gain1, shift1 = m.vecs[0:1, :], m.vecs[1:2, :]
    gain2, shift2 = m.vecs[5:6, :], m.vecs[6:7, :]
    o_bias, down_bias = m.vecs[4:5, :], m.vecs[7:8, :]

    def my_cols(row):
        whole = m.vecs[row:row + 1, :]
        value = whole[:, 0:HW]
        for u in range(1, 4):
            value = jnp.where(t == u, whole[:, HW * u:HW * u + HW], value)
        return value

    q_bias, v_bias = my_cols(2), my_cols(3)
    up_bias = m.vecs[8:9, :]
    for u in range(1, 4):
        up_bias = jnp.where(t == u, m.vecs[8 + u:9 + u, :], up_bias)

    finish(ag_tok)

    def norm1(rows):
        values = m.toka[rows, :].astype(F32)
        mean = jnp.mean(values, axis=-1, keepdims=True)
        center = values - mean
        scale = lax.rsqrt(jnp.mean(center * center, axis=-1, keepdims=True) + EPSILON)
        m.nrm[rows, :] = (center * scale * gain1 + shift1).astype(BF)
        m.stat[rows, 0:1] = mean
        m.stat[rows, 1:2] = scale

    loop(0, 4, ROWS, norm1)
    m.nrmt[...] = m.nrm[...].T

    finish(ends1)
    w1 = m.w1[...].reshape(D, D)
    qkv = dot(m.nrm[...], w1)
    m.q[...] = ((qkv[:, 0:HW] + q_bias) * 0.125).astype(BF)
    kv_bias = jnp.concatenate([jnp.zeros((1, HW), F32), v_bias], axis=1)
    m.kvl[...] = (qkv[:, HW:3 * HW] + kv_bias).astype(BF)

    m.ssrc[...] = dot(pick, m.kvl[...]).astype(BF)
    sum_at = take(16)

    def sum_copy(k):
        return pltpu.make_async_remote_copy(
            src_ref=m.ssrc,
            dst_ref=m.kvs.at[pl.ds(pl.multiple_of(SLOT * s, SLOT), SLOT)],
            send_sem=sum_ss.at[k], recv_sem=rs.at[sum_at + k],
            device_id=dev((s + k) % 16, t, batch), device_id_type=MESH,
        )

    for k in range(1, 16):
        @pl.when(s + k < 16)
        def _(k=k):
            sum_copy(k).start()
    w_o = m.w1[...].reshape(D, D)[:, 3 * HW:]
    m.wosl[t] = jnp.concatenate([w_o[0:D // 2, :], w_o[D // 2:, :]], axis=1)
    m.kv[0] = m.kvl[:, 0:HW]
    m.kv[1] = m.kvl[:, HW:]
    ag_wo = [fly([(m.wosl.at[t], m.wosl.at[t], here(u))]) for u in (over, sib)]

    for h in range(HEADS):
        m.big[:, SEG * h:SEG * h + SEG] = dot_nt(of_head(m.q[...], h), m.kv[0]) + m.bias[...]
    for h in range(HEADS):
        def soften1(rows, h=h):
            score = m.big[rows, SEG * h:SEG * h + SEG]
            peak = jnp.max(score, axis=-1, keepdims=True)
            power = jnp.exp(score - peak)
            m.prob1[h, rows, :] = power.astype(BF)
            m.m1[rows, h:h + 1] = peak
            m.l1[rows, h:h + 1] = jnp.sum(power, axis=-1, keepdims=True)

        loop(0, 4, ROWS, soften1)
        part = dot(m.prob1[h], of_head(m.kv[1], h))
        m.o1[...] = part if h == 0 else m.o1[...] + part
    gather_pass(ag_do, m.doa)

    for k in range(1, 16):
        @pl.when(s >= k)
        def _(k=k):
            sum_copy(k).wait_recv()
    ends2 = spread_pass(m.w2, D, phase2)
    m.ks[...] = m.kvs[:, 0:HW]
    m.vs[...] = m.kvs[:, HW:]

    ag_att = []

    def attend(c):
        rows_c = slice(CHUNK * c, CHUNK * c + CHUNK)
        part = None
        for h in range(HEADS):
            m.ssum[h, rows_c, :] = dot_nt(of_head(m.q[rows_c, :], h), m.ks[...]) + sum_bias

            def soften2(rows, h=h):
                score = m.ssum[h, rows, :]
                peak = jnp.max(score, axis=-1, keepdims=True)
                power = jnp.exp(score - peak)
                m.prob2[h, rows, :] = power.astype(BF)
                m.m2[rows, h:h + 1] = peak
                m.l2[rows, h:h + 1] = jnp.sum(power, axis=-1, keepdims=True)

            loop(CHUNK * c, 2, ROWS, soften2)
            more = dot(m.prob2[h, rows_c, :], of_head(m.vs[...], h))
            part = more if h == 0 else part + more
        m1, m2 = m.m1[rows_c, 0:HEADS], m.m2[rows_c, 0:HEADS]
        peak = jnp.maximum(m1, m2)
        e1, e2 = jnp.exp(m1 - peak), jnp.exp(m2 - peak)
        share = 1.0 / (m.l1[rows_c, 0:HEADS] * e1 + m.l2[rows_c, 0:HEADS] * e2)
        a1, a2 = e1 * share, e2 * share
        m.a1[rows_c, 0:HEADS] = a1
        m.a2[rows_c, 0:HEADS] = a2
        a1x, a2x = by_head(a1), by_head(a2)
        m.a1x[rows_c, :] = a1x
        m.a2x[rows_c, :] = a2x
        attended = m.o1[rows_c, :] * a1x + part * a2x
        m.att[rows_c, :] = attended
        low = attended.astype(BF)
        m.attp[t, c] = jnp.concatenate([low[0:ROWS, :], low[ROWS:, :]], axis=1)
        mine_c = m.attp.at[t, c]
        ag_att.append([fly([(mine_c, mine_c, here(u))]) for u in (over, sib)])

    attend(0)
    ag_wo[0].wait_recv()
    ag_wo.append(fly([(m.wosl.at[over], m.wosl.at[over], here(sib))]))
    attend(1)
    finish(ag_wo)
    m.wof[0:D // 2, :] = jnp.concatenate([m.wosl[u, :, 0:HW] for u in range(4)], axis=1)
    m.wof[D // 2:, :] = jnp.concatenate([m.wosl[u, :, HW:] for u in range(4)], axis=1)

    def att_pass(c):
        ag_att[c][0].wait_recv()
        theirs = m.attp.at[over, c]
        ag_att[c].append(fly([(theirs, theirs, here(sib))]))

    def scatter_start(name, cs):
        src, r1 = getattr(m, name + "_s"), getattr(m, name + "_1")
        return [
            fly([(src.at[block(c, k)], r1.at[c, i], here(sib)) for c in cs],
                r1.at[0:len(cs), i])
            for i, k in ((1, diag), (0, sib))
        ]

    def scatter_pass(name, cs, moves):
        src, r1 = getattr(m, name + "_s"), getattr(m, name + "_1")
        cross, r2 = getattr(m, name + "_x"), getattr(m, name + "_2")
        moves[0].wait_recv()
        for c in cs:
            cross[c] = (src[block(c, over), :].astype(F32) + r1[c, 1].astype(F32)).astype(BF)
        moves.append(
            fly([(cross.at[c], r2.at[c], here(over)) for c in cs], r2.at[0:len(cs)])
        )

    def scatter_end(name, c, moves):
        src, r1 = getattr(m, name + "_s"), getattr(m, name + "_1")
        r2 = getattr(m, name + "_2")
        moves[1].wait_recv()
        moves[2].wait_recv()
        return src[block(c, t), :].astype(F32) + r1[c, 0].astype(F32) + r2[c].astype(F32)

    def gelu(rows):
        a = m.big[rows, 0:D]
        square = a * a
        bend = jnp.tanh(0.7978845608028654 * (a + 0.044715 * (square * a)))
        half = 0.5 * (1.0 + bend)
        m.act[rows, :] = (a * half).astype(BF)
        slope = half + (0.5 * a) * (1.0 - bend * bend) * (
            0.7978845608028654 * (1.0 + 0.134145 * square)
        )
        m.gp[rows, :] = (m.big[rows, D:] * slope).astype(BF)

    def norm2(rows):
        center, scale = norm_stats(m.hid[rows, :])
        m.nm[rows, :] = (center * scale * gain2 + shift2).astype(BF)

    def project(c):
        rows_c = slice(CHUNK * c, CHUNK * c + CHUNK)
        finish(ag_att[c])
        for u in range(4):
            m.atta[u, CHUNK * c:CHUNK * c + ROWS, :] = m.attp[u, c, :, 0:HW]
            m.atta[u, CHUNK * c + ROWS:CHUNK * c + CHUNK, :] = m.attp[u, c, :, HW:]
        branch = dot(m.atta[0, rows_c, :], m.wof[0:HW, :])
        for u in range(1, 4):
            branch = branch + dot(m.atta[u, rows_c, :], m.wof[HW * u:HW * u + HW, :])
        m.hid[rows_c, :] = m.toka[rows_c, :].astype(F32) + branch + o_bias
        loop(CHUNK * c, 2, ROWS, norm2)

    def feed(c):
        rows_c = slice(CHUNK * c, CHUNK * c + CHUNK)
        m.big[rows_c, 0:D] = dot(m.nm[rows_c, :], m.w2[:, :, :, 0:D].reshape(D, D)) + up_bias
        m.big[rows_c, D:] = dot(m.doa[rows_c, :], m.w2[:, :, :, D:].reshape(D, D))
        loop(CHUNK * c, 4, 64, gelu)
        m.rm_s[rows_c, :] = dot_nt(m.gp[rows_c, :], m.w2[:, :, :, 0:D].reshape(D, D)).astype(BF)
        return scatter_start("rm", (c,))

    att_pass(0)
    project(0)
    att_pass(1)
    finish(ag_do)
    finish(ends2)
    rm0 = feed(0)
    project(1)
    scatter_pass("rm", (0,), rm0)
    rm1 = feed(1)

    m.dot_[...] = m.doa[...].T
    m.nmt[...] = m.nm[...].T
    scatter_pass("rm", (1,), rm1)
    m.g2[:, :, :, 0:D] = dot(m.nmt[...], m.gp[...]).astype(BF).reshape(4, 4, 48, D)
    m.g2[:, :, :, D:] = dot(m.dot_[...], m.act[...]).astype(BF).reshape(4, 4, 48, D)

    def reduce_start(g, tag, half):
        rza, rxb = getattr(m, "rza" + tag), getattr(m, "rxb" + tag)
        a, b = pl.ds(0, half), pl.ds(half, half)
        return (
            fly([(g.at[(z + k) % 4, :, :, a], rza.at[k - 1], along_z(k)) for k in (1, 3, 2)], rza),
            fly([(g.at[:, (x + k) % 4, :, b], rxb.at[k - 1], along_x(k)) for k in (1, 3, 2)], rxb),
        )

    def reduce_pass(g, tag, half, moves):
        rza, rxb = getattr(m, "rza" + tag), getattr(m, "rxb" + tag)
        rxa, rzb = getattr(m, "rxa" + tag), getattr(m, "rzb" + tag)
        ha, hb = getattr(m, "ha" + tag), getattr(m, "hb" + tag)
        moves[0].wait_recv()
        for k in range(4):
            ha[k] = add4(g[z, k, :, 0:half], [rza[j, k] for j in range(3)]).astype(BF)
        a2 = fly([(ha.at[(x + k) % 4], rxa.at[k - 1], along_x(k)) for k in (1, 3, 2)], rxa)
        moves[1].wait_recv()
        for k in range(4):
            hb[k] = add4(g[k, x, :, half:], [rxb[j, k] for j in range(3)]).astype(BF)
        b2 = fly([(hb.at[(z + k) % 4], rzb.at[k - 1], along_z(k)) for k in (1, 3, 2)], rzb)
        return a2, b2

    row64 = iota((64, 48), 0)
    expand = (
        (iota((64, 48), 1) == row64 - 4 * (row64 // 16)) & (row64 % 16 < 12)
    ).astype(BF)
    mine = 4 * batch + t
    everyone = [(u, dev(s, u, 1 - batch)) for u in (over, diag, sib, t)]
    everyone += [(u, here(u)) for u in group]

    def reduce_last(tag, half, moves):
        rxa, rzb = getattr(m, "rxa" + tag), getattr(m, "rzb" + tag)
        ha, hb = getattr(m, "ha" + tag), getattr(m, "hb" + tag)
        fx, fin = getattr(m, "fx" + tag), getattr(m, "fin" + tag)
        finish(moves)
        a = add4(ha[x], [rxa[j] for j in range(3)]).astype(BF)
        b = add4(hb[z], [rzb[j] for j in range(3)]).astype(BF)
        fx[:, :, 0:half] = dot(expand, a).astype(BF).reshape(4, 16, half)
        fx[:, :, half:] = dot(expand, b).astype(BF).reshape(4, 16, half)
        moves = fly([(fx.at[u], fin.at[mine], device) for u, device in everyone], fin.at[0:7])
        fin[mine] = fx[t]
        return moves

    rg2 = reduce_start(m.g2, "2", D)

    zero_row = jnp.zeros((1, D), F32)
    ones = jnp.ones((8, SEG), BF)

    def col_sums(value):
        return dot(ones[:, 0:value.shape[0]], value)[0:1, :]

    def norm_back(values, grads, gain):
        center, scale = norm_stats(values)
        unit = center * scale
        inner = grads * gain
        return unit, scale * (
            inner
            - jnp.mean(inner, axis=-1, keepdims=True)
            - unit * jnp.mean(inner * unit, axis=-1, keepdims=True)
        )

    g_gain2, g_shift2 = zero_row, zero_row
    aa = []
    for c in range(2):
        at = slice(HALF * c, HALF * c + HALF)
        grads = scatter_end("rm", c, rm0 if c == 0 else rm1)
        unit, into = norm_back(m.hid[block(c, t), :], grads, gain2)
        into = into + dout[at, :].astype(F32)
        m.gh[at, :] = into
        low = into.astype(BF)
        m.gbr[at, :] = low
        for u in range(4):
            m.sa[c, u] = dot_nt(low, m.wof[HW * u:HW * u + HW, :]).astype(BF)
        aa.append(
            fly([(m.sa.at[c, u], m.do.at[c, t], here(u)) for u in group], m.do.at[c, 0:3])
        )
        m.do[c, t] = m.sa[c, t]
        g_gain2 += jnp.sum(grads * unit, axis=0, keepdims=True)
        g_shift2 += jnp.sum(grads, axis=0, keepdims=True)
    m.ro_s[...] = dot_nt(m.act[...], m.w2[:, :, :, D:].reshape(D, D)).astype(BF)
    for u in range(4):
        cols = m.gbr[:, HW * u:HW * u + HW]
        m.sb[0, u] = cols[0:HALF, :]
        m.sb[1, u] = cols[HALF:, :]
    qt = m.q[...].T
    m.dq[...] = jnp.zeros((SEG, HW), F32)

    finish(aa)
    do_all = m.do[...].reshape(SEG, HW)
    do_wide = do_all.astype(F32)
    weighed = do_wide * m.att[...]
    for h in range(HEADS):
        m.delta[:, h:h + 1] = jnp.sum(of_head(weighed, h), axis=-1, keepdims=True)
    dot1 = (do_wide * m.a1x[...]).astype(BF).T
    dot2 = (do_wide * m.a2x[...]).astype(BF).T
    ab = fly(
        [(m.sb.at[c, u], m.gba.at[c, t], here(u)) for u in group for c in (0, 1)],
        m.gba.at[:, 0:3],
    )
    m.gba[0, t] = m.sb[0, t]
    m.gba[1, t] = m.sb[1, t]
    ro = scatter_start("ro", (0, 1))
    for h in range(HEADS):
        m.ssum[h] = dot_nt(of_head(do_all, h), m.vs[...])

        def back_sum(rows, h=h):
            weight = m.prob2[h, rows, :].astype(F32)
            slope = (m.ssum[h, rows, :] - m.delta[rows, h:h + 1]) * m.a2[rows, h:h + 1]
            m.ds[h, rows, :] = (weight * slope).astype(BF)

        loop(0, 4, ROWS, back_sum)
        feat, feat_v = slice(64 * h, 64 * h + 64), slice(HW + 64 * h, HW + 64 * h + 64)
        m.dkvst[feat, :] = dot(qt[feat, :], m.ds[h])
        m.dkvst[feat_v, :] = dot(dot2[feat, :], m.prob2[h])
    m.dkvs[...] = m.dkvst[...].T.astype(BF)
    for k in range(1, 16):
        @pl.when(s + k < 16)
        def _(k=k):
            sum_copy(k).wait_send()
    grad_at = take(16)

    def grad_copy(k):
        slot = (s + 16 - k) % 16
        return pltpu.make_async_remote_copy(
            src_ref=m.dkvs.at[pl.ds(pl.multiple_of(SLOT * slot, SLOT), SLOT)],
            dst_ref=m.sumg.at[k],
            send_sem=sum_ss.at[k], recv_sem=rs.at[grad_at + k],
            device_id=dev(slot, t, batch), device_id_type=MESH,
        )

    for k in range(1, 16):
        @pl.when(s >= k)
        def _(k=k):
            grad_copy(k).start()
    scatter_pass("ro", (0, 1), ro)

    for h in range(HEADS):
        m.dq[...] += dot(m.ds[h], of_head(m.ks[...], h))
    for h in range(HEADS):
        m.big[:, SEG * h:SEG * h + SEG] = dot_nt(of_head(do_all, h), m.kv[1])
    for h in range(HEADS):
        def back_own(rows, h=h):
            weight = m.prob1[h, rows, :].astype(F32)
            slope = (m.big[rows, SEG * h:SEG * h + SEG] - m.delta[rows, h:h + 1]) * m.a1[rows, h:h + 1]
            m.ds[h, rows, 0:SEG] = (weight * slope).astype(BF)

        loop(0, 4, ROWS, back_own)
        score_grads = m.ds[h, :, 0:SEG]
        m.dq[...] += dot(score_grads, of_head(m.kv[0], h))
        feat, feat_v = slice(64 * h, 64 * h + 64), slice(HW + 64 * h, HW + 64 * h + 64)
        m.dkvt[feat, :] = dot(qt[feat, :], score_grads)
        m.dkvt[feat_v, :] = dot(dot1[feat, :], m.prob1[h])
    for u in range(4):
        m.attt[HW * u:HW * u + HW, :] = m.atta[u].T
    ab.wait_recv()
    g_o = dot(m.attt[...], m.gba[...].reshape(SEG, HW))
    ends_g2 = reduce_pass(m.g2, "2", D, rg2)

    for k in range(1, 16):
        @pl.when(s + k < 16)
        def _(k=k):
            grad_copy(k).wait_recv()

    total = m.sumg[0].astype(F32)
    for k in range(1, SLOTS):
        total = total + m.sumg[k].astype(F32)
    high = total.astype(BF)
    rest = (total - high.astype(F32)).astype(BF)
    dkv = (m.dkvt[...] + dot_tn(high, pick) + dot_tn(rest, pick)).T.astype(BF)
    dq = m.dq[...].astype(BF) * jnp.asarray(0.125, BF)
    m.dqkv[...] = jnp.concatenate([dq, dkv], axis=1)

    g_qkv = dot(m.nrmt[...], m.dqkv[...])
    m.g1[...] = jnp.concatenate([g_qkv, g_o], axis=1).astype(BF).reshape(4, 4, 48, D)
    rg1 = reduce_start(m.g1, "1", D // 2)
    m.rn_s[...] = dot_nt(m.dqkv[...], m.w1[...].reshape(D, D)[:, 0:3 * HW]).astype(BF)
    rn = [scatter_start("rn", (c,)) for c in range(2)]

    def gain_grads(j, carry):
        rows = pl.ds(pl.multiple_of(j * 64, 64), 64)
        grads = m.rn_s[rows, :].astype(F32)
        unit = (m.toka[rows, :].astype(F32) - m.stat[rows, 0:1]) * m.stat[rows, 1:2]
        return (
            carry[0] + jnp.sum((grads * unit).reshape(8, 8, D), axis=0),
            carry[1] + jnp.sum(grads.reshape(8, 8, D), axis=0),
        )

    zero8 = jnp.zeros((8, D), F32)
    g_gain1, g_shift1 = lax.fori_loop(0, 8, gain_grads, (zero8, zero8))
    scatter_pass("rn", (0,), rn[0])
    scatter_pass("rn", (1,), rn[1])
    g_qkvb = col_sums(m.dqkv[...])

    def in_place(row):
        none = jnp.zeros((1, HW), F32)
        return jnp.concatenate([jnp.where(t == u, row, none) for u in range(4)], axis=1)

    rows8 = (
        jnp.sum(g_gain1, axis=0, keepdims=True),
        jnp.sum(g_shift1, axis=0, keepdims=True),
        in_place(g_qkvb[:, 0:HW]),
        in_place(g_qkvb[:, 2 * HW:]),
        col_sums(m.gbr[...]),
        g_gain2,
        g_shift2,
        col_sums(dout[...]),
    )
    m.vgr[...] = jnp.zeros((16, D), F32)
    for k, row in enumerate(rows8):
        m.vgr[k:k + 1, :] = row
    g_ub = col_sums(m.gp[...])
    for u in range(4):
        m.vgr[8 + u:9 + u, :] = jnp.where(t == u, g_ub, zero_row)
    vgx = fly([(m.vgr, m.vgx.at[k - 1], along_x(k)) for k in (1, 2, 3)], m.vgx)
    fin_g2 = reduce_last("2", D, ends_g2)
    for c in range(2):
        out_o[HALF * c:HALF * c + HALF, :] = (
            scatter_end("ro", c, ro) + m.hid[block(c, t), :] + down_bias
        ).astype(BF)
    ends_g1 = reduce_pass(m.g1, "1", D // 2, rg1)
    vgx.wait_recv()
    m.vgs[...] = add4(m.vgr[...], m.vgx)
    vgz = fly([(m.vgs, m.vgz.at[k - 1], along_z(k)) for k in (1, 2, 3)], m.vgz)

    for c in range(2):
        at = slice(HALF * c, HALF * c + HALF)
        grads = scatter_end("rn", c, rn[c])
        _, into = norm_back(tok[at, :].astype(F32), grads, gain1)
        gtok_o[at, :] = into + m.gh[at, :]
    fin_g1 = reduce_last("1", D // 2, ends_g1)
    vgz.wait_recv()
    totals = add4(m.vgs[...], m.vgz)
    moved = moved_by(totals, m.sel[...])
    up_row = jnp.sum(jnp.where(iota((16, 256), 0) == 8 + z, moved[:, 128:384], 0.0), axis=0, keepdims=True)
    m.vgt[...] = jnp.zeros((16, 256), F32)
    m.vgt[0:8, 0:128] = moved[0:8, 0:128]
    m.vgt[8:9, :] = up_row
    fin_v = fly([(m.vgt, m.vfin.at[mine], device) for _, device in everyone], m.vfin.at[0:7])
    m.vfin[mine] = m.vgt[...]

    def both(fin, u, cols):
        return fin[u, 0:12, cols].astype(F32) + fin[4 + u, 0:12, cols].astype(F32)

    fin_g2.wait_recv()
    for u in range(4):
        wide = slice(D * u, D * u + D)
        gu_o[:, wide] = both(m.fin2, u, slice(0, D))
        gd_o[:, wide] = both(m.fin2, u, slice(D, 2 * D))
    fin_v.wait_recv()
    totals = m.vfin[0]
    for k in range(1, 8):
        totals = totals + m.vfin[k]
    source, target = iota((256, 128), 0), iota((256, 128), 1)
    own_12 = ((source - target == 12 * t) & (target < 12)).astype(BF)
    own_48 = ((source - target == 48 * t) & (target < 48)).astype(BF)
    row16 = iota((16, 128), 0)
    gvec_o[...] = jnp.where(row16 < 8, moved_by(totals, own_12), moved_by(totals, own_48))
    fin_g1.wait_recv()
    parts = [both(m.fin1, u, slice(0, D)) for u in range(4)]
    for k, ref in enumerate((gq_o, gk_o, gv_o, go_o)):
        ref[...] = jnp.concatenate([p[:, HW * k:HW * k + HW] for p in parts], axis=1)

    for flight in sent:
        flight.wait_send()
    for k in range(1, 16):
        @pl.when(s >= k)
        def _(k=k):
            grad_copy(k).wait_send()
    assert used[0] <= RECVS, used[0]


def hand_out(*refs):
    whole, vec, outs = refs[:8], refs[8], refs[9:]
    for src, dst in zip(whole, outs[:8]):
        dst[...] = src[...]
    for k, dst in enumerate(outs[8:16]):
        dst[...] = vec[k:k + 1, 0:12]
    outs[16][...] = vec[8:9, 0:48]


def body(
    tokens, seg_lengths, ln1_gain, ln1_bias, w_query, q_bias, w_key, w_value, v_bias,
    w_out, o_bias, ln2_gain, ln2_bias, w_up, up_bias, w_down, down_bias, d_out,
):
    vectors = [ln1_gain, ln1_bias, q_bias, v_bias, o_bias, ln2_gain, ln2_bias, down_bias, up_bias]
    shape = jax.ShapeDtypeStruct
    vmem = pl.BlockSpec(memory_space=pltpu.VMEM)
    shapes = [
        shape((ROWS, D), BF),
        shape((ROWS, D), F32),
        shape((12, D), F32),
        shape((12, D), F32),
        shape((12, D), F32),
        shape((12, D), F32),
        shape((12, 4 * D), F32),
        shape((12, 4 * D), F32),
    ]
    outs = pl.pallas_call(
        layer_kernel,
        out_shape=shapes + [shape((16, 128), F32)],
        in_specs=[pl.BlockSpec(memory_space=pltpu.SMEM)] + [vmem] * 17,
        out_specs=[vmem] * 9,
        scratch_shapes=[pltpu.VMEM(dims, kind) for dims, kind in SCRATCH.values()]
        + [pltpu.SemaphoreType.DMA((n,)) for n in (SENDS, RECVS, SLOTS)],
        compiler_params=pltpu.CompilerParams(
            collective_id=0, has_side_effects=True, vmem_limit_bytes=62 * 2**20
        ),
        name="layer",
    )(
        seg_lengths, tokens[0], d_out[0], w_query, w_key, w_value, w_out, w_up, w_down,
        *[v.reshape(1, -1) for v in vectors],
    )
    outs = pl.pallas_call(
        hand_out,
        out_shape=shapes + [shape((1, 12), F32)] * 8 + [shape((1, 48), F32)],
        in_specs=[vmem] * 9,
        out_specs=[vmem] * 17,
        compiler_params=pltpu.CompilerParams(vmem_limit_bytes=62 * 2**20),
        name="hand_out",
    )(*outs)
    out, g_tok, g_q, g_k, g_v, g_o, g_up, g_down = outs[:8]
    l1g, l1b, qb, vb, ob, l2g, l2b, db, ub = [v.reshape(-1) for v in outs[8:]]
    return (
        out[None], g_tok[None], l1g, l1b, g_q, qb, g_k, g_v, vb,
        g_o, ob, l2g, l2b, g_up, ub, g_down, db,
    )


def solution(mesh):
    rows, cols = P("batch", "seq", None), P("seq", None)
    one = P("seq")
    placed = (
        rows, P("batch", None), one, one, cols, one, cols, cols, one,
        cols, one, one, one, cols, one, cols, one, rows,
    )
    return jax.shard_map(
        body,
        mesh=mesh,
        in_specs=placed,
        out_specs=(
            rows, rows, one, one, cols, one, cols, cols, one,
            cols, one, one, one, cols, one, cols, one,
        ),
        check_vma=False,
    )
```

```python
import functools
import types

import jax
import jax.numpy as jnp
from jax import lax
from jax.experimental import pallas as pl
from jax.experimental.pallas import tpu as pltpu
from jax.sharding import PartitionSpec as P

BF = jnp.bfloat16
F32 = jnp.float32
MESH = pl.DeviceIdType.MESH
EPSILON = 1e-05
MASKED = -1e30
HIGHEST = lax.Precision.HIGHEST

ROWS = 128
SEG = 512
D = 768
HW = 192
HEADS = 3
HALF = 64
CHUNK = 256
SUMMARY = 50
SLOT = 64
SLOTS = 16
SUMS = SLOTS * SLOT


def dot(a, b, **kw):
    return jnp.dot(a, b, preferred_element_type=F32, **kw)


def dot_nt(a, b):
    return lax.dot_general(a, b, (((1,), (1,)), ((), ())), preferred_element_type=F32)


def dot_tn(a, b):
    return lax.dot_general(a, b, (((0,), (0,)), ((), ())), preferred_element_type=F32)


def iota(shape, dim):
    return lax.broadcasted_iota(jnp.int32, shape, dim)


def norm_stats(values):
    center = values - jnp.mean(values, axis=-1, keepdims=True)
    spread = jnp.mean(center * center, axis=-1, keepdims=True)
    return center, lax.rsqrt(spread + EPSILON)


SCRATCH = dict(
    pk1=((4, 16, D), BF),
    pk2=((4, 16, 2 * D), BF),
    p01=((4, 16, D), BF),
    p02=((4, 16, 2 * D), BF),
    w1=((4, 4, 48, D), BF),
    w2=((4, 4, 48, 2 * D), BF),
    wosl=((4, D // 2, 2 * HW), BF),
    wof=((D, D), BF),
    vin=((16, 128), F32),
    vb=((16, D), BF),
    vg=((3, 16, D), BF),
    vs1=((16, D), BF),
    vx=((3, 16, D), BF),
    vs2=((16, D), BF),
    vz=((3, 16, D), BF),
    vecs=((16, D), F32),
    toka=((SEG, D), BF),
    doa=((SEG, D), BF),
    nrm=((SEG, D), BF),
    nrmt=((D, SEG), BF),
    dot_=((D, SEG), BF),
    stat=((SEG, 128), F32),
    bias=((SEG, SEG), F32),
    q=((SEG, HW), BF),
    kv=((2, SEG, HW), BF),
    kvl=((SEG, 2 * HW), BF),
    kvs=((SUMS, 2 * HW), BF),
    ks=((SUMS, HW), BF),
    vs=((SUMS, HW), BF),
    ssrc=((SLOT, 2 * HW), BF),
    big=((SEG, HEADS * SEG), F32),
    ssum=((HEADS, CHUNK, SUMS), F32),
    prob1=((HEADS, SEG, SEG), BF),
    prob2=((HEADS, SEG, SUMS), BF),
    m1=((SEG, 128), F32),
    l1=((SEG, 128), F32),
    m2=((SEG, 128), F32),
    l2=((SEG, 128), F32),
    a1=((SEG, 128), F32),
    a2=((SEG, 128), F32),
    a1x=((SEG, HW), F32),
    a2x=((SEG, HW), F32),
    o1=((SEG, HW), F32),
    att=((SEG, HW), F32),
    attp=((4, 2, ROWS, 2 * HW), BF),
    atta=((4, SEG, HW), BF),
    hid=((SEG, D), F32),
    nm=((SEG, D), BF),
    nmt=((D, SEG), BF),
    act=((SEG, D), BF),
    gp=((SEG, D), BF),
    rm_s=((SEG, D), BF),
    rm_1=((2, 2, HALF, D), BF),
    rm_x=((2, HALF, D), BF),
    rm_2=((2, HALF, D), BF),
    ro_s=((SEG, D), BF),
    ro_1=((2, 2, HALF, D), BF),
    ro_x=((2, HALF, D), BF),
    ro_2=((2, HALF, D), BF),
    rn_s=((SEG, D), BF),
    rn_1=((2, 2, HALF, D), BF),
    rn_x=((2, HALF, D), BF),
    rn_2=((2, HALF, D), BF),
    gh=((ROWS, D), F32),
    gbr=((ROWS, D), BF),
    sa=((2, 4, HALF, HW), BF),
    sb=((2, 4, HALF, HW), BF),
    do=((2, 4, HALF, HW), BF),
    gba=((2, 4, HALF, HW), BF),
    ds=((HEADS, SEG, SUMS), BF),
    dkvs=((SUMS, 2 * HW), BF),
    sumg=((SLOTS, SLOT, 2 * HW), BF),
    dqkv=((SEG, 3 * HW), BF),
    g1=((4, 4, 48, D), BF),
    g2=((4, 4, 48, 2 * D), BF),
    rza1=((3, 4, 48, D // 2), BF),
    rxa1=((3, 48, D // 2), BF),
    rxb1=((3, 4, 48, D // 2), BF),
    rzb1=((3, 48, D // 2), BF),
    ha1=((4, 48, D // 2), BF),
    hb1=((4, 48, D // 2), BF),
    rza2=((3, 4, 48, D), BF),
    rxa2=((3, 48, D), BF),
    rxb2=((3, 4, 48, D), BF),
    rzb2=((3, 48, D), BF),
    ha2=((4, 48, D), BF),
    hb2=((4, 48, D), BF),
    fx1=((4, 16, D), BF),
    fx2=((4, 16, 2 * D), BF),
    fin1=((8, 16, D), BF),
    fin2=((8, 16, 2 * D), BF),
    vgr=((16, D), F32),
    vgx=((3, 16, D), F32),
    vgs=((16, D), F32),
    vgz=((3, 16, D), F32),
    sel=((D, 384), BF),
    vgt=((16, 256), F32),
    vfin=((8, 16, 256), F32),
)
SENDS = 24
RECVS = 66


class Flight:
    def __init__(self, waiter):
        self.waiter = waiter
        self.arrived = False
        self.left = False

    def wait_recv(self):
        if not self.arrived:
            self.waiter.wait_recv()
        self.arrived = True

    def wait_send(self):
        if not self.left:
            self.waiter.wait_send()
        self.left = True


def layer_kernel(
    seg_ref, tok, dout, wq, wk, wv, wo, wu, wd, *refs,
):
    vectors, refs = refs[:9], refs[9:]
    out_o, gtok_o, gq_o, gk_o, gv_o, go_o, gu_o, gd_o, gvec_o = refs[:9]
    scratch = refs[9:]
    m = types.SimpleNamespace(**dict(zip(SCRATCH, scratch[:-4])))
    ss, rs, far_ss, far_rs = scratch[-4:]
    batch = lax.axis_index("batch")
    place = lax.axis_index("seq")
    s = place // 4
    t = place % 4
    z = s // 4
    x = s % 4
    sib = t + 1 - 2 * (t % 2)
    over = (t + 2) % 4
    diag = 3 - t
    group = (over, diag, sib)

    def dev(seg, tt, bb):
        return (4 * seg + tt, bb)

    def here(tt):
        return dev(s, tt, batch)

    def along_x(k):
        return dev(4 * z + (x + k) % 4, t, batch)

    def along_z(k):
        return dev(4 * ((z + k) % 4) + x, t, batch)

    used = [0]
    sent = []

    def take(n=1):
        first = used[0]
        used[0] += n
        return first

    def fly(copies, total=None):
        k = len(sent)
        if k >= SENDS:
            sent[k - SENDS].wait_send()
        send_sem, recv_sem = ss.at[k % SENDS], rs.at[take()]
        for src, dst, device in copies:
            copy = pltpu.make_async_remote_copy(
                src_ref=src, dst_ref=dst, send_sem=send_sem, recv_sem=recv_sem,
                device_id=device, device_id_type=MESH,
            )
            copy.start()
        if total is not None:
            copy = pltpu.make_async_remote_copy(
                src_ref=total, dst_ref=total, send_sem=send_sem, recv_sem=recv_sem,
                device_id=device, device_id_type=MESH,
            )
        flight = Flight(copy)
        sent.append(flight)
        return flight

    def far_copy(which, src, dst, seg):
        return pltpu.make_async_remote_copy(
            src_ref=src, dst_ref=dst, send_sem=far_ss.at[which], recv_sem=far_rs.at[which],
            device_id=dev(seg, t, batch), device_id_type=MESH,
        )

    def slot_of(ref, seg):
        return ref.at[pl.ds(pl.multiple_of(SLOT * seg, SLOT), SLOT)]

    def far_wait(which, count, received):
        for n in range(1, 16):
            @pl.when(count == n)
            def _(n=n):
                part = m.kvs.at[0:SLOT * n]
                if received:
                    far_copy(which, part, part, s).wait_recv()
                else:
                    far_copy(which, part, part, s).wait_send()

    def block(c, k):
        return pl.ds(pl.multiple_of(CHUNK * c + HALF * k, HALF), HALF)

    def within(rows, c):
        return pl.ds(pl.multiple_of(rows.start - CHUNK * c, rows.size), rows.size)

    def loop(first, count, size, fn, unroll=4):
        def step(j, carry):
            fn(pl.ds(pl.multiple_of(first + j * size, size), size))
            return carry

        lax.fori_loop(0, count, step, 0, unroll=unroll)

    m.kvs[...] = jnp.zeros((SUMS, 2 * HW), BF)
    m.sumg[...] = jnp.zeros((SLOTS, SLOT, 2 * HW), BF)
    barrier = pltpu.get_barrier_semaphore()
    partners = [here(u) for u in group]
    partners += [dev((s + k) % 16, t, batch) for k in range(1, 16)]
    partners += [dev(s, u, 1 - batch) for u in (t, sib, over, diag)]
    for partner in partners:
        pl.semaphore_signal(barrier, inc=1, device_id=partner, device_id_type=MESH)
    m.pk1[...] = jnp.zeros((4, 16, D), BF)
    for u in range(4):
        cols = slice(HW * u, HW * u + HW)
        m.pk1[u, 0:12, :] = jnp.concatenate(
            [wk[:, cols], wv[:, cols], wq[:, cols], wo[:, cols]], axis=1
        )
    m.vin[...] = jnp.zeros((16, 128), F32)
    for k, ref in enumerate(vectors[:8]):
        m.vin[k:k + 1, 0:12] = ref[...].astype(F32)
    m.vin[8:9, 0:48] = vectors[8][...].astype(F32)
    shift = iota((128, D), 1) - iota((128, D), 0)
    narrow = dot(m.vin[...].astype(BF), (shift == 12 * place).astype(BF))
    wider = dot(m.vin[...].astype(BF), (shift == 48 * (place % 16)).astype(BF))
    vec_row = iota((16, D), 0)
    m.vb[...] = jnp.where(
        vec_row < 8, narrow, jnp.where(vec_row == 8 + z, wider[8:9, :], 0.0)
    ).astype(BF)
    pl.semaphore_wait(barrier, len(partners))

    first1 = fly([(m.pk1.at[u], m.p01.at[t], here(u)) for u in group], m.p01.at[0:3])
    firstv = fly(
        [(m.vb, m.vg.at[k], here(u)) for k, u in enumerate((sib, over, diag))], m.vg
    )
    m.p01[t] = m.pk1[t]
    m.pk2[...] = jnp.zeros((4, 16, 2 * D), BF)
    for u in range(4):
        wide = slice(D * u, D * u + D)
        m.pk2[u, 0:12, 0:D] = wu[:, wide]
        m.pk2[u, 0:12, D:] = wd[:, wide]
    m.p02[t] = m.pk2[t]
    for c in range(2):
        m.toka[block(c, t), :] = tok[HALF * c:HALF * c + HALF, :]
        m.doa[block(c, t), :] = dout[HALF * c:HALF * c + HALF, :]

    def gather_start(ref):
        moves = [
            fly([(ref.at[block(c, t)], ref.at[block(c, t)], here(u)) for c in (0, 1)],
                ref.at[0:ROWS])
            for u in (over, sib)
        ]
        return moves

    def gather_pass(moves, ref):
        moves[0].wait_recv()
        moves.append(
            fly([(ref.at[block(c, over)], ref.at[block(c, over)], here(sib)) for c in (0, 1)],
                ref.at[0:ROWS])
        )

    def finish(moves):
        for move in moves:
            move.wait_recv()

    row48 = iota((48, 64), 0)
    owner48 = (
        (row48 >= 12).astype(jnp.int32)
        + (row48 >= 24).astype(jnp.int32)
        + (row48 >= 36).astype(jnp.int32)
    )
    squeeze = (iota((48, 64), 1) == row48 + 4 * owner48).astype(BF)

    def spread_start(w, a, b):
        mine_a, mine_b = w.at[z, x, :, a], w.at[z, x, :, b]
        return (
            fly([(mine_a, mine_a, along_x(k)) for k in (1, 3, 2)], w.at[0, 0:3, :, a]),
            fly([(mine_b, mine_b, along_z(k)) for k in (1, 3, 2)], w.at[0, 0:3, :, b]),
        )

    def pass_a(w, a, moves):
        plane_a = w.at[z, :, :, a]
        moves[0].wait_recv()
        return fly([(plane_a, plane_a, along_z(k)) for k in (1, 3, 2)], w.at[0:3, :, :, a])

    def pass_b(w, b, moves):
        plane_b = w.at[:, x, :, b]
        moves[1].wait_recv()
        return fly([(plane_b, plane_b, along_x(k)) for k in (1, 3, 2)], w.at[0:3, :, :, b])

    def spread_pass(w, a, b, moves):
        return pass_a(w, a, moves), pass_b(w, b, moves)

    kv_cols = pl.ds(0, 256), pl.ds(256, 128)
    qo_cols = pl.ds(384, 128), pl.ds(512, 256)
    up_down = pl.ds(0, D), pl.ds(D, D)
    halves = pl.ds(0, D // 2), pl.ds(D // 2, D // 2)

    first1.wait_recv()
    m.w1[z, x] = dot(squeeze, m.p01[...].reshape(64, D)).astype(BF)
    phase1 = spread_start(m.w1, *kv_cols)
    phase1b = spread_start(m.w1, *qo_cols)
    first2 = fly([(m.pk2.at[u], m.p02.at[t], here(u)) for u in group], m.p02.at[0:3])
    ag_tok = gather_start(m.toka)

    seg_len = seg_ref[0, s]

    def token_of(rows):
        return rows + 64 * ((rows % CHUNK) // HALF) - 192 * (rows // CHUNK)

    k_pos = token_of(iota((1, SEG), 1))

    def mask(rows):
        mine = token_of(rows.start + iota((ROWS, 1), 0))
        ok = ((k_pos <= mine) & (k_pos < seg_len)) | (k_pos == mine)
        m.bias[rows, :] = jnp.where(ok, 0.0, MASKED)

    loop(0, 4, ROWS, mask)
    s_col = iota((8, SUMS), 1)
    sum_bias = jnp.where((s_col < SLOT * s) & (s_col % SLOT < SUMMARY), 0.0, MASKED)[0:1, :]
    pick_row = iota((SLOT, SEG), 0)
    pick = ((k_pos == seg_len - SUMMARY + pick_row) & (pick_row < SUMMARY)).astype(BF)
    lane_head = iota((1, HW), 1) // 64

    def of_head(value, h):
        return jnp.where(lane_head == h, value, jnp.zeros_like(value))

    def by_head(cols):
        return jnp.where(
            lane_head == 0, cols[:, 0:1], jnp.where(lane_head == 1, cols[:, 1:2], cols[:, 2:3])
        )

    def add4(own, got):
        return own.astype(F32) + got[0].astype(F32) + got[1].astype(F32) + got[2].astype(F32)

    def moved_by(rows, one_hot):
        high = rows.astype(BF)
        rest = rows - high.astype(F32)
        mid = rest.astype(BF)
        low = (rest - mid.astype(F32)).astype(BF)
        pieces = dot(jnp.concatenate([high, mid, low], axis=0), one_hot)
        return pieces[0:16, :] + pieces[16:32, :] + pieces[32:48, :]

    feature, lane = iota((D, 128), 0), iota((D, 128), 1)
    m.sel[:, 0:128] = ((feature - lane == 48 * s) & (lane < 48)).astype(BF)
    feature, lane = iota((D, 256), 0), iota((D, 256), 1)
    m.sel[:, 128:384] = ((feature - lane == 192 * x) & (lane < 192)).astype(BF)

    firstv.wait_recv()
    m.vs1[...] = add4(m.vb[...], m.vg).astype(BF)
    vx = fly([(m.vs1, m.vx.at[k - 1], along_x(k)) for k in (1, 2, 3)], m.vx)
    ends1 = spread_pass(m.w1, *kv_cols, phase1)
    ends1b = spread_pass(m.w1, *qo_cols, phase1b)
    vx.wait_recv()
    m.vs2[...] = add4(m.vs1[...], m.vx).astype(BF)
    vz = fly([(m.vs2, m.vz.at[k - 1], along_z(k)) for k in (1, 2, 3)], m.vz)
    first2.wait_recv()
    m.w2[z, x] = dot(squeeze, m.p02[...].reshape(64, 2 * D)).astype(BF)
    phase2 = spread_start(m.w2, *up_down)
    gather_pass(ag_tok, m.toka)
    ag_do = gather_start(m.doa)
    vz.wait_recv()
    m.vecs[...] = add4(m.vs2[...], m.vz)
    gain1, shift1 = m.vecs[0:1, :], m.vecs[1:2, :]
    gain2, shift2 = m.vecs[5:6, :], m.vecs[6:7, :]
    o_bias, down_bias = m.vecs[4:5, :], m.vecs[7:8, :]

    def my_cols(row):
        whole = m.vecs[row:row + 1, :]
        value = whole[:, 0:HW]
        for u in range(1, 4):
            value = jnp.where(t == u, whole[:, HW * u:HW * u + HW], value)
        return value

    q_bias, v_bias = my_cols(2), my_cols(3)
    up_bias = m.vecs[8:9, :]
    for u in range(1, 4):
        up_bias = jnp.where(t == u, m.vecs[8 + u:9 + u, :], up_bias)

    finish(ag_tok)

    def norm1(rows):
        values = m.toka[rows, :].astype(F32)
        mean = jnp.mean(values, axis=-1, keepdims=True)
        center = values - mean
        scale = lax.rsqrt(jnp.mean(center * center, axis=-1, keepdims=True) + EPSILON)
        m.nrm[rows, :] = (center * scale * gain1 + shift1).astype(BF)
        m.stat[rows, 0:1] = mean
        m.stat[rows, 1:2] = scale

    loop(0, 4, ROWS, norm1)
    m.nrmt[...] = m.nrm[...].T

    finish(ends1)
    kv_bias = jnp.concatenate([jnp.zeros((1, HW), F32), v_bias], axis=1)
    m.kvl[...] = (dot(m.nrm[...], m.w1[:, :, :, 0:2 * HW].reshape(D, 2 * HW)) + kv_bias).astype(BF)

    m.ssrc[...] = dot(pick, m.kvl[...]).astype(BF)
    for k in range(1, 16):
        @pl.when(s + k < 16)
        def _(k=k):
            far_copy(0, m.ssrc, slot_of(m.kvs, s), (s + k) % 16).start()
    ends2b = pass_b(m.w2, up_down[1], phase2)
    finish(ends1b)
    m.q[...] = (
        (dot(m.nrm[...], m.w1[:, :, :, 2 * HW:3 * HW].reshape(D, HW)) + q_bias) * 0.125
    ).astype(BF)
    w_o = m.w1[...].reshape(D, D)[:, 3 * HW:]
    m.wosl[t] = jnp.concatenate([w_o[0:D // 2, :], w_o[D // 2:, :]], axis=1)
    m.kv[0] = m.kvl[:, 0:HW]
    m.kv[1] = m.kvl[:, HW:]
    ag_wo = [fly([(m.wosl.at[t], m.wosl.at[t], here(u))]) for u in (over, sib)]

    for h in range(HEADS):
        m.big[:, SEG * h:SEG * h + SEG] = dot_nt(of_head(m.q[...], h), m.kv[0]) + m.bias[...]
    for h in range(HEADS):
        def soften1(rows, h=h):
            score = m.big[rows, SEG * h:SEG * h + SEG]
            peak = jnp.max(score, axis=-1, keepdims=True)
            power = jnp.exp(score - peak)
            m.prob1[h, rows, :] = power.astype(BF)
            m.m1[rows, h:h + 1] = peak
            m.l1[rows, h:h + 1] = jnp.sum(power, axis=-1, keepdims=True)

        loop(0, 4, ROWS, soften1)
        part = dot(m.prob1[h], of_head(m.kv[1], h))
        m.o1[...] = part if h == 0 else m.o1[...] + part
    gather_pass(ag_do, m.doa)

    far_wait(0, s, True)
    ends2a = pass_a(m.w2, up_down[0], phase2)
    ends2 = (ends2a, ends2b)
    m.ks[...] = m.kvs[:, 0:HW]
    m.vs[...] = m.kvs[:, HW:]

    ag_att = []

    def attend(c):
        rows_c = slice(CHUNK * c, CHUNK * c + CHUNK)
        part = None
        for h in range(HEADS):
            m.ssum[h] = dot_nt(of_head(m.q[rows_c, :], h), m.ks[...]) + sum_bias

            def soften2(rows, h=h):
                score = m.ssum[h, within(rows, c), :]
                peak = jnp.max(score, axis=-1, keepdims=True)
                power = jnp.exp(score - peak)
                m.prob2[h, rows, :] = power.astype(BF)
                m.m2[rows, h:h + 1] = peak
                m.l2[rows, h:h + 1] = jnp.sum(power, axis=-1, keepdims=True)

            loop(CHUNK * c, 2, ROWS, soften2)
            more = dot(m.prob2[h, rows_c, :], of_head(m.vs[...], h))
            part = more if h == 0 else part + more
        m1, m2 = m.m1[rows_c, 0:HEADS], m.m2[rows_c, 0:HEADS]
        peak = jnp.maximum(m1, m2)
        e1, e2 = jnp.exp(m1 - peak), jnp.exp(m2 - peak)
        share = 1.0 / (m.l1[rows_c, 0:HEADS] * e1 + m.l2[rows_c, 0:HEADS] * e2)
        a1, a2 = e1 * share, e2 * share
        m.a1[rows_c, 0:HEADS] = a1
        m.a2[rows_c, 0:HEADS] = a2
        a1x, a2x = by_head(a1), by_head(a2)
        m.a1x[rows_c, :] = a1x
        m.a2x[rows_c, :] = a2x
        attended = m.o1[rows_c, :] * a1x + part * a2x
        m.att[rows_c, :] = attended
        low = attended.astype(BF)
        m.attp[t, c] = jnp.concatenate([low[0:ROWS, :], low[ROWS:, :]], axis=1)
        mine_c = m.attp.at[t, c]
        ag_att.append([fly([(mine_c, mine_c, here(u))]) for u in (over, sib)])

    attend(0)
    ag_wo[0].wait_recv()
    ag_wo.append(fly([(m.wosl.at[over], m.wosl.at[over], here(sib))]))
    attend(1)
    finish(ag_wo)
    m.wof[0:D // 2, :] = jnp.concatenate([m.wosl[u, :, 0:HW] for u in range(4)], axis=1)
    m.wof[D // 2:, :] = jnp.concatenate([m.wosl[u, :, HW:] for u in range(4)], axis=1)

    def att_pass(c):
        ag_att[c][0].wait_recv()
        theirs = m.attp.at[over, c]
        ag_att[c].append(fly([(theirs, theirs, here(sib))]))

    def scatter_start(name, cs):
        src, r1 = getattr(m, name + "_s"), getattr(m, name + "_1")
        return [
            fly([(src.at[block(c, k)], r1.at[c, i], here(sib)) for c in cs],
                r1.at[0:len(cs), i])
            for i, k in ((1, diag), (0, sib))
        ]

    def scatter_pass(name, cs, moves):
        src, r1 = getattr(m, name + "_s"), getattr(m, name + "_1")
        cross, r2 = getattr(m, name + "_x"), getattr(m, name + "_2")
        moves[0].wait_recv()
        for c in cs:
            cross[c] = (src[block(c, over), :].astype(F32) + r1[c, 1].astype(F32)).astype(BF)
        moves.append(
            fly([(cross.at[c], r2.at[c], here(over)) for c in cs], r2.at[0:len(cs)])
        )

    def scatter_end(name, c, moves):
        src, r1 = getattr(m, name + "_s"), getattr(m, name + "_1")
        r2 = getattr(m, name + "_2")
        moves[1].wait_recv()
        moves[2].wait_recv()
        return src[block(c, t), :].astype(F32) + r1[c, 0].astype(F32) + r2[c].astype(F32)

    def gelu(rows):
        a = m.big[rows, 0:D]
        square = a * a
        bend = jnp.tanh(0.7978845608028654 * (a + 0.044715 * (square * a)))
        half = 0.5 * (1.0 + bend)
        m.act[rows, :] = (a * half).astype(BF)
        slope = half + (0.5 * a) * (1.0 - bend * bend) * (
            0.7978845608028654 * (1.0 + 0.134145 * square)
        )
        m.gp[rows, :] = (m.big[rows, D:] * slope).astype(BF)

    def norm2(rows):
        center, scale = norm_stats(m.hid[rows, :])
        m.nm[rows, :] = (center * scale * gain2 + shift2).astype(BF)

    def project(c):
        rows_c = slice(CHUNK * c, CHUNK * c + CHUNK)
        finish(ag_att[c])
        for u in range(4):
            m.atta[u, CHUNK * c:CHUNK * c + ROWS, :] = m.attp[u, c, :, 0:HW]
            m.atta[u, CHUNK * c + ROWS:CHUNK * c + CHUNK, :] = m.attp[u, c, :, HW:]
        branch = dot(m.atta[0, rows_c, :], m.wof[0:HW, :])
        for u in range(1, 4):
            branch = branch + dot(m.atta[u, rows_c, :], m.wof[HW * u:HW * u + HW, :])
        m.hid[rows_c, :] = m.toka[rows_c, :].astype(F32) + branch + o_bias
        loop(CHUNK * c, 2, ROWS, norm2)

    def feed(c):
        rows_c = slice(CHUNK * c, CHUNK * c + CHUNK)
        m.big[rows_c, 0:D] = dot(m.nm[rows_c, :], m.w2[:, :, :, 0:D].reshape(D, D)) + up_bias
        m.big[rows_c, D:] = dot(m.doa[rows_c, :], m.w2[:, :, :, D:].reshape(D, D))
        loop(CHUNK * c, 4, 64, gelu)
        m.rm_s[rows_c, :] = dot_nt(m.gp[rows_c, :], m.w2[:, :, :, 0:D].reshape(D, D)).astype(BF)
        return scatter_start("rm", (c,))

    att_pass(0)
    project(0)
    att_pass(1)
    finish(ag_do)
    finish(ends2)
    rm0 = feed(0)
    project(1)
    scatter_pass("rm", (0,), rm0)
    rm1 = feed(1)

    m.dot_[...] = m.doa[...].T
    m.nmt[...] = m.nm[...].T
    scatter_pass("rm", (1,), rm1)
    m.g2[:, :, :, 0:D] = dot(m.nmt[...], m.gp[...]).astype(BF).reshape(4, 4, 48, D)
    m.g2[:, :, :, D:] = dot(m.dot_[...], m.act[...]).astype(BF).reshape(4, 4, 48, D)

    def reduce_start(g, tag, a, b, at_a, at_b):
        rza, rxb = getattr(m, "rza" + tag), getattr(m, "rxb" + tag)
        return (
            fly([(g.at[(z + k) % 4, :, :, a], rza.at[k - 1, :, :, at_a], along_z(k))
                 for k in (1, 3, 2)], rza.at[:, :, :, at_a]),
            fly([(g.at[:, (x + k) % 4, :, b], rxb.at[k - 1, :, :, at_b], along_x(k))
                 for k in (1, 3, 2)], rxb.at[:, :, :, at_b]),
        )

    def reduce_pass(g, tag, pieces):
        rza, rxb = getattr(m, "rza" + tag), getattr(m, "rxb" + tag)
        rxa, rzb = getattr(m, "rxa" + tag), getattr(m, "rzb" + tag)
        ha, hb = getattr(m, "ha" + tag), getattr(m, "hb" + tag)
        for (a, b, at_a, at_b), moves in pieces:
            into = slice(at_a.start, at_a.start + at_a.size)
            moves[0].wait_recv()
            for k in range(4):
                ha[k, :, into] = add4(
                    g[z, k, :, a.start:a.start + a.size], [rza[j, k, :, into] for j in range(3)]
                ).astype(BF)
        a2 = fly([(ha.at[(x + k) % 4], rxa.at[k - 1], along_x(k)) for k in (1, 3, 2)], rxa)
        for (a, b, at_a, at_b), moves in pieces:
            into = slice(at_b.start, at_b.start + at_b.size)
            moves[1].wait_recv()
            for k in range(4):
                hb[k, :, into] = add4(
                    g[k, x, :, b.start:b.start + b.size], [rxb[j, k, :, into] for j in range(3)]
                ).astype(BF)
        b2 = fly([(hb.at[(z + k) % 4], rzb.at[k - 1], along_z(k)) for k in (1, 3, 2)], rzb)
        return a2, b2

    row64 = iota((64, 48), 0)
    expand = (
        (iota((64, 48), 1) == row64 - 4 * (row64 // 16)) & (row64 % 16 < 12)
    ).astype(BF)
    mine = 4 * batch + t
    everyone = [(u, dev(s, u, 1 - batch)) for u in (over, diag, sib, t)]
    everyone += [(u, here(u)) for u in group]

    def reduce_last(tag, half, moves):
        rxa, rzb = getattr(m, "rxa" + tag), getattr(m, "rzb" + tag)
        ha, hb = getattr(m, "ha" + tag), getattr(m, "hb" + tag)
        fx, fin = getattr(m, "fx" + tag), getattr(m, "fin" + tag)
        finish(moves)
        a = add4(ha[x], [rxa[j] for j in range(3)]).astype(BF)
        b = add4(hb[z], [rzb[j] for j in range(3)]).astype(BF)
        fx[:, :, 0:half] = dot(expand, a).astype(BF).reshape(4, 16, half)
        fx[:, :, half:] = dot(expand, b).astype(BF).reshape(4, 16, half)
        moves = fly([(fx.at[u], fin.at[mine], device) for u, device in everyone], fin.at[0:7])
        fin[mine] = fx[t]
        return moves

    cols2 = up_down + (pl.ds(0, D), pl.ds(0, D))
    rg2 = reduce_start(m.g2, "2", *cols2)

    zero_row = jnp.zeros((1, D), F32)
    ones = jnp.ones((8, SEG), BF)

    def col_sums(value):
        return dot(ones[:, 0:value.shape[0]], value)[0:1, :]

    def norm_back(values, grads, gain):
        center, scale = norm_stats(values)
        unit = center * scale
        inner = grads * gain
        return unit, scale * (
            inner
            - jnp.mean(inner, axis=-1, keepdims=True)
            - unit * jnp.mean(inner * unit, axis=-1, keepdims=True)
        )

    g_gain2, g_shift2 = zero_row, zero_row
    aa = []
    for c in range(2):
        at = slice(HALF * c, HALF * c + HALF)
        grads = scatter_end("rm", c, rm0 if c == 0 else rm1)
        unit, into = norm_back(m.hid[block(c, t), :], grads, gain2)
        into = into + dout[at, :].astype(F32)
        m.gh[at, :] = into
        low = into.astype(BF)
        m.gbr[at, :] = low
        for u in range(4):
            m.sa[c, u] = dot_nt(low, m.wof[HW * u:HW * u + HW, :]).astype(BF)
        aa.append(
            fly([(m.sa.at[c, u], m.do.at[c, t], here(u)) for u in group], m.do.at[c, 0:3])
        )
        m.do[c, t] = m.sa[c, t]
        g_gain2 += jnp.sum(grads * unit, axis=0, keepdims=True)
        g_shift2 += jnp.sum(grads, axis=0, keepdims=True)
    m.ro_s[...] = dot_nt(m.act[...], m.w2[:, :, :, D:].reshape(D, D)).astype(BF)
    for u in range(4):
        cols = m.gbr[:, HW * u:HW * u + HW]
        m.sb[0, u] = cols[0:HALF, :]
        m.sb[1, u] = cols[HALF:, :]
    qt = m.q[...].T
    m.o1[...] = jnp.zeros((SEG, HW), F32)

    finish(aa)
    do_all = m.do[...].reshape(SEG, HW)
    do_wide = do_all.astype(F32)
    weighed = do_wide * m.att[...]
    for h in range(HEADS):
        m.m1[:, h:h + 1] = jnp.sum(of_head(weighed, h), axis=-1, keepdims=True)
    dot1 = (do_wide * m.a1x[...]).astype(BF).T
    dot2 = (do_wide * m.a2x[...]).astype(BF).T
    ab = fly(
        [(m.sb.at[c, u], m.gba.at[c, t], here(u)) for u in group for c in (0, 1)],
        m.gba.at[:, 0:3],
    )
    m.gba[0, t] = m.sb[0, t]
    m.gba[1, t] = m.sb[1, t]
    ro = scatter_start("ro", (0, 1))
    for c in range(2):
        rows_c = slice(CHUNK * c, CHUNK * c + CHUNK)
        for h in range(HEADS):
            m.ssum[h] = dot_nt(of_head(do_all[rows_c, :], h), m.vs[...])

            def back_sum(rows, h=h, c=c):
                weight = m.prob2[h, rows, :].astype(F32)
                slope = (m.ssum[h, within(rows, c), :] - m.m1[rows, h:h + 1]) * m.a2[rows, h:h + 1]
                m.ds[h, rows, :] = (weight * slope).astype(BF)

            loop(CHUNK * c, 2, ROWS, back_sum)
    for h in range(HEADS):
        feat, feat_v = slice(64 * h, 64 * h + 64), slice(HW + 64 * h, HW + 64 * h + 64)
        m.big[feat, 0:SUMS] = dot(qt[feat, :], m.ds[h])
        m.big[feat_v, 0:SUMS] = dot(dot2[feat, :], m.prob2[h])
    m.dkvs[...] = m.big[0:2 * HW, 0:SUMS].T.astype(BF)
    for k in range(1, 16):
        @pl.when(s >= k)
        def _(k=k):
            seg = (s + 16 - k) % 16
            far_copy(1, slot_of(m.dkvs, seg), m.sumg.at[k], seg).start()
    ends_g2 = reduce_pass(m.g2, "2", [(cols2, rg2)])
    scatter_pass("ro", (0, 1), ro)

    for h in range(HEADS):
        m.o1[...] += dot(m.ds[h], of_head(m.ks[...], h))
    for h in range(HEADS):
        m.big[:, SEG * h:SEG * h + SEG] = dot_nt(of_head(do_all, h), m.kv[1])
    for h in range(HEADS):
        def back_own(rows, h=h):
            weight = m.prob1[h, rows, :].astype(F32)
            slope = (m.big[rows, SEG * h:SEG * h + SEG] - m.m1[rows, h:h + 1]) * m.a1[rows, h:h + 1]
            m.ds[h, rows, 0:SEG] = (weight * slope).astype(BF)

        loop(0, 4, ROWS, back_own)
        score_grads = m.ds[h, :, 0:SEG]
        m.o1[...] += dot(score_grads, of_head(m.kv[0], h))
        feat, feat_v = slice(64 * h, 64 * h + 64), slice(HW + 64 * h, HW + 64 * h + 64)
        m.bias[feat, :] = dot(qt[feat, :], score_grads)
        m.bias[feat_v, :] = dot(dot1[feat, :], m.prob1[h])
    for u in range(4):
        m.nmt[HW * u:HW * u + HW, :] = m.atta[u].T
    ab.wait_recv()
    g_o = dot(m.nmt[...], m.gba[...].reshape(SEG, HW))
    dq = m.o1[...].astype(BF) * jnp.asarray(0.125, BF)
    m.g1[:, :, :, 2 * HW:] = (
        jnp.concatenate([dot(m.nrmt[...], dq), g_o], axis=1).astype(BF).reshape(4, 4, 48, 2 * HW)
    )
    cols_qo = qo_cols + (pl.ds(256, 128), pl.ds(128, 256))
    cols_kv = kv_cols + (pl.ds(0, 256), pl.ds(0, 128))
    rg1_qo = reduce_start(m.g1, "1", *cols_qo)

    far_wait(1, 15 - s, True)

    total = m.sumg[0].astype(F32)
    for k in range(1, SLOTS):
        total = total + m.sumg[k].astype(F32)
    high = total.astype(BF)
    rest = (total - high.astype(F32)).astype(BF)
    dkv = (m.bias[0:2 * HW, :] + dot_tn(high, pick) + dot_tn(rest, pick)).T.astype(BF)
    m.dqkv[...] = jnp.concatenate([dkv, dq], axis=1)

    m.g1[:, :, :, 0:2 * HW] = dot(m.nrmt[...], dkv).astype(BF).reshape(4, 4, 48, 2 * HW)
    rg1_kv = reduce_start(m.g1, "1", *cols_kv)
    m.rn_s[...] = dot_nt(m.dqkv[...], m.w1[...].reshape(D, D)[:, 0:3 * HW]).astype(BF)
    rn = [scatter_start("rn", (c,)) for c in range(2)]

    def gain_grads(j, carry):
        rows = pl.ds(pl.multiple_of(j * 64, 64), 64)
        grads = m.rn_s[rows, :].astype(F32)
        unit = (m.toka[rows, :].astype(F32) - m.stat[rows, 0:1]) * m.stat[rows, 1:2]
        return (
            carry[0] + jnp.sum((grads * unit).reshape(8, 8, D), axis=0),
            carry[1] + jnp.sum(grads.reshape(8, 8, D), axis=0),
        )

    zero8 = jnp.zeros((8, D), F32)
    g_gain1, g_shift1 = lax.fori_loop(0, 8, gain_grads, (zero8, zero8), unroll=4)
    scatter_pass("rn", (0,), rn[0])
    scatter_pass("rn", (1,), rn[1])
    g_qkvb = col_sums(m.dqkv[...])

    def in_place(row):
        none = jnp.zeros((1, HW), F32)
        return jnp.concatenate([jnp.where(t == u, row, none) for u in range(4)], axis=1)

    rows8 = (
        jnp.sum(g_gain1, axis=0, keepdims=True),
        jnp.sum(g_shift1, axis=0, keepdims=True),
        in_place(g_qkvb[:, 2 * HW:]),
        in_place(g_qkvb[:, HW:2 * HW]),
        col_sums(m.gbr[...]),
        g_gain2,
        g_shift2,
        col_sums(dout[...]),
    )
    m.vgr[...] = jnp.zeros((16, D), F32)
    for k, row in enumerate(rows8):
        m.vgr[k:k + 1, :] = row
    g_ub = col_sums(m.gp[...])
    for u in range(4):
        m.vgr[8 + u:9 + u, :] = jnp.where(t == u, g_ub, zero_row)
    vgx = fly([(m.vgr, m.vgx.at[k - 1], along_x(k)) for k in (1, 2, 3)], m.vgx)
    fin_g2 = reduce_last("2", D, ends_g2)
    for c in range(2):
        out_o[HALF * c:HALF * c + HALF, :] = (
            scatter_end("ro", c, ro) + m.hid[block(c, t), :] + down_bias
        ).astype(BF)
    ends_g1 = reduce_pass(m.g1, "1", [(cols_qo, rg1_qo), (cols_kv, rg1_kv)])
    vgx.wait_recv()
    m.vgs[...] = add4(m.vgr[...], m.vgx)
    vgz = fly([(m.vgs, m.vgz.at[k - 1], along_z(k)) for k in (1, 2, 3)], m.vgz)

    for c in range(2):
        at = slice(HALF * c, HALF * c + HALF)
        grads = scatter_end("rn", c, rn[c])
        _, into = norm_back(tok[at, :].astype(F32), grads, gain1)
        gtok_o[at, :] = into + m.gh[at, :]
    fin_g1 = reduce_last("1", D // 2, ends_g1)
    vgz.wait_recv()
    totals = add4(m.vgs[...], m.vgz)
    moved = moved_by(totals, m.sel[...])
    up_row = jnp.sum(jnp.where(iota((16, 256), 0) == 8 + z, moved[:, 128:384], 0.0), axis=0, keepdims=True)
    m.vgt[...] = jnp.zeros((16, 256), F32)
    m.vgt[0:8, 0:128] = moved[0:8, 0:128]
    m.vgt[8:9, :] = up_row
    fin_v = fly([(m.vgt, m.vfin.at[mine], device) for _, device in everyone], m.vfin.at[0:7])
    m.vfin[mine] = m.vgt[...]

    def both(fin, u, cols):
        return fin[u, 0:12, cols].astype(F32) + fin[4 + u, 0:12, cols].astype(F32)

    fin_g2.wait_recv()
    for u in range(4):
        wide = slice(D * u, D * u + D)
        gu_o[:, wide] = both(m.fin2, u, slice(0, D))
        gd_o[:, wide] = both(m.fin2, u, slice(D, 2 * D))
    fin_v.wait_recv()
    totals = m.vfin[0]
    for k in range(1, 8):
        totals = totals + m.vfin[k]
    source, target = iota((256, 128), 0), iota((256, 128), 1)
    own_12 = ((source - target == 12 * t) & (target < 12)).astype(BF)
    own_48 = ((source - target == 48 * t) & (target < 48)).astype(BF)
    row16 = iota((16, 128), 0)
    gvec_o[...] = jnp.where(row16 < 8, moved_by(totals, own_12), moved_by(totals, own_48))
    fin_g1.wait_recv()
    for u in range(4):
        part = both(m.fin1, u, slice(0, D))
        ordered = jnp.concatenate(
            [part[:, 0:256], part[:, 384:512], part[:, 256:384], part[:, 512:]], axis=1
        )
        for k, ref in enumerate((gk_o, gv_o, gq_o, go_o)):
            ref[:, HW * u:HW * u + HW] = ordered[:, HW * k:HW * k + HW]

    for flight in sent:
        flight.wait_send()
    far_wait(0, 15 - s, False)
    far_wait(1, s, False)
    assert used[0] <= RECVS, used[0]


def hand_out(*refs):
    whole, vec, outs = refs[:8], refs[8], refs[9:]
    for src, dst in zip(whole, outs[:8]):
        dst[...] = src[...]
    for k, dst in enumerate(outs[8:16]):
        dst[...] = vec[k:k + 1, 0:12]
    outs[16][...] = vec[8:9, 0:48]


def body(
    tokens, seg_lengths, ln1_gain, ln1_bias, w_query, q_bias, w_key, w_value, v_bias,
    w_out, o_bias, ln2_gain, ln2_bias, w_up, up_bias, w_down, down_bias, d_out,
):
    vectors = [ln1_gain, ln1_bias, q_bias, v_bias, o_bias, ln2_gain, ln2_bias, down_bias, up_bias]
    shape = jax.ShapeDtypeStruct
    vmem = pl.BlockSpec(memory_space=pltpu.VMEM)
    shapes = [
        shape((ROWS, D), BF),
        shape((ROWS, D), F32),
        shape((12, D), F32),
        shape((12, D), F32),
        shape((12, D), F32),
        shape((12, D), F32),
        shape((12, 4 * D), F32),
        shape((12, 4 * D), F32),
    ]
    outs = pl.pallas_call(
        layer_kernel,
        out_shape=shapes + [shape((16, 128), F32)],
        in_specs=[pl.BlockSpec(memory_space=pltpu.SMEM)] + [vmem] * 17,
        out_specs=[vmem] * 9,
        scratch_shapes=[pltpu.VMEM(dims, kind) for dims, kind in SCRATCH.values()]
        + [pltpu.SemaphoreType.DMA((n,)) for n in (SENDS, RECVS, 2, 2)],
        compiler_params=pltpu.CompilerParams(
            collective_id=0, has_side_effects=True, vmem_limit_bytes=62 * 2**20
        ),
        name="layer",
    )(
        seg_lengths, tokens[0], d_out[0], w_query, w_key, w_value, w_out, w_up, w_down,
        *[v.reshape(1, -1) for v in vectors],
    )
    outs = pl.pallas_call(
        hand_out,
        out_shape=shapes + [shape((1, 12), F32)] * 8 + [shape((1, 48), F32)],
        in_specs=[vmem] * 9,
        out_specs=[vmem] * 17,
        compiler_params=pltpu.CompilerParams(vmem_limit_bytes=62 * 2**20),
        name="hand_out",
    )(*outs)
    out, g_tok, g_q, g_k, g_v, g_o, g_up, g_down = outs[:8]
    l1g, l1b, qb, vb, ob, l2g, l2b, db, ub = [v.reshape(-1) for v in outs[8:]]
    return (
        out[None], g_tok[None], l1g, l1b, g_q, qb, g_k, g_v, vb,
        g_o, ob, l2g, l2b, g_up, ub, g_down, db,
    )


def solution(mesh):
    rows, cols = P("batch", "seq", None), P("seq", None)
    one = P("seq")
    placed = (
        rows, P("batch", None), one, one, cols, one, cols, cols, one,
        cols, one, one, one, cols, one, cols, one, rows,
    )
    return jax.shard_map(
        body,
        mesh=mesh,
        in_specs=placed,
        out_specs=(
            rows, rows, one, one, cols, one, cols, cols, one,
            cols, one, one, one, cols, one, cols, one,
        ),
        check_vma=False,
    )
```

```python
import functools
import types

import jax
import jax.numpy as jnp
from jax import lax
from jax.experimental import pallas as pl
from jax.experimental.pallas import tpu as pltpu
from jax.sharding import PartitionSpec as P

BF = jnp.bfloat16
F32 = jnp.float32
MESH = pl.DeviceIdType.MESH
EPSILON = 1e-05
MASKED = -1e30
HIGHEST = lax.Precision.HIGHEST

ROWS = 128
SEG = 512
D = 768
HW = 192
HEADS = 3
HALF = 64
CHUNK = 256
SUMMARY = 50
SLOT = 64
SLOTS = 16
SUMS = SLOTS * SLOT


def dot(a, b, **kw):
    return jnp.dot(a, b, preferred_element_type=F32, **kw)


def dot_nt(a, b):
    return lax.dot_general(a, b, (((1,), (1,)), ((), ())), preferred_element_type=F32)


def dot_tn(a, b):
    return lax.dot_general(a, b, (((0,), (0,)), ((), ())), preferred_element_type=F32)


def iota(shape, dim):
    return lax.broadcasted_iota(jnp.int32, shape, dim)


def norm_stats(values):
    center = values - jnp.mean(values, axis=-1, keepdims=True)
    spread = jnp.mean(center * center, axis=-1, keepdims=True)
    return center, lax.rsqrt(spread + EPSILON)


SCRATCH = dict(
    pk1=((4, 16, D), BF),
    pk2=((4, 16, 2 * D), BF),
    p01=((4, 16, D), BF),
    p02=((4, 16, 2 * D), BF),
    w1=((4, 4, 48, D), BF),
    w2=((4, 4, 48, 2 * D), BF),
    wosl=((4, D // 2, 2 * HW), BF),
    wof=((D, D), BF),
    vin=((16, 128), F32),
    vb=((16, D), BF),
    vg=((3, 16, D), BF),
    vs1=((16, D), BF),
    vx=((3, 16, D), BF),
    vs2=((16, D), BF),
    vz=((3, 16, D), BF),
    vecs=((16, D), F32),
    toka=((SEG, D), BF),
    doa=((SEG, D), BF),
    nrm=((SEG, D), BF),
    nrmt=((D, SEG), BF),
    dot_=((D, SEG), BF),
    stat=((SEG, 128), F32),
    bias=((SEG, SEG), F32),
    q=((SEG, HW), BF),
    kv=((2, SEG, HW), BF),
    kvl=((SEG, 2 * HW), BF),
    kvs=((SUMS, 2 * HW), BF),
    ks=((SUMS, HW), BF),
    vs=((SUMS, HW), BF),
    ssrc=((SLOT, 2 * HW), BF),
    big=((SEG, HEADS * SEG), F32),
    ssum=((HEADS, CHUNK, SUMS), F32),
    prob1=((HEADS, SEG, SEG), BF),
    prob2=((HEADS, SEG, SUMS), BF),
    m1=((SEG, 128), F32),
    l1=((SEG, 128), F32),
    m2=((SEG, 128), F32),
    l2=((SEG, 128), F32),
    a1=((SEG, 128), F32),
    a2=((SEG, 128), F32),
    a1x=((SEG, HW), F32),
    a2x=((SEG, HW), F32),
    o1=((SEG, HW), F32),
    att=((SEG, HW), F32),
    attp=((4, 2, ROWS, 2 * HW), BF),
    atta=((4, SEG, HW), BF),
    hid=((SEG, D), F32),
    nm=((SEG, D), BF),
    nmt=((D, SEG), BF),
    act=((SEG, D), BF),
    gp=((SEG, D), BF),
    rm_s=((SEG, D), BF),
    rm_1=((2, 2, HALF, D), BF),
    rm_x=((2, HALF, D), BF),
    rm_2=((2, HALF, D), BF),
    ro_s=((SEG, D), BF),
    ro_1=((2, 2, HALF, D), BF),
    ro_x=((2, HALF, D), BF),
    ro_2=((2, HALF, D), BF),
    rn_s=((SEG, D), BF),
    rn_1=((2, 2, HALF, D), BF),
    rn_x=((2, HALF, D), BF),
    rn_2=((2, HALF, D), BF),
    gh=((ROWS, D), F32),
    gbr=((ROWS, D), BF),
    sa=((2, 4, HALF, HW), BF),
    sb=((2, 4, HALF, HW), BF),
    do=((2, 4, HALF, HW), BF),
    gba=((2, 4, HALF, HW), BF),
    ds=((HEADS, SEG, SUMS), BF),
    dkvs=((SUMS, 2 * HW), BF),
    sumg=((SLOTS, SLOT, 2 * HW), BF),
    dqkv=((SEG, 3 * HW), BF),
    g1=((4, 4, 48, D), BF),
    g2=((4, 4, 48, 2 * D), BF),
    rza1=((3, 4, 48, D // 2), BF),
    rxa1=((3, 48, D // 2), BF),
    rxb1=((3, 4, 48, D // 2), BF),
    rzb1=((3, 48, D // 2), BF),
    ha1=((4, 48, D // 2), BF),
    hb1=((4, 48, D // 2), BF),
    r1a=((2, 2, 48, D), BF),
    s2a=((2, 2, 48, D), BF),
    r2a=((2, 4, 48, D), BF),
    r1b=((2, 2, 48, D), BF),
    s2b=((2, 2, 48, D), BF),
    r2b=((2, 4, 48, D), BF),
    rxa2=((3, 48, D), BF),
    rzb2=((3, 48, D), BF),
    ha2=((4, 48, D), BF),
    hb2=((4, 48, D), BF),
    fx1=((4, 16, D), BF),
    fx2=((4, 16, 2 * D), BF),
    fin1=((8, 16, D), BF),
    fin2=((8, 16, 2 * D), BF),
    vgr=((16, D), F32),
    vgx=((3, 16, D), F32),
    vgs=((16, D), F32),
    vgz=((3, 16, D), F32),
    sel=((D, 384), BF),
    vgt=((16, 256), F32),
    vfin=((8, 16, 256), F32),
)
SENDS = 24
RECVS = 72


class Flight:
    def __init__(self, waiter):
        self.waiter = waiter
        self.arrived = False
        self.left = False

    def wait_recv(self):
        if not self.arrived:
            self.waiter.wait_recv()
        self.arrived = True

    def wait_send(self):
        if not self.left:
            self.waiter.wait_send()
        self.left = True


def layer_kernel(
    seg_ref, tok, dout, wq, wk, wv, wo, wu, wd, *refs,
):
    vectors, refs = refs[:9], refs[9:]
    out_o, gtok_o, gq_o, gk_o, gv_o, go_o, gu_o, gd_o, gvec_o = refs[:9]
    scratch = refs[9:]
    m = types.SimpleNamespace(**dict(zip(SCRATCH, scratch[:-4])))
    ss, rs, far_ss, far_rs = scratch[-4:]
    batch = lax.axis_index("batch")
    place = lax.axis_index("seq")
    s = place // 4
    t = place % 4
    z = s // 4
    x = s % 4
    sib = t + 1 - 2 * (t % 2)
    over = (t + 2) % 4
    diag = 3 - t
    group = (over, diag, sib)

    def dev(seg, tt, bb):
        return (4 * seg + tt, bb)

    def here(tt):
        return dev(s, tt, batch)

    def along_x(k):
        return dev(4 * z + (x + k) % 4, t, batch)

    def along_z(k):
        return dev(4 * ((z + k) % 4) + x, t, batch)

    used = [0]
    sent = []

    def take(n=1):
        first = used[0]
        used[0] += n
        return first

    def fly(copies, total=None):
        k = len(sent)
        if k >= SENDS:
            sent[k - SENDS].wait_send()
        send_sem, recv_sem = ss.at[k % SENDS], rs.at[take()]
        for src, dst, device in copies:
            copy = pltpu.make_async_remote_copy(
                src_ref=src, dst_ref=dst, send_sem=send_sem, recv_sem=recv_sem,
                device_id=device, device_id_type=MESH,
            )
            copy.start()
        if total is not None:
            copy = pltpu.make_async_remote_copy(
                src_ref=total, dst_ref=total, send_sem=send_sem, recv_sem=recv_sem,
                device_id=device, device_id_type=MESH,
            )
        flight = Flight(copy)
        sent.append(flight)
        return flight

    def far_copy(which, src, dst, seg):
        return pltpu.make_async_remote_copy(
            src_ref=src, dst_ref=dst, send_sem=far_ss.at[which], recv_sem=far_rs.at[which],
            device_id=dev(seg, t, batch), device_id_type=MESH,
        )

    def slot_of(ref, seg):
        return ref.at[pl.ds(pl.multiple_of(SLOT * seg, SLOT), SLOT)]

    def far_wait(which, count, received):
        for n in range(1, 16):
            @pl.when(count == n)
            def _(n=n):
                part = m.kvs.at[0:SLOT * n]
                if received:
                    far_copy(which, part, part, s).wait_recv()
                else:
                    far_copy(which, part, part, s).wait_send()

    def block(c, k):
        return pl.ds(pl.multiple_of(CHUNK * c + HALF * k, HALF), HALF)

    def within(rows, c):
        return pl.ds(pl.multiple_of(rows.start - CHUNK * c, rows.size), rows.size)

    def loop(first, count, size, fn, unroll=4):
        def step(j, carry):
            fn(pl.ds(pl.multiple_of(first + j * size, size), size))
            return carry

        lax.fori_loop(0, count, step, 0, unroll=unroll)

    m.kvs[...] = jnp.zeros((SUMS, 2 * HW), BF)
    m.sumg[...] = jnp.zeros((SLOTS, SLOT, 2 * HW), BF)
    barrier = pltpu.get_barrier_semaphore()
    partners = [here(u) for u in group]
    partners += [dev((s + k) % 16, t, batch) for k in range(1, 16)]
    partners += [dev(s, u, 1 - batch) for u in (t, sib, over, diag)]
    for partner in partners:
        pl.semaphore_signal(barrier, inc=1, device_id=partner, device_id_type=MESH)
    m.pk1[...] = jnp.zeros((4, 16, D), BF)
    for u in range(4):
        cols = slice(HW * u, HW * u + HW)
        m.pk1[u, 0:12, :] = jnp.concatenate(
            [wk[:, cols], wv[:, cols], wq[:, cols], wo[:, cols]], axis=1
        )
    m.vin[...] = jnp.zeros((16, 128), F32)
    for k, ref in enumerate(vectors[:8]):
        m.vin[k:k + 1, 0:12] = ref[...].astype(F32)
    m.vin[8:9, 0:48] = vectors[8][...].astype(F32)
    shift = iota((128, D), 1) - iota((128, D), 0)
    narrow = dot(m.vin[...].astype(BF), (shift == 12 * place).astype(BF))
    wider = dot(m.vin[...].astype(BF), (shift == 48 * (place % 16)).astype(BF))
    vec_row = iota((16, D), 0)
    m.vb[...] = jnp.where(
        vec_row < 8, narrow, jnp.where(vec_row == 8 + z, wider[8:9, :], 0.0)
    ).astype(BF)
    pl.semaphore_wait(barrier, len(partners))

    first1 = fly([(m.pk1.at[u], m.p01.at[t], here(u)) for u in group], m.p01.at[0:3])
    firstv = fly(
        [(m.vb, m.vg.at[k], here(u)) for k, u in enumerate((sib, over, diag))], m.vg
    )
    m.p01[t] = m.pk1[t]
    m.pk2[...] = jnp.zeros((4, 16, 2 * D), BF)
    for u in range(4):
        wide = slice(D * u, D * u + D)
        m.pk2[u, 0:12, 0:D] = wu[:, wide]
        m.pk2[u, 0:12, D:] = wd[:, wide]
    m.p02[t] = m.pk2[t]
    for c in range(2):
        m.toka[block(c, t), :] = tok[HALF * c:HALF * c + HALF, :]
        m.doa[block(c, t), :] = dout[HALF * c:HALF * c + HALF, :]

    def gather_start(ref):
        moves = [
            fly([(ref.at[block(c, t)], ref.at[block(c, t)], here(u)) for c in (0, 1)],
                ref.at[0:ROWS])
            for u in (over, sib)
        ]
        return moves

    def gather_pass(moves, ref):
        moves[0].wait_recv()
        moves.append(
            fly([(ref.at[block(c, over)], ref.at[block(c, over)], here(sib)) for c in (0, 1)],
                ref.at[0:ROWS])
        )

    def finish(moves):
        for move in moves:
            move.wait_recv()

    row48 = iota((48, 64), 0)
    owner48 = (
        (row48 >= 12).astype(jnp.int32)
        + (row48 >= 24).astype(jnp.int32)
        + (row48 >= 36).astype(jnp.int32)
    )
    squeeze = (iota((48, 64), 1) == row48 + 4 * owner48).astype(BF)

    def spread_start(w, a, b):
        mine_a, mine_b = w.at[z, x, :, a], w.at[z, x, :, b]
        return (
            fly([(mine_a, mine_a, along_x(k)) for k in (1, 3, 2)], w.at[0, 0:3, :, a]),
            fly([(mine_b, mine_b, along_z(k)) for k in (1, 3, 2)], w.at[0, 0:3, :, b]),
        )

    def pass_a(w, a, moves):
        plane_a = w.at[z, :, :, a]
        moves[0].wait_recv()
        return fly([(plane_a, plane_a, along_z(k)) for k in (1, 3, 2)], w.at[0:3, :, :, a])

    def pass_b(w, b, moves):
        plane_b = w.at[:, x, :, b]
        moves[1].wait_recv()
        return fly([(plane_b, plane_b, along_x(k)) for k in (1, 3, 2)], w.at[0:3, :, :, b])

    def spread_pass(w, a, b, moves):
        return pass_a(w, a, moves), pass_b(w, b, moves)

    kv_cols = pl.ds(0, 256), pl.ds(256, 128)
    qo_cols = pl.ds(384, 128), pl.ds(512, 256)
    up_down = pl.ds(0, D), pl.ds(D, D)
    halves = pl.ds(0, D // 2), pl.ds(D // 2, D // 2)

    first1.wait_recv()
    m.w1[z, x] = dot(squeeze, m.p01[...].reshape(64, D)).astype(BF)
    phase1 = spread_start(m.w1, *kv_cols)
    phase1b = spread_start(m.w1, *qo_cols)
    first2 = fly([(m.pk2.at[u], m.p02.at[t], here(u)) for u in group], m.p02.at[0:3])
    ag_tok = gather_start(m.toka)

    seg_len = seg_ref[0, s]

    def token_of(rows):
        return rows + 64 * ((rows % CHUNK) // HALF) - 192 * (rows // CHUNK)

    k_pos = token_of(iota((1, SEG), 1))

    def mask(rows):
        mine = token_of(rows.start + iota((ROWS, 1), 0))
        ok = ((k_pos <= mine) & (k_pos < seg_len)) | (k_pos == mine)
        m.bias[rows, :] = jnp.where(ok, 0.0, MASKED)

    loop(0, 4, ROWS, mask)
    s_col = iota((8, SUMS), 1)
    sum_bias = jnp.where((s_col < SLOT * s) & (s_col % SLOT < SUMMARY), 0.0, MASKED)[0:1, :]
    pick_row = iota((SLOT, SEG), 0)
    pick = ((k_pos == seg_len - SUMMARY + pick_row) & (pick_row < SUMMARY)).astype(BF)
    lane_head = iota((1, HW), 1) // 64

    def of_head(value, h):
        return jnp.where(lane_head == h, value, jnp.zeros_like(value))

    def by_head(cols):
        return jnp.where(
            lane_head == 0, cols[:, 0:1], jnp.where(lane_head == 1, cols[:, 1:2], cols[:, 2:3])
        )

    def add4(own, got):
        return own.astype(F32) + got[0].astype(F32) + got[1].astype(F32) + got[2].astype(F32)

    def moved_by(rows, one_hot):
        high = rows.astype(BF)
        rest = rows - high.astype(F32)
        mid = rest.astype(BF)
        low = (rest - mid.astype(F32)).astype(BF)
        pieces = dot(jnp.concatenate([high, mid, low], axis=0), one_hot)
        return pieces[0:16, :] + pieces[16:32, :] + pieces[32:48, :]

    feature, lane = iota((D, 128), 0), iota((D, 128), 1)
    m.sel[:, 0:128] = ((feature - lane == 48 * s) & (lane < 48)).astype(BF)
    feature, lane = iota((D, 256), 0), iota((D, 256), 1)
    m.sel[:, 128:384] = ((feature - lane == 192 * x) & (lane < 192)).astype(BF)

    firstv.wait_recv()
    m.vs1[...] = add4(m.vb[...], m.vg).astype(BF)
    vx = fly([(m.vs1, m.vx.at[k - 1], along_x(k)) for k in (1, 2, 3)], m.vx)
    ends1 = spread_pass(m.w1, *kv_cols, phase1)
    ends1b = spread_pass(m.w1, *qo_cols, phase1b)
    vx.wait_recv()
    m.vs2[...] = add4(m.vs1[...], m.vx).astype(BF)
    vz = fly([(m.vs2, m.vz.at[k - 1], along_z(k)) for k in (1, 2, 3)], m.vz)
    first2.wait_recv()
    m.w2[z, x] = dot(squeeze, m.p02[...].reshape(64, 2 * D)).astype(BF)
    phase2 = spread_start(m.w2, *up_down)
    gather_pass(ag_tok, m.toka)
    ag_do = gather_start(m.doa)
    vz.wait_recv()
    m.vecs[...] = add4(m.vs2[...], m.vz)
    gain1, shift1 = m.vecs[0:1, :], m.vecs[1:2, :]
    gain2, shift2 = m.vecs[5:6, :], m.vecs[6:7, :]
    o_bias, down_bias = m.vecs[4:5, :], m.vecs[7:8, :]

    def my_cols(row):
        whole = m.vecs[row:row + 1, :]
        value = whole[:, 0:HW]
        for u in range(1, 4):
            value = jnp.where(t == u, whole[:, HW * u:HW * u + HW], value)
        return value

    q_bias, v_bias = my_cols(2), my_cols(3)
    up_bias = m.vecs[8:9, :]
    for u in range(1, 4):
        up_bias = jnp.where(t == u, m.vecs[8 + u:9 + u, :], up_bias)

    finish(ag_tok)

    def norm1(rows):
        values = m.toka[rows, :].astype(F32)
        mean = jnp.mean(values, axis=-1, keepdims=True)
        center = values - mean
        scale = lax.rsqrt(jnp.mean(center * center, axis=-1, keepdims=True) + EPSILON)
        m.nrm[rows, :] = (center * scale * gain1 + shift1).astype(BF)
        m.stat[rows, 0:1] = mean
        m.stat[rows, 1:2] = scale

    loop(0, 4, ROWS, norm1)
    m.nrmt[...] = m.nrm[...].T

    finish(ends1)
    kv_bias = jnp.concatenate([jnp.zeros((1, HW), F32), v_bias], axis=1)
    m.kvl[...] = (dot(m.nrm[...], m.w1[:, :, :, 0:2 * HW].reshape(D, 2 * HW)) + kv_bias).astype(BF)

    m.ssrc[...] = dot(pick, m.kvl[...]).astype(BF)
    for k in range(1, 16):
        @pl.when(s + k < 16)
        def _(k=k):
            far_copy(0, m.ssrc, slot_of(m.kvs, s), (s + k) % 16).start()
    ends2b = pass_b(m.w2, up_down[1], phase2)
    finish(ends1b)
    m.q[...] = (
        (dot(m.nrm[...], m.w1[:, :, :, 2 * HW:3 * HW].reshape(D, HW)) + q_bias) * 0.125
    ).astype(BF)
    w_o = m.w1[...].reshape(D, D)[:, 3 * HW:]
    m.wosl[t] = jnp.concatenate([w_o[0:D // 2, :], w_o[D // 2:, :]], axis=1)
    m.kv[0] = m.kvl[:, 0:HW]
    m.kv[1] = m.kvl[:, HW:]
    ag_wo = [fly([(m.wosl.at[t], m.wosl.at[t], here(u))]) for u in (over, sib)]

    for h in range(HEADS):
        m.big[:, SEG * h:SEG * h + SEG] = dot_nt(of_head(m.q[...], h), m.kv[0]) + m.bias[...]
    for h in range(HEADS):
        def soften1(rows, h=h):
            score = m.big[rows, SEG * h:SEG * h + SEG]
            peak = jnp.max(score, axis=-1, keepdims=True)
            power = jnp.exp(score - peak)
            m.prob1[h, rows, :] = power.astype(BF)
            m.m1[rows, h:h + 1] = peak
            m.l1[rows, h:h + 1] = jnp.sum(power, axis=-1, keepdims=True)

        loop(0, 4, ROWS, soften1)
        part = dot(m.prob1[h], of_head(m.kv[1], h))
        m.o1[...] = part if h == 0 else m.o1[...] + part
    gather_pass(ag_do, m.doa)

    far_wait(0, s, True)
    ends2a = pass_a(m.w2, up_down[0], phase2)
    ends2 = (ends2a, ends2b)
    m.ks[...] = m.kvs[:, 0:HW]
    m.vs[...] = m.kvs[:, HW:]

    ag_att = []

    def attend(c):
        rows_c = slice(CHUNK * c, CHUNK * c + CHUNK)
        part = None
        for h in range(HEADS):
            m.ssum[h] = dot_nt(of_head(m.q[rows_c, :], h), m.ks[...]) + sum_bias

            def soften2(rows, h=h):
                score = m.ssum[h, within(rows, c), :]
                peak = jnp.max(score, axis=-1, keepdims=True)
                power = jnp.exp(score - peak)
                m.prob2[h, rows, :] = power.astype(BF)
                m.m2[rows, h:h + 1] = peak
                m.l2[rows, h:h + 1] = jnp.sum(power, axis=-1, keepdims=True)

            loop(CHUNK * c, 2, ROWS, soften2)
            more = dot(m.prob2[h, rows_c, :], of_head(m.vs[...], h))
            part = more if h == 0 else part + more
        m1, m2 = m.m1[rows_c, 0:HEADS], m.m2[rows_c, 0:HEADS]
        peak = jnp.maximum(m1, m2)
        e1, e2 = jnp.exp(m1 - peak), jnp.exp(m2 - peak)
        share = 1.0 / (m.l1[rows_c, 0:HEADS] * e1 + m.l2[rows_c, 0:HEADS] * e2)
        a1, a2 = e1 * share, e2 * share
        m.a1[rows_c, 0:HEADS] = a1
        m.a2[rows_c, 0:HEADS] = a2
        a1x, a2x = by_head(a1), by_head(a2)
        m.a1x[rows_c, :] = a1x
        m.a2x[rows_c, :] = a2x
        attended = m.o1[rows_c, :] * a1x + part * a2x
        m.att[rows_c, :] = attended
        low = attended.astype(BF)
        m.attp[t, c] = jnp.concatenate([low[0:ROWS, :], low[ROWS:, :]], axis=1)
        mine_c = m.attp.at[t, c]
        ag_att.append([fly([(mine_c, mine_c, here(u))]) for u in (over, sib)])

    attend(0)
    ag_wo[0].wait_recv()
    ag_wo.append(fly([(m.wosl.at[over], m.wosl.at[over], here(sib))]))
    attend(1)
    finish(ag_wo)
    m.wof[0:D // 2, :] = jnp.concatenate([m.wosl[u, :, 0:HW] for u in range(4)], axis=1)
    m.wof[D // 2:, :] = jnp.concatenate([m.wosl[u, :, HW:] for u in range(4)], axis=1)

    def att_pass(c):
        ag_att[c][0].wait_recv()
        theirs = m.attp.at[over, c]
        ag_att[c].append(fly([(theirs, theirs, here(sib))]))

    def scatter_start(name, cs):
        src, r1 = getattr(m, name + "_s"), getattr(m, name + "_1")
        return [
            fly([(src.at[block(c, k)], r1.at[c, i], here(sib)) for c in cs],
                r1.at[0:len(cs), i])
            for i, k in ((1, diag), (0, sib))
        ]

    def scatter_pass(name, cs, moves):
        src, r1 = getattr(m, name + "_s"), getattr(m, name + "_1")
        cross, r2 = getattr(m, name + "_x"), getattr(m, name + "_2")
        moves[0].wait_recv()
        for c in cs:
            cross[c] = (src[block(c, over), :].astype(F32) + r1[c, 1].astype(F32)).astype(BF)
        moves.append(
            fly([(cross.at[c], r2.at[c], here(over)) for c in cs], r2.at[0:len(cs)])
        )

    def scatter_end(name, c, moves):
        src, r1 = getattr(m, name + "_s"), getattr(m, name + "_1")
        r2 = getattr(m, name + "_2")
        moves[1].wait_recv()
        moves[2].wait_recv()
        return src[block(c, t), :].astype(F32) + r1[c, 0].astype(F32) + r2[c].astype(F32)

    def gelu(rows):
        a = m.big[rows, 0:D]
        square = a * a
        bend = jnp.tanh(0.7978845608028654 * (a + 0.044715 * (square * a)))
        half = 0.5 * (1.0 + bend)
        m.act[rows, :] = (a * half).astype(BF)
        slope = half + (0.5 * a) * (1.0 - bend * bend) * (
            0.7978845608028654 * (1.0 + 0.134145 * square)
        )
        m.gp[rows, :] = (m.big[rows, D:] * slope).astype(BF)

    def norm2(rows):
        center, scale = norm_stats(m.hid[rows, :])
        m.nm[rows, :] = (center * scale * gain2 + shift2).astype(BF)

    def project(c):
        rows_c = slice(CHUNK * c, CHUNK * c + CHUNK)
        finish(ag_att[c])
        for u in range(4):
            m.atta[u, CHUNK * c:CHUNK * c + ROWS, :] = m.attp[u, c, :, 0:HW]
            m.atta[u, CHUNK * c + ROWS:CHUNK * c + CHUNK, :] = m.attp[u, c, :, HW:]
        branch = dot(m.atta[0, rows_c, :], m.wof[0:HW, :])
        for u in range(1, 4):
            branch = branch + dot(m.atta[u, rows_c, :], m.wof[HW * u:HW * u + HW, :])
        m.hid[rows_c, :] = m.toka[rows_c, :].astype(F32) + branch + o_bias
        loop(CHUNK * c, 2, ROWS, norm2)

    def feed(c):
        rows_c = slice(CHUNK * c, CHUNK * c + CHUNK)
        m.big[rows_c, 0:D] = dot(m.nm[rows_c, :], m.w2[:, :, :, 0:D].reshape(D, D)) + up_bias
        m.big[rows_c, D:] = dot(m.doa[rows_c, :], m.w2[:, :, :, D:].reshape(D, D))
        loop(CHUNK * c, 4, 64, gelu)
        m.rm_s[rows_c, :] = dot_nt(m.gp[rows_c, :], m.w2[:, :, :, 0:D].reshape(D, D)).astype(BF)
        return scatter_start("rm", (c,))

    att_pass(0)
    project(0)
    att_pass(1)
    finish(ag_do)
    finish(ends2)
    rm0 = feed(0)
    project(1)
    scatter_pass("rm", (0,), rm0)
    rm1 = feed(1)

    m.dot_[...] = m.doa[...].T
    m.nmt[...] = m.nm[...].T
    scatter_pass("rm", (1,), rm1)
    m.g2[:, :, :, 0:D] = dot(m.nmt[...], m.gp[...]).astype(BF).reshape(4, 4, 48, D)
    m.g2[:, :, :, D:] = dot(m.dot_[...], m.act[...]).astype(BF).reshape(4, 4, 48, D)

    def reduce_start(g, tag, a, b, at_a, at_b):
        rza, rxb = getattr(m, "rza" + tag), getattr(m, "rxb" + tag)
        return (
            fly([(g.at[(z + k) % 4, :, :, a], rza.at[k - 1, :, :, at_a], along_z(k))
                 for k in (1, 3, 2)], rza.at[:, :, :, at_a]),
            fly([(g.at[:, (x + k) % 4, :, b], rxb.at[k - 1, :, :, at_b], along_x(k))
                 for k in (1, 3, 2)], rxb.at[:, :, :, at_b]),
        )

    def reduce_pass(g, tag, pieces):
        rza, rxb = getattr(m, "rza" + tag), getattr(m, "rxb" + tag)
        rxa, rzb = getattr(m, "rxa" + tag), getattr(m, "rzb" + tag)
        ha, hb = getattr(m, "ha" + tag), getattr(m, "hb" + tag)
        for (a, b, at_a, at_b), moves in pieces:
            into = slice(at_a.start, at_a.start + at_a.size)
            moves[0].wait_recv()
            for k in range(4):
                ha[k, :, into] = add4(
                    g[z, k, :, a.start:a.start + a.size], [rza[j, k, :, into] for j in range(3)]
                ).astype(BF)
        a2 = fly([(ha.at[(x + k) % 4], rxa.at[k - 1], along_x(k)) for k in (1, 3, 2)], rxa)
        for (a, b, at_a, at_b), moves in pieces:
            into = slice(at_b.start, at_b.start + at_b.size)
            moves[1].wait_recv()
            for k in range(4):
                hb[k, :, into] = add4(
                    g[k, x, :, b.start:b.start + b.size], [rxb[j, k, :, into] for j in range(3)]
                ).astype(BF)
        b2 = fly([(hb.at[(z + k) % 4], rzb.at[k - 1], along_z(k)) for k in (1, 3, 2)], rzb)
        return a2, b2

    row64 = iota((64, 48), 0)
    expand = (
        (iota((64, 48), 1) == row64 - 4 * (row64 // 16)) & (row64 % 16 < 12)
    ).astype(BF)
    mine = 4 * batch + t
    everyone = [(u, dev(s, u, 1 - batch)) for u in (over, diag, sib, t)]
    everyone += [(u, here(u)) for u in group]

    def reduce_last(tag, half, moves):
        rxa, rzb = getattr(m, "rxa" + tag), getattr(m, "rzb" + tag)
        ha, hb = getattr(m, "ha" + tag), getattr(m, "hb" + tag)
        fx, fin = getattr(m, "fx" + tag), getattr(m, "fin" + tag)
        finish(moves)
        a = add4(ha[x], [rxa[j] for j in range(3)]).astype(BF)
        b = add4(hb[z], [rzb[j] for j in range(3)]).astype(BF)
        fx[:, :, 0:half] = dot(expand, a).astype(BF).reshape(4, 16, half)
        fx[:, :, half:] = dot(expand, b).astype(BF).reshape(4, 16, half)
        moves = fly([(fx.at[u], fin.at[mine], device) for u, device in everyone], fin.at[0:7])
        fin[mine] = fx[t]
        return moves


    up_c, down_c = up_down
    lo, hi = pl.ds(0, 2), pl.ds(2, 2)
    z1, z2, z3 = (z + 1) % 4, (z + 2) % 4, (z + 3) % 4
    x1, x2, x3 = (x + 1) % 4, (x + 2) % 4, (x + 3) % 4
    relay_a = fly(
        [(m.g2.at[z2, lo, :, up_c], m.r1a.at[0], along_z(1)),
         (m.g2.at[z2, hi, :, up_c], m.r1a.at[1], along_z(3))], m.r1a
    )
    relay_b = fly(
        [(m.g2.at[lo, x2, :, down_c], m.r1b.at[0], along_x(1)),
         (m.g2.at[hi, x2, :, down_c], m.r1b.at[1], along_x(3))], m.r1b
    )
    plain_a = fly(
        [(m.g2.at[z1, hi, :, up_c], m.r2a.at[0, hi], along_z(1)),
         (m.g2.at[z3, lo, :, up_c], m.r2a.at[1, lo], along_z(3))], m.r1a
    )
    plain_b = fly(
        [(m.g2.at[hi, x1, :, down_c], m.r2b.at[0, hi], along_x(1)),
         (m.g2.at[lo, x3, :, down_c], m.r2b.at[1, lo], along_x(3))], m.r1b
    )

    def relay():
        relay_a.wait_recv()
        m.s2a[0] = (m.g2[z1, 0:2, :, 0:D].astype(F32) + m.r1a[0].astype(F32)).astype(BF)
        m.s2a[1] = (m.g2[z3, 2:4, :, 0:D].astype(F32) + m.r1a[1].astype(F32)).astype(BF)
        a = fly(
            [(m.s2a.at[0], m.r2a.at[0, lo], along_z(1)),
             (m.s2a.at[1], m.r2a.at[1, hi], along_z(3))], m.r1a
        )
        relay_b.wait_recv()
        m.s2b[0] = (m.g2[0:2, x1, :, D:].astype(F32) + m.r1b[0].astype(F32)).astype(BF)
        m.s2b[1] = (m.g2[2:4, x3, :, D:].astype(F32) + m.r1b[1].astype(F32)).astype(BF)
        b = fly(
            [(m.s2b.at[0], m.r2b.at[0, lo], along_x(1)),
             (m.s2b.at[1], m.r2b.at[1, hi], along_x(3))], m.r1b
        )
        return a, b

    def relayed(moves):
        plain_a.wait_recv()
        moves[0].wait_recv()
        for k in range(4):
            m.ha2[k] = (
                m.g2[z, k, :, 0:D].astype(F32) + m.r2a[0, k].astype(F32) + m.r2a[1, k].astype(F32)
            ).astype(BF)
        a2 = fly([(m.ha2.at[(x + k) % 4], m.rxa2.at[k - 1], along_x(k)) for k in (1, 3, 2)], m.rxa2)
        plain_b.wait_recv()
        moves[1].wait_recv()
        for k in range(4):
            m.hb2[k] = (
                m.g2[k, x, :, D:].astype(F32) + m.r2b[0, k].astype(F32) + m.r2b[1, k].astype(F32)
            ).astype(BF)
        b2 = fly([(m.hb2.at[(z + k) % 4], m.rzb2.at[k - 1], along_z(k)) for k in (1, 3, 2)], m.rzb2)
        return a2, b2


    zero_row = jnp.zeros((1, D), F32)
    ones = jnp.ones((8, SEG), BF)

    def col_sums(value):
        return dot(ones[:, 0:value.shape[0]], value)[0:1, :]

    def norm_back(values, grads, gain):
        center, scale = norm_stats(values)
        unit = center * scale
        inner = grads * gain
        return unit, scale * (
            inner
            - jnp.mean(inner, axis=-1, keepdims=True)
            - unit * jnp.mean(inner * unit, axis=-1, keepdims=True)
        )

    g_gain2, g_shift2 = zero_row, zero_row
    aa = []
    for c in range(2):
        at = slice(HALF * c, HALF * c + HALF)
        grads = scatter_end("rm", c, rm0 if c == 0 else rm1)
        unit, into = norm_back(m.hid[block(c, t), :], grads, gain2)
        into = into + dout[at, :].astype(F32)
        m.gh[at, :] = into
        low = into.astype(BF)
        m.gbr[at, :] = low
        for u in range(4):
            m.sa[c, u] = dot_nt(low, m.wof[HW * u:HW * u + HW, :]).astype(BF)
        aa.append(
            fly([(m.sa.at[c, u], m.do.at[c, t], here(u)) for u in group], m.do.at[c, 0:3])
        )
        m.do[c, t] = m.sa[c, t]
        g_gain2 += jnp.sum(grads * unit, axis=0, keepdims=True)
        g_shift2 += jnp.sum(grads, axis=0, keepdims=True)
    m.ro_s[...] = dot_nt(m.act[...], m.w2[:, :, :, D:].reshape(D, D)).astype(BF)
    for u in range(4):
        cols = m.gbr[:, HW * u:HW * u + HW]
        m.sb[0, u] = cols[0:HALF, :]
        m.sb[1, u] = cols[HALF:, :]
    qt = m.q[...].T
    m.o1[...] = jnp.zeros((SEG, HW), F32)

    ab = fly(
        [(m.sb.at[c, u], m.gba.at[c, t], here(u)) for u in group for c in (0, 1)],
        m.gba.at[:, 0:3],
    )
    m.gba[0, t] = m.sb[0, t]
    m.gba[1, t] = m.sb[1, t]
    ro = scatter_start("ro", (0, 1))
    for c in range(2):
        rows_c = slice(CHUNK * c, CHUNK * c + CHUNK)
        aa[c].wait_recv()
        do_c = m.do[c].reshape(CHUNK, HW)
        weighed = do_c.astype(F32) * m.att[rows_c, :]
        for h in range(HEADS):
            m.m1[rows_c, h:h + 1] = jnp.sum(of_head(weighed, h), axis=-1, keepdims=True)
        for h in range(HEADS):
            m.ssum[h] = dot_nt(of_head(do_c, h), m.vs[...])

            def back_sum(rows, h=h, c=c):
                slope = (m.ssum[h, within(rows, c), :] - m.m1[rows, h:h + 1]) * m.a2[rows, h:h + 1]
                m.ds[h, rows, :] = (m.prob2[h, rows, :].astype(F32) * slope).astype(BF)

            loop(CHUNK * c, 2, ROWS, back_sum)
        if c == 0:
            rg2 = relay()
    do_all = m.do[...].reshape(SEG, HW)
    do_wide = do_all.astype(F32)
    dot1 = (do_wide * m.a1x[...]).astype(BF).T
    dot2 = (do_wide * m.a2x[...]).astype(BF).T
    for h in range(HEADS):
        feat, feat_v = slice(64 * h, 64 * h + 64), slice(HW + 64 * h, HW + 64 * h + 64)
        m.big[feat, 0:SUMS] = dot(qt[feat, :], m.ds[h])
        m.big[feat_v, 0:SUMS] = dot(dot2[feat, :], m.prob2[h])
    m.dkvs[...] = m.big[0:2 * HW, 0:SUMS].T.astype(BF)
    for k in range(1, 16):
        @pl.when(s >= k)
        def _(k=k):
            seg = (s + 16 - k) % 16
            far_copy(1, slot_of(m.dkvs, seg), m.sumg.at[k], seg).start()
    ends_g2 = relayed(rg2)
    scatter_pass("ro", (0, 1), ro)

    for h in range(HEADS):
        m.o1[...] += dot(m.ds[h], of_head(m.ks[...], h))
    for h in range(HEADS):
        m.big[:, SEG * h:SEG * h + SEG] = dot_nt(of_head(do_all, h), m.kv[1])
    for h in range(HEADS):
        def back_own(rows, h=h):
            weight = m.prob1[h, rows, :].astype(F32)
            slope = (m.big[rows, SEG * h:SEG * h + SEG] - m.m1[rows, h:h + 1]) * m.a1[rows, h:h + 1]
            m.ds[h, rows, 0:SEG] = (weight * slope).astype(BF)

        loop(0, 4, ROWS, back_own)
        score_grads = m.ds[h, :, 0:SEG]
        m.o1[...] += dot(score_grads, of_head(m.kv[0], h))
        feat, feat_v = slice(64 * h, 64 * h + 64), slice(HW + 64 * h, HW + 64 * h + 64)
        m.bias[feat, :] = dot(qt[feat, :], score_grads)
        m.bias[feat_v, :] = dot(dot1[feat, :], m.prob1[h])
    for u in range(4):
        m.nmt[HW * u:HW * u + HW, :] = m.atta[u].T
    ab.wait_recv()
    g_o = dot(m.nmt[...], m.gba[...].reshape(SEG, HW))
    dq = m.o1[...].astype(BF) * jnp.asarray(0.125, BF)
    m.g1[:, :, :, 2 * HW:] = (
        jnp.concatenate([dot(m.nrmt[...], dq), g_o], axis=1).astype(BF).reshape(4, 4, 48, 2 * HW)
    )
    cols_qo = qo_cols + (pl.ds(256, 128), pl.ds(128, 256))
    cols_kv = kv_cols + (pl.ds(0, 256), pl.ds(0, 128))
    rg1_qo = reduce_start(m.g1, "1", *cols_qo)

    m.big[:, 0:2 * HW] = m.bias[0:2 * HW, :].T
    pick_t = pick.T

    far_wait(1, 15 - s, True)

    total = m.sumg[0].astype(F32)
    for k in range(1, SLOTS):
        total = total + m.sumg[k].astype(F32)
    high = total.astype(BF)
    rest = (total - high.astype(F32)).astype(BF)
    dkv = (m.big[:, 0:2 * HW] + dot(pick_t, high) + dot(pick_t, rest)).astype(BF)
    m.dqkv[...] = jnp.concatenate([dkv, dq], axis=1)

    m.g1[:, :, :, 0:2 * HW] = dot(m.nrmt[...], dkv).astype(BF).reshape(4, 4, 48, 2 * HW)
    rg1_kv = reduce_start(m.g1, "1", *cols_kv)
    m.rn_s[...] = dot_nt(m.dqkv[...], m.w1[...].reshape(D, D)[:, 0:3 * HW]).astype(BF)
    rn = [scatter_start("rn", (c,)) for c in range(2)]

    def gain_grads(j, carry):
        rows = pl.ds(pl.multiple_of(j * 64, 64), 64)
        grads = m.rn_s[rows, :].astype(F32)
        unit = (m.toka[rows, :].astype(F32) - m.stat[rows, 0:1]) * m.stat[rows, 1:2]
        return (
            carry[0] + jnp.sum((grads * unit).reshape(8, 8, D), axis=0),
            carry[1] + jnp.sum(grads.reshape(8, 8, D), axis=0),
        )

    zero8 = jnp.zeros((8, D), F32)
    g_gain1, g_shift1 = lax.fori_loop(0, 8, gain_grads, (zero8, zero8), unroll=4)
    scatter_pass("rn", (0,), rn[0])
    scatter_pass("rn", (1,), rn[1])
    g_qkvb = col_sums(m.dqkv[...])

    def in_place(row):
        none = jnp.zeros((1, HW), F32)
        return jnp.concatenate([jnp.where(t == u, row, none) for u in range(4)], axis=1)

    rows8 = (
        jnp.sum(g_gain1, axis=0, keepdims=True),
        jnp.sum(g_shift1, axis=0, keepdims=True),
        in_place(g_qkvb[:, 2 * HW:]),
        in_place(g_qkvb[:, HW:2 * HW]),
        col_sums(m.gbr[...]),
        g_gain2,
        g_shift2,
        col_sums(dout[...]),
    )
    m.vgr[...] = jnp.zeros((16, D), F32)
    for k, row in enumerate(rows8):
        m.vgr[k:k + 1, :] = row
    g_ub = col_sums(m.gp[...])
    for u in range(4):
        m.vgr[8 + u:9 + u, :] = jnp.where(t == u, g_ub, zero_row)
    vgx = fly([(m.vgr, m.vgx.at[k - 1], along_x(k)) for k in (1, 2, 3)], m.vgx)
    fin_g2 = reduce_last("2", D, ends_g2)
    for c in range(2):
        out_o[HALF * c:HALF * c + HALF, :] = (
            scatter_end("ro", c, ro) + m.hid[block(c, t), :] + down_bias
        ).astype(BF)
    ends_g1 = reduce_pass(m.g1, "1", [(cols_qo, rg1_qo), (cols_kv, rg1_kv)])
    vgx.wait_recv()
    m.vgs[...] = add4(m.vgr[...], m.vgx)
    vgz = fly([(m.vgs, m.vgz.at[k - 1], along_z(k)) for k in (1, 2, 3)], m.vgz)

    for c in range(2):
        at = slice(HALF * c, HALF * c + HALF)
        grads = scatter_end("rn", c, rn[c])
        _, into = norm_back(tok[at, :].astype(F32), grads, gain1)
        gtok_o[at, :] = into + m.gh[at, :]
    fin_g1 = reduce_last("1", D // 2, ends_g1)
    vgz.wait_recv()
    totals = add4(m.vgs[...], m.vgz)
    moved = moved_by(totals, m.sel[...])
    up_row = jnp.sum(jnp.where(iota((16, 256), 0) == 8 + z, moved[:, 128:384], 0.0), axis=0, keepdims=True)
    m.vgt[...] = jnp.zeros((16, 256), F32)
    m.vgt[0:8, 0:128] = moved[0:8, 0:128]
    m.vgt[8:9, :] = up_row
    fin_v = fly([(m.vgt, m.vfin.at[mine], device) for _, device in everyone], m.vfin.at[0:7])
    m.vfin[mine] = m.vgt[...]

    def both(fin, u, cols):
        return fin[u, 0:12, cols].astype(F32) + fin[4 + u, 0:12, cols].astype(F32)

    fin_g2.wait_recv()
    for u in range(4):
        wide = slice(D * u, D * u + D)
        gu_o[:, wide] = both(m.fin2, u, slice(0, D))
        gd_o[:, wide] = both(m.fin2, u, slice(D, 2 * D))
    fin_v.wait_recv()
    totals = m.vfin[0]
    for k in range(1, 8):
        totals = totals + m.vfin[k]
    source, target = iota((256, 128), 0), iota((256, 128), 1)
    own_12 = ((source - target == 12 * t) & (target < 12)).astype(BF)
    own_48 = ((source - target == 48 * t) & (target < 48)).astype(BF)
    row16 = iota((16, 128), 0)
    gvec_o[...] = jnp.where(row16 < 8, moved_by(totals, own_12), moved_by(totals, own_48))
    fin_g1.wait_recv()
    for u in range(4):
        part = both(m.fin1, u, slice(0, D))
        ordered = jnp.concatenate(
            [part[:, 0:256], part[:, 384:512], part[:, 256:384], part[:, 512:]], axis=1
        )
        for k, ref in enumerate((gk_o, gv_o, gq_o, go_o)):
            ref[:, HW * u:HW * u + HW] = ordered[:, HW * k:HW * k + HW]

    for flight in sent:
        flight.wait_send()
    far_wait(0, 15 - s, False)
    far_wait(1, s, False)
    assert used[0] <= RECVS, used[0]


def hand_out(*refs):
    whole, vec, outs = refs[:8], refs[8], refs[9:]
    for src, dst in zip(whole, outs[:8]):
        dst[...] = src[...]
    for k, dst in enumerate(outs[8:16]):
        dst[...] = vec[k:k + 1, 0:12]
    outs[16][...] = vec[8:9, 0:48]


def body(
    tokens, seg_lengths, ln1_gain, ln1_bias, w_query, q_bias, w_key, w_value, v_bias,
    w_out, o_bias, ln2_gain, ln2_bias, w_up, up_bias, w_down, down_bias, d_out,
):
    vectors = [ln1_gain, ln1_bias, q_bias, v_bias, o_bias, ln2_gain, ln2_bias, down_bias, up_bias]
    shape = jax.ShapeDtypeStruct
    vmem = pl.BlockSpec(memory_space=pltpu.VMEM)
    shapes = [
        shape((ROWS, D), BF),
        shape((ROWS, D), F32),
        shape((12, D), F32),
        shape((12, D), F32),
        shape((12, D), F32),
        shape((12, D), F32),
        shape((12, 4 * D), F32),
        shape((12, 4 * D), F32),
    ]
    outs = pl.pallas_call(
        layer_kernel,
        out_shape=shapes + [shape((16, 128), F32)],
        in_specs=[pl.BlockSpec(memory_space=pltpu.SMEM)] + [vmem] * 17,
        out_specs=[vmem] * 9,
        scratch_shapes=[pltpu.VMEM(dims, kind) for dims, kind in SCRATCH.values()]
        + [pltpu.SemaphoreType.DMA((n,)) for n in (SENDS, RECVS, 2, 2)],
        compiler_params=pltpu.CompilerParams(
            collective_id=0, has_side_effects=True, vmem_limit_bytes=62 * 2**20
        ),
        name="layer",
    )(
        seg_lengths, tokens[0], d_out[0], w_query, w_key, w_value, w_out, w_up, w_down,
        *[v.reshape(1, -1) for v in vectors],
    )
    outs = pl.pallas_call(
        hand_out,
        out_shape=shapes + [shape((1, 12), F32)] * 8 + [shape((1, 48), F32)],
        in_specs=[vmem] * 9,
        out_specs=[vmem] * 17,
        compiler_params=pltpu.CompilerParams(vmem_limit_bytes=62 * 2**20),
        name="hand_out",
    )(*outs)
    out, g_tok, g_q, g_k, g_v, g_o, g_up, g_down = outs[:8]
    l1g, l1b, qb, vb, ob, l2g, l2b, db, ub = [v.reshape(-1) for v in outs[8:]]
    return (
        out[None], g_tok[None], l1g, l1b, g_q, qb, g_k, g_v, vb,
        g_o, ob, l2g, l2b, g_up, ub, g_down, db,
    )


def solution(mesh):
    rows, cols = P("batch", "seq", None), P("seq", None)
    one = P("seq")
    placed = (
        rows, P("batch", None), one, one, cols, one, cols, cols, one,
        cols, one, one, one, cols, one, cols, one, rows,
    )
    return jax.shard_map(
        body,
        mesh=mesh,
        in_specs=placed,
        out_specs=(
            rows, rows, one, one, cols, one, cols, cols, one,
            cols, one, one, one, cols, one, cols, one,
        ),
        check_vma=False,
    )
```

```python
import functools
import types

import jax
import jax.numpy as jnp
from jax import lax
from jax.experimental import pallas as pl
from jax.experimental.pallas import tpu as pltpu
from jax.sharding import PartitionSpec as P

BF = jnp.bfloat16
F32 = jnp.float32
MESH = pl.DeviceIdType.MESH
EPSILON = 1e-05
MASKED = -1e30
HIGHEST = lax.Precision.HIGHEST

ROWS = 128
SEG = 512
D = 768
HW = 192
HEADS = 3
HALF = 64
CHUNK = 256
SUMMARY = 50
SLOT = 64
SLOTS = 16
SUMS = SLOTS * SLOT


def dot(a, b, **kw):
    return jnp.dot(a, b, preferred_element_type=F32, **kw)


def dot_nt(a, b):
    return lax.dot_general(a, b, (((1,), (1,)), ((), ())), preferred_element_type=F32)


def dot_tn(a, b):
    return lax.dot_general(a, b, (((0,), (0,)), ((), ())), preferred_element_type=F32)


def iota(shape, dim):
    return lax.broadcasted_iota(jnp.int32, shape, dim)


def norm_stats(values):
    center = values - jnp.mean(values, axis=-1, keepdims=True)
    spread = jnp.mean(center * center, axis=-1, keepdims=True)
    return center, lax.rsqrt(spread + EPSILON)


SCRATCH = dict(
    pk1=((4, 16, D), BF),
    pk2=((4, 16, 2 * D), BF),
    p01=((4, 16, D), BF),
    p02=((4, 16, 2 * D), BF),
    w1=((4, 4, 48, D), BF),
    w2=((4, 4, 48, 2 * D), BF),
    wosl=((4, D // 2, 2 * HW), BF),
    wof=((D, D), BF),
    vin=((16, 128), F32),
    vb=((16, D), BF),
    vg=((3, 16, D), BF),
    vs1=((16, D), BF),
    vx=((3, 16, D), BF),
    vs2=((16, D), BF),
    vz=((3, 16, D), BF),
    vecs=((16, D), F32),
    toka=((SEG, D), BF),
    doa=((SEG, D), BF),
    nrm=((SEG, D), BF),
    nrmt=((D, SEG), BF),
    dot_=((D, SEG), BF),
    stat=((SEG, 128), F32),
    bias=((SEG, SEG), F32),
    q=((SEG, HW), BF),
    kv=((2, SEG, HW), BF),
    kvl=((SEG, 2 * HW), BF),
    kvs=((SUMS, 2 * HW), BF),
    ks=((SUMS, HW), BF),
    vs=((SUMS, HW), BF),
    ssrc=((SLOT, 2 * HW), BF),
    big=((SEG, HEADS * SEG), F32),
    ssum=((HEADS, CHUNK, SUMS), F32),
    prob1=((HEADS, SEG, SEG), BF),
    prob2=((HEADS, SEG, SUMS), BF),
    m1=((SEG, 128), F32),
    l1=((SEG, 128), F32),
    m2=((SEG, 128), F32),
    l2=((SEG, 128), F32),
    a1=((SEG, 128), F32),
    a2=((SEG, 128), F32),
    a1x=((SEG, HW), F32),
    a2x=((SEG, HW), F32),
    o1=((SEG, HW), F32),
    att=((SEG, HW), F32),
    attp=((4, 2, ROWS, 2 * HW), BF),
    atta=((4, SEG, HW), BF),
    hid=((SEG, D), F32),
    nm=((SEG, D), BF),
    nmt=((D, SEG), BF),
    act=((SEG, D), BF),
    gp=((SEG, D), BF),
    rm_s=((SEG, D), BF),
    rm_1=((2, 2, HALF, D), BF),
    rm_x=((2, HALF, D), BF),
    rm_2=((2, HALF, D), BF),
    ro_s=((SEG, D), BF),
    ro_1=((2, 2, HALF, D), BF),
    ro_x=((2, HALF, D), BF),
    ro_2=((2, HALF, D), BF),
    rn_s=((SEG, D), BF),
    rn_1=((2, 2, HALF, D), BF),
    rn_x=((2, HALF, D), BF),
    rn_2=((2, HALF, D), BF),
    gh=((ROWS, D), F32),
    gbr=((ROWS, D), BF),
    sa=((2, 4, HALF, HW), BF),
    sb=((2, 4, HALF, HW), BF),
    do=((2, 4, HALF, HW), BF),
    gba=((2, 4, HALF, HW), BF),
    ds=((HEADS, SEG, SUMS), BF),
    dkvs=((SUMS, 2 * HW), BF),
    sumg=((SLOTS, SLOT, 2 * HW), BF),
    dqkv=((SEG, 3 * HW), BF),
    g1=((4, 4, 48, D), BF),
    g2=((4, 4, 48, 2 * D), BF),
    rza1=((3, 4, 48, D // 2), BF),
    rxa1=((3, 48, D // 2), BF),
    rxb1=((3, 4, 48, D // 2), BF),
    rzb1=((3, 48, D // 2), BF),
    ha1=((4, 48, D // 2), BF),
    hb1=((4, 48, D // 2), BF),
    r1a=((2, 2, 48, D), BF),
    s2a=((2, 2, 48, D), BF),
    r2a=((2, 4, 48, D), BF),
    r1b=((2, 2, 48, D), BF),
    s2b=((2, 2, 48, D), BF),
    r2b=((2, 4, 48, D), BF),
    rxa2=((3, 48, D), BF),
    rzb2=((3, 48, D), BF),
    ha2=((4, 48, D), BF),
    hb2=((4, 48, D), BF),
    fx1=((4, 16, D), BF),
    fx2=((4, 16, 2 * D), BF),
    fin1=((8, 16, D), BF),
    fin2=((8, 16, 2 * D), BF),
    vgr=((16, D), F32),
    vgx=((3, 16, D), F32),
    vgs=((16, D), F32),
    vgz=((3, 16, D), F32),
    sel=((D, 384), BF),
    vgt=((16, 256), F32),
    vfin=((8, 16, 256), F32),
)
SENDS = 24
RECVS = 72


class Flight:
    def __init__(self, waiter):
        self.waiter = waiter
        self.arrived = False
        self.left = False

    def wait_recv(self):
        if not self.arrived:
            self.waiter.wait_recv()
        self.arrived = True

    def wait_send(self):
        if not self.left:
            self.waiter.wait_send()
        self.left = True


def layer_kernel(
    seg_ref, tok, dout, wq, wk, wv, wo, wu, wd, *refs,
):
    vectors, refs = refs[:9], refs[9:]
    out_o, gtok_o, gq_o, gk_o, gv_o, go_o, gu_o, gd_o, gvec_o = refs[:9]
    scratch = refs[9:]
    m = types.SimpleNamespace(**dict(zip(SCRATCH, scratch[:-4])))
    ss, rs, far_ss, far_rs = scratch[-4:]
    batch = lax.axis_index("batch")
    place = lax.axis_index("seq")
    s = place // 4
    t = place % 4
    z = s // 4
    x = s % 4
    sib = t + 1 - 2 * (t % 2)
    over = (t + 2) % 4
    diag = 3 - t
    group = (over, diag, sib)

    def dev(seg, tt, bb):
        return (4 * seg + tt, bb)

    def here(tt):
        return dev(s, tt, batch)

    def along_x(k):
        return dev(4 * z + (x + k) % 4, t, batch)

    def along_z(k):
        return dev(4 * ((z + k) % 4) + x, t, batch)

    used = [0]
    sent = []

    def take(n=1):
        first = used[0]
        used[0] += n
        return first

    def fly(copies, total=None):
        k = len(sent)
        if k >= SENDS:
            sent[k - SENDS].wait_send()
        send_sem, recv_sem = ss.at[k % SENDS], rs.at[take()]
        for src, dst, device in copies:
            copy = pltpu.make_async_remote_copy(
                src_ref=src, dst_ref=dst, send_sem=send_sem, recv_sem=recv_sem,
                device_id=device, device_id_type=MESH,
            )
            copy.start()
        if total is not None:
            copy = pltpu.make_async_remote_copy(
                src_ref=total, dst_ref=total, send_sem=send_sem, recv_sem=recv_sem,
                device_id=device, device_id_type=MESH,
            )
        flight = Flight(copy)
        sent.append(flight)
        return flight

    def far_copy(which, src, dst, seg):
        return pltpu.make_async_remote_copy(
            src_ref=src, dst_ref=dst, send_sem=far_ss.at[which], recv_sem=far_rs.at[which],
            device_id=dev(seg, t, batch), device_id_type=MESH,
        )

    def slot_of(ref, seg):
        return ref.at[pl.ds(pl.multiple_of(SLOT * seg, SLOT), SLOT)]

    def far_wait(which, count, received):
        for n in range(1, 16):
            @pl.when(count == n)
            def _(n=n):
                part = m.kvs.at[0:SLOT * n]
                if received:
                    far_copy(which, part, part, s).wait_recv()
                else:
                    far_copy(which, part, part, s).wait_send()

    def block(c, k):
        return pl.ds(pl.multiple_of(CHUNK * c + HALF * k, HALF), HALF)

    def within(rows, c):
        return pl.ds(pl.multiple_of(rows.start - CHUNK * c, rows.size), rows.size)

    def loop(first, count, size, fn, unroll=4):
        def step(j, carry):
            fn(pl.ds(pl.multiple_of(first + j * size, size), size))
            return carry

        lax.fori_loop(0, count, step, 0, unroll=unroll)

    m.kvs[...] = jnp.zeros((SUMS, 2 * HW), BF)
    m.sumg[...] = jnp.zeros((SLOTS, SLOT, 2 * HW), BF)
    barrier = pltpu.get_barrier_semaphore()
    partners = [here(u) for u in group]
    partners += [dev((s + k) % 16, t, batch) for k in range(1, 16)]
    partners += [dev(s, u, 1 - batch) for u in (t, sib, over, diag)]
    for partner in partners:
        pl.semaphore_signal(barrier, inc=1, device_id=partner, device_id_type=MESH)
    m.pk1[...] = jnp.zeros((4, 16, D), BF)
    for u in range(4):
        cols = slice(HW * u, HW * u + HW)
        m.pk1[u, 0:12, :] = jnp.concatenate(
            [wk[:, cols], wv[:, cols], wq[:, cols], wo[:, cols]], axis=1
        )
    m.vin[...] = jnp.zeros((16, 128), F32)
    for k, ref in enumerate(vectors[:8]):
        m.vin[k:k + 1, 0:12] = ref[...].astype(F32)
    m.vin[8:9, 0:48] = vectors[8][...].astype(F32)
    shift = iota((128, D), 1) - iota((128, D), 0)
    narrow = dot(m.vin[...].astype(BF), (shift == 12 * place).astype(BF))
    wider = dot(m.vin[...].astype(BF), (shift == 48 * (place % 16)).astype(BF))
    vec_row = iota((16, D), 0)
    m.vb[...] = jnp.where(
        vec_row < 8, narrow, jnp.where(vec_row == 8 + z, wider[8:9, :], 0.0)
    ).astype(BF)
    pl.semaphore_wait(barrier, len(partners))

    first1 = fly([(m.pk1.at[u], m.p01.at[t], here(u)) for u in group], m.p01.at[0:3])
    firstv = fly(
        [(m.vb, m.vg.at[k], here(u)) for k, u in enumerate((sib, over, diag))], m.vg
    )
    m.p01[t] = m.pk1[t]
    m.pk2[...] = jnp.zeros((4, 16, 2 * D), BF)
    for u in range(4):
        wide = slice(D * u, D * u + D)
        m.pk2[u, 0:12, 0:D] = wu[:, wide]
        m.pk2[u, 0:12, D:] = wd[:, wide]
    m.p02[t] = m.pk2[t]
    for c in range(2):
        m.toka[block(c, t), :] = tok[HALF * c:HALF * c + HALF, :]
        m.doa[block(c, t), :] = dout[HALF * c:HALF * c + HALF, :]

    def gather_start(ref):
        moves = [
            fly([(ref.at[block(c, t)], ref.at[block(c, t)], here(u)) for c in (0, 1)],
                ref.at[0:ROWS])
            for u in (over, sib)
        ]
        return moves

    def gather_pass(moves, ref):
        moves[0].wait_recv()
        moves.append(
            fly([(ref.at[block(c, over)], ref.at[block(c, over)], here(sib)) for c in (0, 1)],
                ref.at[0:ROWS])
        )

    def finish(moves):
        for move in moves:
            move.wait_recv()

    row48 = iota((48, 64), 0)
    owner48 = (
        (row48 >= 12).astype(jnp.int32)
        + (row48 >= 24).astype(jnp.int32)
        + (row48 >= 36).astype(jnp.int32)
    )
    squeeze = (iota((48, 64), 1) == row48 + 4 * owner48).astype(BF)

    def spread_start(w, a, b):
        mine_a, mine_b = w.at[z, x, :, a], w.at[z, x, :, b]
        return (
            fly([(mine_a, mine_a, along_x(k)) for k in (1, 3, 2)], w.at[0, 0:3, :, a]),
            fly([(mine_b, mine_b, along_z(k)) for k in (1, 3, 2)], w.at[0, 0:3, :, b]),
        )

    def pass_a(w, a, moves):
        plane_a = w.at[z, :, :, a]
        moves[0].wait_recv()
        return fly([(plane_a, plane_a, along_z(k)) for k in (1, 3, 2)], w.at[0:3, :, :, a])

    def pass_b(w, b, moves):
        plane_b = w.at[:, x, :, b]
        moves[1].wait_recv()
        return fly([(plane_b, plane_b, along_x(k)) for k in (1, 3, 2)], w.at[0:3, :, :, b])

    def spread_pass(w, a, b, moves):
        return pass_a(w, a, moves), pass_b(w, b, moves)

    kv_cols = pl.ds(0, 256), pl.ds(256, 128)
    qo_cols = pl.ds(384, 128), pl.ds(512, 256)
    up_down = pl.ds(0, D), pl.ds(D, D)
    halves = pl.ds(0, D // 2), pl.ds(D // 2, D // 2)

    first1.wait_recv()
    m.w1[z, x] = dot(squeeze, m.p01[...].reshape(64, D)).astype(BF)
    phase1 = spread_start(m.w1, *kv_cols)
    phase1b = spread_start(m.w1, *qo_cols)
    first2 = fly([(m.pk2.at[u], m.p02.at[t], here(u)) for u in group], m.p02.at[0:3])
    ag_tok = gather_start(m.toka)

    seg_len = seg_ref[0, s]

    def token_of(rows):
        return rows + 64 * ((rows % CHUNK) // HALF) - 192 * (rows // CHUNK)

    k_pos = token_of(iota((1, SEG), 1))

    def mask(rows):
        mine = token_of(rows.start + iota((ROWS, 1), 0))
        ok = ((k_pos <= mine) & (k_pos < seg_len)) | (k_pos == mine)
        m.bias[rows, :] = jnp.where(ok, 0.0, MASKED)

    loop(0, 4, ROWS, mask)
    s_col = iota((8, SUMS), 1)
    sum_bias = jnp.where((s_col < SLOT * s) & (s_col % SLOT < SUMMARY), 0.0, MASKED)[0:1, :]
    pick_row = iota((SLOT, SEG), 0)
    pick = ((k_pos == seg_len - SUMMARY + pick_row) & (pick_row < SUMMARY)).astype(BF)
    lane_head = iota((1, HW), 1) // 64

    def of_head(value, h):
        return jnp.where(lane_head == h, value, jnp.zeros_like(value))

    def by_head(cols):
        return jnp.where(
            lane_head == 0, cols[:, 0:1], jnp.where(lane_head == 1, cols[:, 1:2], cols[:, 2:3])
        )

    def add4(own, got):
        return own.astype(F32) + got[0].astype(F32) + got[1].astype(F32) + got[2].astype(F32)

    def moved_by(rows, one_hot):
        high = rows.astype(BF)
        rest = rows - high.astype(F32)
        mid = rest.astype(BF)
        low = (rest - mid.astype(F32)).astype(BF)
        pieces = dot(jnp.concatenate([high, mid, low], axis=0), one_hot)
        return pieces[0:16, :] + pieces[16:32, :] + pieces[32:48, :]

    feature, lane = iota((D, 128), 0), iota((D, 128), 1)
    m.sel[:, 0:128] = ((feature - lane == 48 * s) & (lane < 48)).astype(BF)
    feature, lane = iota((D, 256), 0), iota((D, 256), 1)
    m.sel[:, 128:384] = ((feature - lane == 192 * x) & (lane < 192)).astype(BF)

    firstv.wait_recv()
    m.vs1[...] = add4(m.vb[...], m.vg).astype(BF)
    vx = fly([(m.vs1, m.vx.at[k - 1], along_x(k)) for k in (1, 2, 3)], m.vx)
    ends1 = spread_pass(m.w1, *kv_cols, phase1)
    ends1b = spread_pass(m.w1, *qo_cols, phase1b)
    vx.wait_recv()
    m.vs2[...] = add4(m.vs1[...], m.vx).astype(BF)
    vz = fly([(m.vs2, m.vz.at[k - 1], along_z(k)) for k in (1, 2, 3)], m.vz)
    first2.wait_recv()
    m.w2[z, x] = dot(squeeze, m.p02[...].reshape(64, 2 * D)).astype(BF)
    phase2 = spread_start(m.w2, *up_down)
    gather_pass(ag_tok, m.toka)
    ag_do = gather_start(m.doa)
    vz.wait_recv()
    m.vecs[...] = add4(m.vs2[...], m.vz)
    gain1, shift1 = m.vecs[0:1, :], m.vecs[1:2, :]
    gain2, shift2 = m.vecs[5:6, :], m.vecs[6:7, :]
    o_bias, down_bias = m.vecs[4:5, :], m.vecs[7:8, :]

    def my_cols(row):
        whole = m.vecs[row:row + 1, :]
        value = whole[:, 0:HW]
        for u in range(1, 4):
            value = jnp.where(t == u, whole[:, HW * u:HW * u + HW], value)
        return value

    q_bias, v_bias = my_cols(2), my_cols(3)
    up_bias = m.vecs[8:9, :]
    for u in range(1, 4):
        up_bias = jnp.where(t == u, m.vecs[8 + u:9 + u, :], up_bias)

    finish(ag_tok)

    def norm1(rows):
        values = m.toka[rows, :].astype(F32)
        mean = jnp.mean(values, axis=-1, keepdims=True)
        center = values - mean
        scale = lax.rsqrt(jnp.mean(center * center, axis=-1, keepdims=True) + EPSILON)
        m.nrm[rows, :] = (center * scale * gain1 + shift1).astype(BF)
        m.stat[rows, 0:1] = mean
        m.stat[rows, 1:2] = scale

    loop(0, 4, ROWS, norm1)
    m.nrmt[...] = m.nrm[...].T

    finish(ends1)
    kv_bias = jnp.concatenate([jnp.zeros((1, HW), F32), v_bias], axis=1)
    m.kvl[...] = (dot(m.nrm[...], m.w1[:, :, :, 0:2 * HW].reshape(D, 2 * HW)) + kv_bias).astype(BF)

    m.ssrc[...] = dot(pick, m.kvl[...]).astype(BF)
    for k in range(1, 16):
        @pl.when(s + k < 16)
        def _(k=k):
            far_copy(0, m.ssrc, slot_of(m.kvs, s), (s + k) % 16).start()
    ends2b = pass_b(m.w2, up_down[1], phase2)
    finish(ends1b)
    m.q[...] = (
        (dot(m.nrm[...], m.w1[:, :, :, 2 * HW:3 * HW].reshape(D, HW)) + q_bias) * 0.125
    ).astype(BF)
    w_o = m.w1[...].reshape(D, D)[:, 3 * HW:]
    m.wosl[t] = jnp.concatenate([w_o[0:D // 2, :], w_o[D // 2:, :]], axis=1)
    m.kv[0] = m.kvl[:, 0:HW]
    m.kv[1] = m.kvl[:, HW:]
    ag_wo = [fly([(m.wosl.at[t], m.wosl.at[t], here(u))]) for u in (over, sib)]

    for h in range(HEADS):
        m.big[:, SEG * h:SEG * h + SEG] = dot_nt(of_head(m.q[...], h), m.kv[0]) + m.bias[...]
    for h in range(HEADS):
        def soften1(rows, h=h):
            score = m.big[rows, SEG * h:SEG * h + SEG]
            peak = jnp.max(score, axis=-1, keepdims=True)
            power = jnp.exp(score - peak)
            m.prob1[h, rows, :] = power.astype(BF)
            m.m1[rows, h:h + 1] = peak
            m.l1[rows, h:h + 1] = jnp.sum(power, axis=-1, keepdims=True)

        loop(0, 4, ROWS, soften1)
        part = dot(m.prob1[h], of_head(m.kv[1], h))
        m.o1[...] = part if h == 0 else m.o1[...] + part
    gather_pass(ag_do, m.doa)

    far_wait(0, s, True)
    ends2a = pass_a(m.w2, up_down[0], phase2)
    ends2 = (ends2a, ends2b)
    m.ks[...] = m.kvs[:, 0:HW]
    m.vs[...] = m.kvs[:, HW:]

    ag_att = []

    def attend(c):
        rows_c = slice(CHUNK * c, CHUNK * c + CHUNK)
        part = None
        for h in range(HEADS):
            m.ssum[h] = dot_nt(of_head(m.q[rows_c, :], h), m.ks[...]) + sum_bias

            def soften2(rows, h=h):
                score = m.ssum[h, within(rows, c), :]
                peak = jnp.max(score, axis=-1, keepdims=True)
                power = jnp.exp(score - peak)
                m.prob2[h, rows, :] = power.astype(BF)
                m.m2[rows, h:h + 1] = peak
                m.l2[rows, h:h + 1] = jnp.sum(power, axis=-1, keepdims=True)

            loop(CHUNK * c, 2, ROWS, soften2)
            more = dot(m.prob2[h, rows_c, :], of_head(m.vs[...], h))
            part = more if h == 0 else part + more
        m1, m2 = m.m1[rows_c, 0:HEADS], m.m2[rows_c, 0:HEADS]
        peak = jnp.maximum(m1, m2)
        e1, e2 = jnp.exp(m1 - peak), jnp.exp(m2 - peak)
        share = 1.0 / (m.l1[rows_c, 0:HEADS] * e1 + m.l2[rows_c, 0:HEADS] * e2)
        a1, a2 = e1 * share, e2 * share
        m.a1[rows_c, 0:HEADS] = a1
        m.a2[rows_c, 0:HEADS] = a2
        a1x, a2x = by_head(a1), by_head(a2)
        m.a1x[rows_c, :] = a1x
        m.a2x[rows_c, :] = a2x
        attended = m.o1[rows_c, :] * a1x + part * a2x
        m.att[rows_c, :] = attended
        low = attended.astype(BF)
        m.attp[t, c] = jnp.concatenate([low[0:ROWS, :], low[ROWS:, :]], axis=1)
        mine_c = m.attp.at[t, c]
        ag_att.append([fly([(mine_c, mine_c, here(u))]) for u in (over, sib)])

    attend(0)
    ag_wo[0].wait_recv()
    ag_wo.append(fly([(m.wosl.at[over], m.wosl.at[over], here(sib))]))
    attend(1)
    finish(ag_wo)
    m.wof[0:D // 2, :] = jnp.concatenate([m.wosl[u, :, 0:HW] for u in range(4)], axis=1)
    m.wof[D // 2:, :] = jnp.concatenate([m.wosl[u, :, HW:] for u in range(4)], axis=1)

    def att_pass(c):
        ag_att[c][0].wait_recv()
        theirs = m.attp.at[over, c]
        ag_att[c].append(fly([(theirs, theirs, here(sib))]))

    def scatter_start(name, cs):
        src, r1 = getattr(m, name + "_s"), getattr(m, name + "_1")
        return [
            fly([(src.at[block(c, k)], r1.at[c, i], here(sib)) for c in cs],
                r1.at[0:len(cs), i])
            for i, k in ((1, diag), (0, sib))
        ]

    def scatter_pass(name, cs, moves):
        src, r1 = getattr(m, name + "_s"), getattr(m, name + "_1")
        cross, r2 = getattr(m, name + "_x"), getattr(m, name + "_2")
        moves[0].wait_recv()
        for c in cs:
            cross[c] = (src[block(c, over), :].astype(F32) + r1[c, 1].astype(F32)).astype(BF)
        moves.append(
            fly([(cross.at[c], r2.at[c], here(over)) for c in cs], r2.at[0:len(cs)])
        )

    def scatter_end(name, c, moves):
        src, r1 = getattr(m, name + "_s"), getattr(m, name + "_1")
        r2 = getattr(m, name + "_2")
        moves[1].wait_recv()
        moves[2].wait_recv()
        return src[block(c, t), :].astype(F32) + r1[c, 0].astype(F32) + r2[c].astype(F32)

    def gelu(rows):
        a = m.big[rows, 0:D]
        square = a * a
        bend = jnp.tanh(0.7978845608028654 * (a + 0.044715 * (square * a)))
        half = 0.5 * (1.0 + bend)
        m.act[rows, :] = (a * half).astype(BF)
        slope = half + (0.5 * a) * (1.0 - bend * bend) * (
            0.7978845608028654 * (1.0 + 0.134145 * square)
        )
        m.gp[rows, :] = (m.big[rows, D:] * slope).astype(BF)

    def norm2(rows):
        center, scale = norm_stats(m.hid[rows, :])
        m.nm[rows, :] = (center * scale * gain2 + shift2).astype(BF)

    def project(c):
        rows_c = slice(CHUNK * c, CHUNK * c + CHUNK)
        finish(ag_att[c])
        for u in range(4):
            m.atta[u, CHUNK * c:CHUNK * c + ROWS, :] = m.attp[u, c, :, 0:HW]
            m.atta[u, CHUNK * c + ROWS:CHUNK * c + CHUNK, :] = m.attp[u, c, :, HW:]
        branch = dot(m.atta[0, rows_c, :], m.wof[0:HW, :])
        for u in range(1, 4):
            branch = branch + dot(m.atta[u, rows_c, :], m.wof[HW * u:HW * u + HW, :])
        m.hid[rows_c, :] = m.toka[rows_c, :].astype(F32) + branch + o_bias
        loop(CHUNK * c, 2, ROWS, norm2)

    def feed(c):
        rows_c = slice(CHUNK * c, CHUNK * c + CHUNK)
        m.big[rows_c, 0:D] = dot(m.nm[rows_c, :], m.w2[:, :, :, 0:D].reshape(D, D)) + up_bias
        m.big[rows_c, D:] = dot(m.doa[rows_c, :], m.w2[:, :, :, D:].reshape(D, D))
        loop(CHUNK * c, 4, 64, gelu)
        m.rm_s[rows_c, :] = dot_nt(m.gp[rows_c, :], m.w2[:, :, :, 0:D].reshape(D, D)).astype(BF)
        return scatter_start("rm", (c,))

    att_pass(0)
    project(0)
    att_pass(1)
    finish(ag_do)
    finish(ends2)
    rm0 = feed(0)
    project(1)
    scatter_pass("rm", (0,), rm0)
    rm1 = feed(1)

    m.dot_[...] = m.doa[...].T
    m.nmt[...] = m.nm[...].T
    scatter_pass("rm", (1,), rm1)
    m.g2[:, :, :, 0:D] = dot(m.nmt[...], m.gp[...]).astype(BF).reshape(4, 4, 48, D)
    m.g2[:, :, :, D:] = dot(m.dot_[...], m.act[...]).astype(BF).reshape(4, 4, 48, D)

    def reduce_start(g, tag, a, b, at_a, at_b):
        rza, rxb = getattr(m, "rza" + tag), getattr(m, "rxb" + tag)
        return (
            fly([(g.at[(z + k) % 4, :, :, a], rza.at[k - 1, :, :, at_a], along_z(k))
                 for k in (1, 3, 2)], rza.at[:, :, :, at_a]),
            fly([(g.at[:, (x + k) % 4, :, b], rxb.at[k - 1, :, :, at_b], along_x(k))
                 for k in (1, 3, 2)], rxb.at[:, :, :, at_b]),
        )

    def reduce_pass(g, tag, pieces):
        rza, rxb = getattr(m, "rza" + tag), getattr(m, "rxb" + tag)
        rxa, rzb = getattr(m, "rxa" + tag), getattr(m, "rzb" + tag)
        ha, hb = getattr(m, "ha" + tag), getattr(m, "hb" + tag)
        for (a, b, at_a, at_b), moves in pieces:
            into = slice(at_a.start, at_a.start + at_a.size)
            moves[0].wait_recv()
            for k in range(4):
                ha[k, :, into] = add4(
                    g[z, k, :, a.start:a.start + a.size], [rza[j, k, :, into] for j in range(3)]
                ).astype(BF)
        a2 = fly([(ha.at[(x + k) % 4], rxa.at[k - 1], along_x(k)) for k in (1, 3, 2)], rxa)
        for (a, b, at_a, at_b), moves in pieces:
            into = slice(at_b.start, at_b.start + at_b.size)
            moves[1].wait_recv()
            for k in range(4):
                hb[k, :, into] = add4(
                    g[k, x, :, b.start:b.start + b.size], [rxb[j, k, :, into] for j in range(3)]
                ).astype(BF)
        b2 = fly([(hb.at[(z + k) % 4], rzb.at[k - 1], along_z(k)) for k in (1, 3, 2)], rzb)
        return a2, b2

    row64 = iota((64, 48), 0)
    expand = (
        (iota((64, 48), 1) == row64 - 4 * (row64 // 16)) & (row64 % 16 < 12)
    ).astype(BF)
    mine = 4 * batch + t
    everyone = [(u, dev(s, u, 1 - batch)) for u in (over, diag, sib, t)]
    everyone += [(u, here(u)) for u in group]

    def reduce_last(tag, half, moves):
        rxa, rzb = getattr(m, "rxa" + tag), getattr(m, "rzb" + tag)
        ha, hb = getattr(m, "ha" + tag), getattr(m, "hb" + tag)
        fx, fin = getattr(m, "fx" + tag), getattr(m, "fin" + tag)
        finish(moves)
        a = add4(ha[x], [rxa[j] for j in range(3)]).astype(BF)
        b = add4(hb[z], [rzb[j] for j in range(3)]).astype(BF)
        fx[:, :, 0:half] = dot(expand, a).astype(BF).reshape(4, 16, half)
        fx[:, :, half:] = dot(expand, b).astype(BF).reshape(4, 16, half)
        moves = fly([(fx.at[u], fin.at[mine], device) for u, device in everyone], fin.at[0:7])
        fin[mine] = fx[t]
        return moves


    up_c, down_c = up_down
    lo, hi = pl.ds(0, 2), pl.ds(2, 2)
    z1, z2, z3 = (z + 1) % 4, (z + 2) % 4, (z + 3) % 4
    x1, x2, x3 = (x + 1) % 4, (x + 2) % 4, (x + 3) % 4
    relay_a = fly(
        [(m.g2.at[z2, lo, :, up_c], m.r1a.at[0], along_z(1)),
         (m.g2.at[z2, hi, :, up_c], m.r1a.at[1], along_z(3))], m.r1a
    )
    relay_b = fly(
        [(m.g2.at[lo, x2, :, down_c], m.r1b.at[0], along_x(1)),
         (m.g2.at[hi, x2, :, down_c], m.r1b.at[1], along_x(3))], m.r1b
    )
    plain_a = fly(
        [(m.g2.at[z1, hi, :, up_c], m.r2a.at[0, hi], along_z(1)),
         (m.g2.at[z3, lo, :, up_c], m.r2a.at[1, lo], along_z(3))], m.r1a
    )
    plain_b = fly(
        [(m.g2.at[hi, x1, :, down_c], m.r2b.at[0, hi], along_x(1)),
         (m.g2.at[lo, x3, :, down_c], m.r2b.at[1, lo], along_x(3))], m.r1b
    )

    def relay():
        relay_a.wait_recv()
        m.s2a[0] = (m.g2[z1, 0:2, :, 0:D].astype(F32) + m.r1a[0].astype(F32)).astype(BF)
        m.s2a[1] = (m.g2[z3, 2:4, :, 0:D].astype(F32) + m.r1a[1].astype(F32)).astype(BF)
        a = fly(
            [(m.s2a.at[0], m.r2a.at[0, lo], along_z(1)),
             (m.s2a.at[1], m.r2a.at[1, hi], along_z(3))], m.r1a
        )
        relay_b.wait_recv()
        m.s2b[0] = (m.g2[0:2, x1, :, D:].astype(F32) + m.r1b[0].astype(F32)).astype(BF)
        m.s2b[1] = (m.g2[2:4, x3, :, D:].astype(F32) + m.r1b[1].astype(F32)).astype(BF)
        b = fly(
            [(m.s2b.at[0], m.r2b.at[0, lo], along_x(1)),
             (m.s2b.at[1], m.r2b.at[1, hi], along_x(3))], m.r1b
        )
        return a, b

    def relayed(moves):
        plain_a.wait_recv()
        moves[0].wait_recv()
        for k in range(4):
            m.ha2[k] = (
                m.g2[z, k, :, 0:D].astype(F32) + m.r2a[0, k].astype(F32) + m.r2a[1, k].astype(F32)
            ).astype(BF)
        a2 = fly([(m.ha2.at[(x + k) % 4], m.rxa2.at[k - 1], along_x(k)) for k in (1, 3, 2)], m.rxa2)
        plain_b.wait_recv()
        moves[1].wait_recv()
        for k in range(4):
            m.hb2[k] = (
                m.g2[k, x, :, D:].astype(F32) + m.r2b[0, k].astype(F32) + m.r2b[1, k].astype(F32)
            ).astype(BF)
        b2 = fly([(m.hb2.at[(z + k) % 4], m.rzb2.at[k - 1], along_z(k)) for k in (1, 3, 2)], m.rzb2)
        return a2, b2


    zero_row = jnp.zeros((1, D), F32)
    ones = jnp.ones((8, SEG), BF)

    def col_sums(value):
        return dot(ones[:, 0:value.shape[0]], value)[0:1, :]

    def norm_back(values, grads, gain):
        center, scale = norm_stats(values)
        unit = center * scale
        inner = grads * gain
        return unit, scale * (
            inner
            - jnp.mean(inner, axis=-1, keepdims=True)
            - unit * jnp.mean(inner * unit, axis=-1, keepdims=True)
        )

    g_gain2, g_shift2 = zero_row, zero_row
    aa = []
    for c in range(2):
        at = slice(HALF * c, HALF * c + HALF)
        grads = scatter_end("rm", c, rm0 if c == 0 else rm1)
        unit, into = norm_back(m.hid[block(c, t), :], grads, gain2)
        into = into + dout[at, :].astype(F32)
        m.gh[at, :] = into
        low = into.astype(BF)
        m.gbr[at, :] = low
        for u in range(4):
            m.sa[c, u] = dot_nt(low, m.wof[HW * u:HW * u + HW, :]).astype(BF)
        aa.append(
            fly([(m.sa.at[c, u], m.do.at[c, t], here(u)) for u in group], m.do.at[c, 0:3])
        )
        m.do[c, t] = m.sa[c, t]
        g_gain2 += jnp.sum(grads * unit, axis=0, keepdims=True)
        g_shift2 += jnp.sum(grads, axis=0, keepdims=True)
    m.ro_s[...] = dot_nt(m.act[...], m.w2[:, :, :, D:].reshape(D, D)).astype(BF)
    for u in range(4):
        cols = m.gbr[:, HW * u:HW * u + HW]
        m.sb[0, u] = cols[0:HALF, :]
        m.sb[1, u] = cols[HALF:, :]
    qt = m.q[...].T
    m.o1[...] = jnp.zeros((SEG, HW), F32)

    ab = fly(
        [(m.sb.at[c, u], m.gba.at[c, t], here(u)) for u in group for c in (0, 1)],
        m.gba.at[:, 0:3],
    )
    m.gba[0, t] = m.sb[0, t]
    m.gba[1, t] = m.sb[1, t]
    ro = scatter_start("ro", (0, 1))
    for c in range(2):
        rows_c = slice(CHUNK * c, CHUNK * c + CHUNK)
        aa[c].wait_recv()
        do_c = m.do[c].reshape(CHUNK, HW)
        weighed = do_c.astype(F32) * m.att[rows_c, :]
        for h in range(HEADS):
            m.m1[rows_c, h:h + 1] = jnp.sum(of_head(weighed, h), axis=-1, keepdims=True)
        for h in range(HEADS):
            m.ssum[h] = dot_nt(of_head(do_c, h), m.vs[...])

            def back_sum(rows, h=h, c=c):
                slope = (m.ssum[h, within(rows, c), :] - m.m1[rows, h:h + 1]) * m.a2[rows, h:h + 1]
                m.ds[h, rows, :] = (m.prob2[h, rows, :].astype(F32) * slope).astype(BF)

            loop(CHUNK * c, 2, ROWS, back_sum)
        if c == 0:
            rg2 = relay()
    do_all = m.do[...].reshape(SEG, HW)
    do_wide = do_all.astype(F32)
    dot1 = (do_wide * m.a1x[...]).astype(BF).T
    dot2 = (do_wide * m.a2x[...]).astype(BF).T
    for h in range(HEADS):
        feat, feat_v = slice(64 * h, 64 * h + 64), slice(HW + 64 * h, HW + 64 * h + 64)
        m.big[feat, 0:SUMS] = dot(qt[feat, :], m.ds[h])
        m.big[feat_v, 0:SUMS] = dot(dot2[feat, :], m.prob2[h])
    m.dkvs[...] = m.big[0:2 * HW, 0:SUMS].T.astype(BF)
    for k in range(1, 16):
        @pl.when(s >= k)
        def _(k=k):
            seg = (s + 16 - k) % 16
            far_copy(1, slot_of(m.dkvs, seg), m.sumg.at[k], seg).start()
    scatter_pass("ro", (0, 1), ro)

    for h in range(HEADS):
        m.o1[...] += dot(m.ds[h], of_head(m.ks[...], h))
    for h in range(HEADS):
        m.big[:, SEG * h:SEG * h + SEG] = dot_nt(of_head(do_all, h), m.kv[1])
    for h in range(HEADS):
        def back_own(rows, h=h):
            weight = m.prob1[h, rows, :].astype(F32)
            slope = (m.big[rows, SEG * h:SEG * h + SEG] - m.m1[rows, h:h + 1]) * m.a1[rows, h:h + 1]
            m.ds[h, rows, 0:SEG] = (weight * slope).astype(BF)

        loop(0, 4, ROWS, back_own)
        score_grads = m.ds[h, :, 0:SEG]
        m.o1[...] += dot(score_grads, of_head(m.kv[0], h))
        feat, feat_v = slice(64 * h, 64 * h + 64), slice(HW + 64 * h, HW + 64 * h + 64)
        m.bias[feat, :] = dot(qt[feat, :], score_grads)
        m.bias[feat_v, :] = dot(dot1[feat, :], m.prob1[h])
    for u in range(4):
        m.nmt[HW * u:HW * u + HW, :] = m.atta[u].T
    ends_g2 = relayed(rg2)
    ab.wait_recv()
    g_o = dot(m.nmt[...], m.gba[...].reshape(SEG, HW))
    dq = m.o1[...].astype(BF) * jnp.asarray(0.125, BF)
    m.g1[:, :, :, 2 * HW:] = (
        jnp.concatenate([dot(m.nrmt[...], dq), g_o], axis=1).astype(BF).reshape(4, 4, 48, 2 * HW)
    )
    cols_qo = qo_cols + (pl.ds(256, 128), pl.ds(128, 256))
    cols_kv = kv_cols + (pl.ds(0, 256), pl.ds(0, 128))
    rg1_qo = reduce_start(m.g1, "1", *cols_qo)

    m.big[:, 0:2 * HW] = m.bias[0:2 * HW, :].T
    pick_t = pick.T

    far_wait(1, 15 - s, True)

    total = m.sumg[0].astype(F32)
    for k in range(1, SLOTS):
        total = total + m.sumg[k].astype(F32)
    high = total.astype(BF)
    rest = (total - high.astype(F32)).astype(BF)
    dkv = (m.big[:, 0:2 * HW] + dot(pick_t, high) + dot(pick_t, rest)).astype(BF)
    m.dqkv[...] = jnp.concatenate([dkv, dq], axis=1)

    m.g1[:, :, :, 0:2 * HW] = dot(m.nrmt[...], dkv).astype(BF).reshape(4, 4, 48, 2 * HW)
    rg1_kv = reduce_start(m.g1, "1", *cols_kv)
    m.rn_s[...] = dot_nt(m.dqkv[...], m.w1[...].reshape(D, D)[:, 0:3 * HW]).astype(BF)
    rn = [scatter_start("rn", (c,)) for c in range(2)]

    def gain_grads(j, carry):
        rows = pl.ds(pl.multiple_of(j * 64, 64), 64)
        grads = m.rn_s[rows, :].astype(F32)
        unit = (m.toka[rows, :].astype(F32) - m.stat[rows, 0:1]) * m.stat[rows, 1:2]
        return (
            carry[0] + jnp.sum((grads * unit).reshape(8, 8, D), axis=0),
            carry[1] + jnp.sum(grads.reshape(8, 8, D), axis=0),
        )

    zero8 = jnp.zeros((8, D), F32)
    g_gain1, g_shift1 = lax.fori_loop(0, 8, gain_grads, (zero8, zero8), unroll=4)
    scatter_pass("rn", (0,), rn[0])
    scatter_pass("rn", (1,), rn[1])
    g_qkvb = col_sums(m.dqkv[...])

    def in_place(row):
        none = jnp.zeros((1, HW), F32)
        return jnp.concatenate([jnp.where(t == u, row, none) for u in range(4)], axis=1)

    rows8 = (
        jnp.sum(g_gain1, axis=0, keepdims=True),
        jnp.sum(g_shift1, axis=0, keepdims=True),
        in_place(g_qkvb[:, 2 * HW:]),
        in_place(g_qkvb[:, HW:2 * HW]),
        col_sums(m.gbr[...]),
        g_gain2,
        g_shift2,
        col_sums(dout[...]),
    )
    m.vgr[...] = jnp.zeros((16, D), F32)
    for k, row in enumerate(rows8):
        m.vgr[k:k + 1, :] = row
    g_ub = col_sums(m.gp[...])
    for u in range(4):
        m.vgr[8 + u:9 + u, :] = jnp.where(t == u, g_ub, zero_row)
    vgx = fly([(m.vgr, m.vgx.at[k - 1], along_x(k)) for k in (1, 2, 3)], m.vgx)
    fin_g2 = reduce_last("2", D, ends_g2)
    for c in range(2):
        out_o[HALF * c:HALF * c + HALF, :] = (
            scatter_end("ro", c, ro) + m.hid[block(c, t), :] + down_bias
        ).astype(BF)
    ends_g1 = reduce_pass(m.g1, "1", [(cols_qo, rg1_qo), (cols_kv, rg1_kv)])
    vgx.wait_recv()
    m.vgs[...] = add4(m.vgr[...], m.vgx)
    vgz = fly([(m.vgs, m.vgz.at[k - 1], along_z(k)) for k in (1, 2, 3)], m.vgz)

    for c in range(2):
        at = slice(HALF * c, HALF * c + HALF)
        grads = scatter_end("rn", c, rn[c])
        _, into = norm_back(tok[at, :].astype(F32), grads, gain1)
        gtok_o[at, :] = into + m.gh[at, :]
    fin_g1 = reduce_last("1", D // 2, ends_g1)
    vgz.wait_recv()
    totals = add4(m.vgs[...], m.vgz)
    moved = moved_by(totals, m.sel[...])
    up_row = jnp.sum(jnp.where(iota((16, 256), 0) == 8 + z, moved[:, 128:384], 0.0), axis=0, keepdims=True)
    m.vgt[...] = jnp.zeros((16, 256), F32)
    m.vgt[0:8, 0:128] = moved[0:8, 0:128]
    m.vgt[8:9, :] = up_row
    fin_v = fly([(m.vgt, m.vfin.at[mine], device) for _, device in everyone], m.vfin.at[0:7])
    m.vfin[mine] = m.vgt[...]

    def both(fin, u, cols):
        return fin[u, 0:12, cols].astype(F32) + fin[4 + u, 0:12, cols].astype(F32)

    fin_g2.wait_recv()
    for u in range(4):
        wide = slice(D * u, D * u + D)
        gu_o[:, wide] = both(m.fin2, u, slice(0, D))
        gd_o[:, wide] = both(m.fin2, u, slice(D, 2 * D))
    fin_v.wait_recv()
    totals = m.vfin[0]
    for k in range(1, 8):
        totals = totals + m.vfin[k]
    source, target = iota((256, 128), 0), iota((256, 128), 1)
    own_12 = ((source - target == 12 * t) & (target < 12)).astype(BF)
    own_48 = ((source - target == 48 * t) & (target < 48)).astype(BF)
    row16 = iota((16, 128), 0)
    gvec_o[...] = jnp.where(row16 < 8, moved_by(totals, own_12), moved_by(totals, own_48))
    fin_g1.wait_recv()
    for u in range(4):
        part = both(m.fin1, u, slice(0, D))
        ordered = jnp.concatenate(
            [part[:, 0:256], part[:, 384:512], part[:, 256:384], part[:, 512:]], axis=1
        )
        for k, ref in enumerate((gk_o, gv_o, gq_o, go_o)):
            ref[:, HW * u:HW * u + HW] = ordered[:, HW * k:HW * k + HW]

    for flight in sent:
        flight.wait_send()
    far_wait(0, 15 - s, False)
    far_wait(1, s, False)
    assert used[0] <= RECVS, used[0]


def hand_out(*refs):
    whole, vec, outs = refs[:8], refs[8], refs[9:]
    for src, dst in zip(whole, outs[:8]):
        dst[...] = src[...]
    for k, dst in enumerate(outs[8:16]):
        dst[...] = vec[k:k + 1, 0:12]
    outs[16][...] = vec[8:9, 0:48]


def body(
    tokens, seg_lengths, ln1_gain, ln1_bias, w_query, q_bias, w_key, w_value, v_bias,
    w_out, o_bias, ln2_gain, ln2_bias, w_up, up_bias, w_down, down_bias, d_out,
):
    vectors = [ln1_gain, ln1_bias, q_bias, v_bias, o_bias, ln2_gain, ln2_bias, down_bias, up_bias]
    shape = jax.ShapeDtypeStruct
    vmem = pl.BlockSpec(memory_space=pltpu.VMEM)
    shapes = [
        shape((ROWS, D), BF),
        shape((ROWS, D), F32),
        shape((12, D), F32),
        shape((12, D), F32),
        shape((12, D), F32),
        shape((12, D), F32),
        shape((12, 4 * D), F32),
        shape((12, 4 * D), F32),
    ]
    outs = pl.pallas_call(
        layer_kernel,
        out_shape=shapes + [shape((16, 128), F32)],
        in_specs=[pl.BlockSpec(memory_space=pltpu.SMEM)] + [vmem] * 17,
        out_specs=[vmem] * 9,
        scratch_shapes=[pltpu.VMEM(dims, kind) for dims, kind in SCRATCH.values()]
        + [pltpu.SemaphoreType.DMA((n,)) for n in (SENDS, RECVS, 2, 2)],
        compiler_params=pltpu.CompilerParams(
            collective_id=0, has_side_effects=True, vmem_limit_bytes=62 * 2**20
        ),
        name="layer",
    )(
        seg_lengths, tokens[0], d_out[0], w_query, w_key, w_value, w_out, w_up, w_down,
        *[v.reshape(1, -1) for v in vectors],
    )
    outs = pl.pallas_call(
        hand_out,
        out_shape=shapes + [shape((1, 12), F32)] * 8 + [shape((1, 48), F32)],
        in_specs=[vmem] * 9,
        out_specs=[vmem] * 17,
        compiler_params=pltpu.CompilerParams(vmem_limit_bytes=62 * 2**20),
        name="hand_out",
    )(*outs)
    out, g_tok, g_q, g_k, g_v, g_o, g_up, g_down = outs[:8]
    l1g, l1b, qb, vb, ob, l2g, l2b, db, ub = [v.reshape(-1) for v in outs[8:]]
    return (
        out[None], g_tok[None], l1g, l1b, g_q, qb, g_k, g_v, vb,
        g_o, ob, l2g, l2b, g_up, ub, g_down, db,
    )


def solution(mesh):
    rows, cols = P("batch", "seq", None), P("seq", None)
    one = P("seq")
    placed = (
        rows, P("batch", None), one, one, cols, one, cols, cols, one,
        cols, one, one, one, cols, one, cols, one, rows,
    )
    return jax.shard_map(
        body,
        mesh=mesh,
        in_specs=placed,
        out_specs=(
            rows, rows, one, one, cols, one, cols, cols, one,
            cols, one, one, one, cols, one, cols, one,
        ),
        check_vma=False,
    )
```
